32 devices in a mesh: dp: 4 (over y, x), mp: 8 (over z, core).
Axes of the slice: x: 2, y: 2, z: 4, core: 2. Of those that a mesh axis runs over, the one named last changes fastest.
Arguments:
- inputs: bfloat16 [8192, 2048], P(('dp', 'mp')), may hold values from -6 to 6
- cotangent: bfloat16 [8192, 2048], P(('dp', 'mp')), may hold values from -6 to 6
- widths: int32 [4], P('dp'), may hold values from 0 to 3, as said below
- norm_gain: float32 [2048], replicated, may hold values from 0.5 to 1.5
- in_weight: bfloat16 [2048, 8512], P('mp'), may hold values from -0.125 to 0.125
- conv_weight: float32 [4, 4352], replicated, may hold values from -3 to 3
- conv_bias: float32 [4352], replicated, may hold values from -3 to 3
- step_bias: float32 [64], replicated, may hold values from -4 to -0.5
- rate_log: float32 [64], replicated, may hold values from -4.6 to -0.7
- skip_gain: float32 [64], replicated, may hold values from 0.5 to 1.5
- out_gain: float32 [4096], replicated, may hold values from 0.5 to 1.5
- out_weight: bfloat16 [4096, 2048], P('mp'), may hold values from -0.09375 to 0.09375
Outputs:
- outputs: bfloat16 [8192, 2048], P(('dp', 'mp'))
- input_grad: bfloat16 [8192, 2048], P(('dp', 'mp'))
- norm_gain_grad: float32 [2048], replicated
- in_weight_grad: float32 [2048, 8512], P('mp')
- conv_weight_grad: float32 [4, 4352], replicated
- conv_bias_grad: float32 [4352], replicated
- step_bias_grad: float32 [64], replicated
- rate_log_grad: float32 [64], replicated
- skip_gain_grad: float32 [64], replicated
- out_gain_grad: float32 [4096], replicated
- out_weight_grad: float32 [4096, 2048], P('mp')
The draws below stay inside these ranges and needn't reach their ends.
Inputs may be any that keep to these rules, and one draw needn't show every extreme that they name: `widths`: each index of dp holds 1 sequence in a row, and at least one of them has width index 3.
All inputs are finite; a program needn't handle non-finite values.
Results may differ from the reference program's by a relative error of at most 0.01.
Values may be sent and summed in bfloat16 or wider, within the bound.
No kernel may reach another device: no remote copies, remote signals or barrier semaphores. Data moves between devices by JAX's collectives and lax.ppermute only.
A program may use at most 320 MiB of HBM per device.

```python
import jax
import jax.numpy as jnp
from jax import lax

D = 2048
H = 64
HEADDIM = 64
STATE = 128
CONV = 4
STRETCH = 256
SEQ = 2048
INNER = 4096
XBC = 4352
E = 8512
SEQ_GROUP = 1
SEQS = 4
TOKENS = 8192


def draw_widths(key, part):
    key = jax.random.fold_in(key, 5)
    base = jax.random.randint(jax.random.fold_in(key, 1), (SEQS,), 0, 4, dtype=jnp.int32)
    groups = SEQS // SEQ_GROUP
    picks = jax.random.randint(jax.random.fold_in(key, 2), (groups,), 0, SEQ_GROUP, dtype=jnp.int32)
    spots = jnp.arange(groups, dtype=jnp.int32) * SEQ_GROUP + picks
    return base.at[spots].set(3)


def steps_of(own_key, extent, pieces, smallest, high):
    loudness = 1.0
    for dim, shards_of in pieces:
        steps = jax.random.uniform(jax.random.fold_in(jax.random.fold_in(own_key, 6), dim), (shards_of,), jnp.float32, smallest / len(pieces), high / len(pieces))
        loudness = loudness * jnp.repeat(jnp.exp(steps), extent[dim] // shards_of).reshape((-1,) + (1,) * (len(extent) - 1 - dim))
    return loudness


def bell_draw(own_key, shape, width, bound, cuts=(), held_as=jnp.bfloat16):
    drawn = width * jax.random.normal(own_key, shape, jnp.float32)
    if cuts:
        drawn = drawn * steps_of(own_key, shape, cuts, -0.22, 0.18)
    return jnp.clip(drawn, -bound, bound).astype(held_as)


def setup_inputs(seed: int = 0) -> dict:
    key_of = jax.random.split(jax.random.key(seed), 13)
    return {
        "inputs": bell_draw(key_of[0], (TOKENS, D), 1.0, 6.0, ((0, 32),)),
        "cotangent": bell_draw(key_of[1], (TOKENS, D), 1.0, 6.0, ((0, 32),)),
        "widths": draw_widths(jax.random.fold_in(key_of[12], 71), 0),
        "norm_gain": jnp.clip(1.0 + 0.1 * jax.random.normal(key_of[3], (D,), jnp.float32), 0.5, 1.5),
        "in_weight": bell_draw(key_of[4], (D, E), D ** -0.5, 0.125, ((0, 8),)),
        "conv_weight": bell_draw(key_of[5], (CONV, XBC), CONV ** -0.5, 3.0, (), jnp.float32),
        "conv_bias": bell_draw(key_of[6], (XBC,), 0.5, 3.0, (), jnp.float32),
        "step_bias": jnp.clip(jax.random.uniform(key_of[7], (H,), jnp.float32, -4.0, -0.5), -4.0, -0.5),
        "rate_log": jnp.clip(jax.random.uniform(key_of[8], (H,), jnp.float32, -4.6, -0.7), -4.6, -0.7),
        "skip_gain": jnp.clip(jax.random.uniform(key_of[9], (H,), jnp.float32, 0.5, 1.5), 0.5, 1.5),
        "out_gain": jnp.clip(1.0 + 0.1 * jax.random.normal(key_of[10], (INNER,), jnp.float32), 0.5, 1.5),
        "out_weight": bell_draw(key_of[11], (INNER, D), INNER ** -0.5, 0.09375, ((0, 8),)),
    }


EPS = 1e-05
HIGH = lax.Precision.HIGHEST

@jax.custom_vjp
def low(v):
    return lax.optimization_barrier(v.astype(jnp.bfloat16)).astype(jnp.float32)

@jax.custom_vjp
def low_back(v):
    return v

def low_keep(v):
    return (low(v), None)

def low_pass(kept, grad):
    return (grad,)

def back_keep(v):
    return (v, None)

def back_low(kept, grad):
    return (low(grad),)
low.defvjp(low_keep, low_pass)
low_back.defvjp(back_keep, back_low)

def conv_act(extended, conv_weight, conv_bias):
    conv_span = conv_weight.shape[0]
    length = extended.shape[0] - conv_span + 1
    summed = conv_bias[None, :] + extended[0:length] * conv_weight[0][None, :]
    for offset in range(1, conv_span):
        summed = summed + extended[offset:offset + length] * conv_weight[offset][None, :]
    return jax.nn.silu(summed)

def prepare(extended, step_raw, conv_weight, conv_bias, step_bias, rate_log, head_mask, inner_width):
    conv_out = conv_act(extended, conv_weight, conv_bias)
    length = conv_out.shape[0]
    head_count = step_raw.shape[1]
    state_dim = (conv_out.shape[1] - inner_width) // 2
    values = conv_out[:, :inner_width].reshape(length, head_count, inner_width // head_count) * head_mask[None, :, None]
    b_coef = conv_out[:, inner_width:inner_width + state_dim]
    c_coef = conv_out[:, inner_width + state_dim:]
    step_size = jax.nn.softplus(step_raw + step_bias[None, :])
    decay_rate = -jnp.exp(rate_log)[None, :] * step_size
    scaled = values * step_size[:, :, None]
    return (values, scaled, b_coef, c_coef, decay_rate)

def stretch_step(carry_state, block_parts):
    scaled, b_coef, c_coef, decay_rate = block_parts
    cumulative = jnp.cumsum(decay_rate, axis=0)
    block_len = decay_rate.shape[0]
    causal = lax.broadcasted_iota(jnp.int32, (block_len, block_len), 0) >= lax.broadcasted_iota(jnp.int32, (block_len, block_len), 1)
    gap_logs = jnp.where(causal[:, :, None], cumulative[:, None, :] - cumulative[None, :, :], -1e+30)
    scores = jnp.dot(c_coef, b_coef.T, precision=HIGH)
    mixing = scores[:, :, None] * jnp.exp(gap_logs)
    within = jnp.einsum('lsh,shp->lhp', mixing, scaled, precision=HIGH)
    carried = jnp.einsum('ln,hpn->lhp', c_coef, carry_state, precision=HIGH) * jnp.exp(cumulative)[:, :, None]
    tail_logs = jnp.exp(cumulative[-1][None, :] - cumulative)
    fresh_state = jnp.einsum('sh,shp,sn->hpn', tail_logs, scaled, b_coef, precision=HIGH)
    new_state = carry_state * jnp.exp(cumulative[-1])[:, None, None] + fresh_state
    return (new_state, within + carried)

def run_stretches(scaled, b_coef, c_coef, decay_rate, carry_state):
    length = scaled.shape[0]
    head_count = scaled.shape[1]
    head_dim = scaled.shape[2]
    block_count = length // STRETCH
    block_parts = (scaled.reshape(block_count, STRETCH, head_count, head_dim), b_coef.reshape(block_count, STRETCH, b_coef.shape[1]), c_coef.reshape(block_count, STRETCH, c_coef.shape[1]), decay_rate.reshape(block_count, STRETCH, head_count))
    final_state, outputs = lax.scan(jax.checkpoint(stretch_step), carry_state, block_parts)
    return (final_state, outputs.reshape(length, head_count, head_dim))

def sequence_forward(seq_x, width_index, weights_f):
    norm_gain, in_weight, conv_weight, conv_bias, step_bias, rate_log, skip_gain, out_gain, out_weight = weights_f
    mean_sq = lax.optimization_barrier(jnp.mean(seq_x * seq_x, axis=-1, keepdims=True))
    normed = seq_x * lax.rsqrt(mean_sq + EPS)
    hidden = low(normed * norm_gain[None, :])
    projected = low_back(low(jnp.dot(hidden, in_weight, precision=HIGH)))
    gate_z = projected[:, :INNER]
    conv_input = projected[:, INNER:INNER + XBC]
    step_raw = projected[:, INNER + XBC:]
    active_heads = H // 8 * jnp.left_shift(jnp.int32(1), width_index)
    head_mask = (jnp.arange(H, dtype=jnp.int32) < active_heads).astype(jnp.float32)
    chan_mask = jnp.repeat(head_mask, HEADDIM)
    extended = jnp.concatenate([jnp.zeros((CONV - 1, XBC), jnp.float32), conv_input], axis=0)
    values, scaled, b_coef, c_coef, decay_rate = prepare(extended, step_raw, conv_weight, conv_bias, step_bias, rate_log, head_mask, INNER)
    start_state = jnp.zeros((H, HEADDIM, STATE), jnp.float32)
    _, mixed = run_stretches(scaled, b_coef, c_coef, decay_rate, start_state)
    y_all = low_back(low((mixed + skip_gain[None, :, None] * values).reshape(SEQ, INNER)))
    gated = y_all * jax.nn.silu(gate_z)
    active_count = (active_heads * HEADDIM).astype(jnp.float32)
    mean_g = lax.optimization_barrier(jnp.sum(gated * gated * chan_mask[None, :], axis=-1, keepdims=True)) / active_count
    normed_out = low(gated * lax.rsqrt(mean_g + EPS) * out_gain[None, :] * chan_mask[None, :])
    return seq_x + jnp.dot(normed_out, out_weight, precision=HIGH)

def reference(inputs, cotangent, widths, norm_gain, in_weight, conv_weight, conv_bias, step_bias, rate_log, skip_gain, out_gain, out_weight):
    weights_f = (norm_gain, in_weight.astype(jnp.float32), conv_weight, conv_bias, step_bias, rate_log, skip_gain, out_gain, out_weight.astype(jnp.float32))
    seq_inputs = inputs.astype(jnp.float32).reshape(SEQS, SEQ, D)
    seq_cots = cotangent.astype(jnp.float32).reshape(SEQS, SEQ, D)

    def per_sequence(grad_total, seq_item):
        seq_x, seq_cot, width_index = seq_item
        result, pullback = jax.vjp(lambda part_x, part_w: sequence_forward(part_x, width_index, part_w), seq_x, weights_f)
        d_input, d_weights = pullback(seq_cot)
        grad_total = jax.tree.map(lambda left, right: left + right, grad_total, d_weights)
        return (grad_total, (result.astype(jnp.bfloat16), d_input.astype(jnp.bfloat16)))
    zero_grads = jax.tree.map(jnp.zeros_like, weights_f)
    grad_total, (results, d_inputs) = lax.scan(per_sequence, zero_grads, (seq_inputs, seq_cots, widths))
    return (results.reshape(TOKENS, D), d_inputs.reshape(TOKENS, D), grad_total[0], grad_total[1], grad_total[2], grad_total[3], grad_total[4], grad_total[5], grad_total[6], grad_total[7], grad_total[8])
```

```python
import jax
import jax.numpy as jnp
from jax import lax
from jax.experimental import pallas as pl
from jax.experimental.pallas import tpu as pltpu
from jax.sharding import PartitionSpec as P

SEQ = 2048
BLOCK = 256
EPS = 1e-05
LANES = 128
VMEM = 56 * 2**20

F32 = jnp.float32
BF16 = jnp.bfloat16
NN = (((1,), (0,)), ((), ()))
NT = (((1,), (1,)), ((), ()))
TN = (((0,), (0,)), ((), ()))


def mm(left, right, dims=NN):
    return lax.dot_general(left, right, dims, preferred_element_type=F32)


def halves(value):
    high = value.astype(BF16)
    return high, (value - high.astype(F32)).astype(BF16)


def mm3(left, right, dims=NN):
    return mm(left[0], right[0], dims) + (mm(left[0], right[1], dims) + mm(left[1], right[0], dims))


def mm_exact(ones, value, dims=NN):
    first, rest = value.astype(BF16), None
    rest = value - first.astype(F32)
    second = rest.astype(BF16)
    third = (rest - second.astype(F32)).astype(BF16)
    return mm(ones, first, dims) + (mm(ones, second, dims) + mm(ones, third, dims))


def spread(per_head, width):
    rows = per_head.shape[0]
    low_half = lax.broadcasted_iota(jnp.int32, (rows, LANES), 1) < LANES // 2
    parts = []
    for pair in range(width // LANES):
        parts.append(
            jnp.where(
                low_half, per_head[:, 2 * pair : 2 * pair + 1], per_head[:, 2 * pair + 1 : 2 * pair + 2]
            )
        )
    return parts[0] if len(parts) == 1 else jnp.concatenate(parts, axis=1)


def head_ones(width):
    chan = lax.broadcasted_iota(jnp.int32, (width, LANES), 0)
    head = lax.broadcasted_iota(jnp.int32, (width, LANES), 1)
    return (chan // (LANES // 2) == head).astype(BF16)


def head_sum(per_chan, ones):
    high, low = halves(per_chan)
    return mm(high, ones) + mm(low, ones)


def conv_block(ext_ref, taps_ref, width):
    span = 4
    pre = taps_ref[span : span + 1, :] + ext_ref[5 : 5 + BLOCK, :] * taps_ref[0:1, :]
    for tap in range(1, span):
        pre = pre + ext_ref[5 + tap : 5 + tap + BLOCK, :] * taps_ref[tap : tap + 1, :]
    return pre


def step_rates(step_raw, heads_ref):
    biased = step_raw + heads_ref[0:1, :]
    step_size = jnp.maximum(biased, 0.0) + jnp.log1p(jnp.exp(-jnp.abs(biased)))
    decay = heads_ref[1:2, :] * step_size
    return biased, step_size, decay


def triangle(keep):
    row = lax.broadcasted_iota(jnp.int32, (BLOCK, BLOCK), 0)
    col = lax.broadcasted_iota(jnp.int32, (BLOCK, BLOCK), 1)
    return keep(row, col)


def forward_kernel(
    mask_ref, hidden_ref, weight_ref, taps_ref, heads_ref, skip_ref,
    proj_ref, y_ref, state_ref, square_ref,
    ext, state, *, state_dim, width,
):
    joint = 2 * state_dim + width

    @pl.when(pl.program_id(1) == 0)
    def _():
        ext[0:8, :] = jnp.zeros((8, joint), F32)
        state[...] = jnp.zeros_like(state)

    projected = mm(hidden_ref[...], weight_ref[...]).astype(BF16)
    proj_ref[...] = projected
    ext[8 : 8 + BLOCK, :] = projected[:, :joint].astype(F32)
    pre = conv_block(ext, taps_ref, joint)
    ext[0:8, :] = ext[BLOCK : BLOCK + 8, :]
    conv_out = pre * jax.nn.sigmoid(pre)
    values = conv_out[:, 2 * state_dim :] * mask_ref[0]
    b_coef = halves(conv_out[:, :state_dim])
    c_coef = halves(conv_out[:, state_dim : 2 * state_dim])
    _, step_size, decay = step_rates(projected[:, joint + width :].astype(F32), heads_ref)
    causal = triangle(lambda row, col: row >= col)
    cumulative = mm_exact(causal.astype(BF16), decay)
    across = cumulative.T
    last = cumulative[BLOCK - 1 : BLOCK, :]
    scaled = values * spread(step_size, width)
    scaled_parts = halves(scaled)
    scores = mm3(c_coef, b_coef, NT)
    low_half = lax.broadcasted_iota(jnp.int32, (BLOCK, LANES), 1) < LANES // 2
    old = state[...]
    state_ref[0] = old
    mixed = spread(jnp.exp(cumulative), width) * mm3(c_coef, halves(old))
    within = []
    for pair in range(width // LANES):
        lanes = slice(pair * LANES, (pair + 1) * LANES)
        rhs = (scaled_parts[0][:, lanes], scaled_parts[1][:, lanes])
        sides = []
        for head in (2 * pair, 2 * pair + 1):
            gap = jnp.where(causal, cumulative[:, head : head + 1] - across[head : head + 1, :], -1e30)
            sides.append(mm3(halves(scores * jnp.exp(gap)), rhs))
        within.append(jnp.where(low_half, sides[0], sides[1]))
    mixed = mixed + (within[0] if len(within) == 1 else jnp.concatenate(within, axis=1))
    tail = halves(scaled * spread(jnp.exp(last - cumulative), width))
    state[...] = old * spread(jnp.exp(last), width) + mm3(b_coef, tail, TN)
    y_low = (mixed + skip_ref[0:1, :] * values).astype(BF16)
    y_ref[...] = y_low
    gate = projected[:, joint : joint + width].astype(F32)
    gated = y_low.astype(F32) * (gate * jax.nn.sigmoid(gate))
    square = halves(gated * gated * mask_ref[0])
    ones = jnp.ones((8, width), BF16)
    square_ref[0] = mm(ones, square[0], NT) + mm(ones, square[1], NT)


def backward_kernel(
    mask_ref, joint_ref, before_ref, raw_ref, dy_ref, dgate_ref, state_ref, taps_ref, heads_ref, skip_ref,
    dproj_ref, conv_grad_ref, head_grad_ref,
    ext, dext, dstate, rows, *, state_dim, width, blocks,
):
    joint = 2 * state_dim + width
    place = blocks - 1 - pl.program_id(1)

    @pl.when((pl.program_id(0) == 0) & (pl.program_id(1) == 0))
    def _():
        conv_grad_ref[...] = jnp.zeros_like(conv_grad_ref)
        head_grad_ref[...] = jnp.zeros_like(head_grad_ref)
        rows[...] = jnp.zeros_like(rows)

    @pl.when(pl.program_id(1) == 0)
    def _():
        dext[0:8, :] = jnp.zeros((8, joint), F32)
        dstate[...] = jnp.zeros_like(dstate)

    before = before_ref[...].astype(F32)[8:16, :]
    ext[0:8, :] = jnp.where(place > 0, before, 0.0)
    ext[8 : 8 + BLOCK, :] = joint_ref[...].astype(F32)
    pre = conv_block(ext, taps_ref, joint)
    sig = jax.nn.sigmoid(pre)
    conv_out = pre * sig
    mask = mask_ref[0]
    values = conv_out[:, 2 * state_dim :] * mask
    b_coef = halves(conv_out[:, :state_dim])
    c_coef = halves(conv_out[:, state_dim : 2 * state_dim])
    biased, step_size, decay = step_rates(raw_ref[...].astype(F32), heads_ref)
    later = triangle(lambda row, col: col >= row)
    cumulative = mm_exact(triangle(lambda row, col: row >= col).astype(BF16), decay)
    across = cumulative.T
    last = cumulative[BLOCK - 1 : BLOCK, :]
    step_chan = spread(step_size, width)
    scaled = values * step_chan
    scaled_parts = halves(scaled)
    dy_low = dy_ref[...]
    dy = dy_low.astype(F32)
    scores = mm3(b_coef, c_coef, NT)
    low_half = lax.broadcasted_iota(jnp.int32, (BLOCK, LANES), 1) < LANES // 2
    lane = lax.broadcasted_iota(jnp.int32, (BLOCK, LANES), 1)
    d_scores = jnp.zeros((BLOCK, BLOCK), F32)
    from_rows = jnp.zeros((BLOCK, LANES), F32)
    d_within = []
    for pair in range(width // LANES):
        lanes = slice(pair * LANES, (pair + 1) * LANES)
        dy_pair = dy_low[:, lanes]
        dy_twice = jnp.concatenate([dy_pair, dy_pair], axis=1)
        sides = []
        for side in range(2):
            head = 2 * pair + side
            own = low_half if side == 0 else jnp.logical_not(low_half)
            left = jnp.concatenate(
                [jnp.where(own, part[:, lanes], jnp.zeros((), BF16)) for part in scaled_parts], axis=1
            )
            d_mixing = mm(left, dy_twice, NT)
            gap = jnp.where(later, across[head : head + 1, :] - cumulative[:, head : head + 1], -1e30)
            weight = jnp.exp(gap)
            mixing = scores * weight
            d_scores = d_scores + d_mixing * weight
            product = d_mixing * mixing
            rows[head : head + 1, :] = jnp.sum(product, axis=0, keepdims=True)
            from_rows = jnp.where(lane == head, jnp.sum(product, axis=1, keepdims=True), from_rows)
            parts = halves(mixing)
            sides.append(mm(parts[0], dy_pair) + mm(parts[1], dy_pair))
        d_within.append(jnp.where(low_half, sides[0], sides[1]))
    ones = head_ones(width)
    old = state_ref[0]
    old_parts = halves(old)
    grown = dstate[...]
    grown_parts = halves(grown)
    ey = spread(jnp.exp(cumulative), width) * dy
    ey_parts = halves(ey)
    tail_chan = spread(jnp.exp(last - cumulative), width)
    tail = scaled * tail_chan
    tail_parts = halves(tail)
    last_chan = spread(jnp.exp(last), width)
    into_state = mm3(b_coef, grown_parts)
    d_scaled = (d_within[0] if len(d_within) == 1 else jnp.concatenate(d_within, axis=1)) + tail_chan * into_state
    d_parts = halves(d_scores)
    d_c = mm3(d_parts, b_coef, TN) + mm3(ey_parts, old_parts, NT)
    d_b = mm3(d_parts, c_coef) + mm3(tail_parts, grown_parts, NT)
    end_terms = head_sum(ey * mm3(c_coef, old_parts), ones)
    start_terms = head_sum(tail * into_state, ones)
    kept = jnp.sum(last_chan * grown * old, axis=0, keepdims=True)
    skip_part = jnp.sum(dy * values, axis=0, keepdims=True)
    kept_heads = mm_exact_left(jnp.concatenate([kept, skip_part, jnp.zeros((6, width), F32)], axis=0), ones)
    dstate[...] = last_chan * grown + mm3(c_coef, ey_parts, TN)
    gaps = rows[...].T - from_rows + end_terms
    d_decay = (
        mm_exact(later.astype(BF16), gaps)
        + mm_exact(triangle(lambda row, col: col < row).astype(BF16), start_terms)
        + kept_heads[0:1, :]
    )
    d_step = head_sum(d_scaled * values, ones) + d_decay * heads_ref[1:2, :]
    d_raw = d_step * jax.nn.sigmoid(biased)
    head_grad_ref[0:1, :] += jnp.sum(d_raw, axis=0, keepdims=True)
    head_grad_ref[1:2, :] += jnp.sum(d_decay * decay, axis=0, keepdims=True)
    head_grad_ref[2:3, :] += kept_heads[1:2, :]
    d_values = (d_scaled * step_chan + skip_ref[0:1, :] * dy) * mask
    d_conv = jnp.concatenate([d_b, d_c, d_values], axis=1)
    d_pre = d_conv * (sig * (1.0 + pre * (1.0 - sig)))
    for tap in range(4):
        conv_grad_ref[tap : tap + 1, :] += jnp.sum(d_pre * ext[5 + tap : 5 + tap + BLOCK, :], axis=0, keepdims=True)
    conv_grad_ref[4:5, :] += jnp.sum(d_pre, axis=0, keepdims=True)
    dext[BLOCK : BLOCK + 8, :] = dext[0:8, :]
    dext[0:BLOCK, :] = d_pre
    d_in = dext[3 : 3 + BLOCK, :] * taps_ref[0:1, :]
    for tap in range(1, 4):
        d_in = d_in + dext[3 - tap : 3 - tap + BLOCK, :] * taps_ref[tap : tap + 1, :]
    dproj_ref[:, :joint] = d_in.astype(BF16)
    dproj_ref[:, joint : joint + width] = dgate_ref[...]
    dproj_ref[:, joint + width :] = d_raw.astype(BF16)


def mm_exact_left(value, ones):
    first = value.astype(BF16)
    rest = value - first.astype(F32)
    second = rest.astype(BF16)
    third = (rest - second.astype(F32)).astype(BF16)
    return mm(first, ones) + (mm(second, ones) + mm(third, ones))


def mixer_forward(mask, hidden, weight, taps, heads, skip, state_dim, width):
    seqs = mask.shape[0]
    tokens, depth = hidden.shape
    blocks = tokens // seqs // BLOCK
    columns = weight.shape[1]
    joint = 2 * state_dim + width
    row = lambda s, c: (s * blocks + c, 0)
    whole = lambda s, c: (0, 0)
    return pl.pallas_call(
        lambda *refs: forward_kernel(*refs, state_dim=state_dim, width=width),
        grid=(seqs, blocks),
        in_specs=[
            pl.BlockSpec((1, 1, width), lambda s, c: (s, 0, 0)),
            pl.BlockSpec((BLOCK, depth), row),
            pl.BlockSpec((depth, columns), whole),
            pl.BlockSpec((8, joint), whole),
            pl.BlockSpec((8, LANES), whole),
            pl.BlockSpec((8, width), whole),
        ],
        out_specs=[
            pl.BlockSpec((BLOCK, columns), row),
            pl.BlockSpec((BLOCK, width), row),
            pl.BlockSpec((1, state_dim, width), lambda s, c: (s * blocks + c, 0, 0)),
            pl.BlockSpec((1, 8, BLOCK), lambda s, c: (s * blocks + c, 0, 0)),
        ],
        out_shape=[
            jax.ShapeDtypeStruct((tokens, columns), BF16),
            jax.ShapeDtypeStruct((tokens, width), BF16),
            jax.ShapeDtypeStruct((seqs * blocks, state_dim, width), F32),
            jax.ShapeDtypeStruct((seqs * blocks, 8, BLOCK), F32),
        ],
        scratch_shapes=[
            pltpu.VMEM((BLOCK + 8, joint), F32),
            pltpu.VMEM((state_dim, width), F32),
        ],
        compiler_params=pltpu.CompilerParams(
            dimension_semantics=("arbitrary", "arbitrary"), vmem_limit_bytes=VMEM
        ),
        name="mixer_forward",
    )(mask, hidden, weight, taps, heads, skip)


def mixer_backward(mask, projected, d_y, d_gate, states, taps, heads, skip, state_dim, width):
    seqs = mask.shape[0]
    tokens, columns = projected.shape
    blocks = tokens // seqs // BLOCK
    joint = 2 * state_dim + width
    place = lambda s, c: s * blocks + blocks - 1 - c
    row = lambda s, c: (place(s, c), 0)
    whole = lambda s, c: (0, 0)
    return pl.pallas_call(
        lambda *refs: backward_kernel(*refs, state_dim=state_dim, width=width, blocks=blocks),
        grid=(seqs, blocks),
        in_specs=[
            pl.BlockSpec((1, 1, width), lambda s, c: (s, 0, 0)),
            pl.BlockSpec((BLOCK, joint), row),
            pl.BlockSpec((16, joint), lambda s, c: (jnp.maximum(place(s, c) * (BLOCK // 16) - 1, 0), 0)),
            pl.BlockSpec((BLOCK, LANES), lambda s, c: (place(s, c), (joint + width) // LANES)),
            pl.BlockSpec((BLOCK, width), row),
            pl.BlockSpec((BLOCK, width), row),
            pl.BlockSpec((1, state_dim, width), lambda s, c: (place(s, c), 0, 0)),
            pl.BlockSpec((8, joint), whole),
            pl.BlockSpec((8, LANES), whole),
            pl.BlockSpec((8, width), whole),
        ],
        out_specs=[
            pl.BlockSpec((BLOCK, columns), row),
            pl.BlockSpec((8, joint), whole),
            pl.BlockSpec((8, LANES), whole),
        ],
        out_shape=[
            jax.ShapeDtypeStruct((tokens, columns), BF16),
            jax.ShapeDtypeStruct((8, joint), F32),
            jax.ShapeDtypeStruct((8, LANES), F32),
        ],
        scratch_shapes=[
            pltpu.VMEM((BLOCK + 8, joint), F32),
            pltpu.VMEM((BLOCK + 8, joint), F32),
            pltpu.VMEM((state_dim, width), F32),
            pltpu.VMEM((LANES, BLOCK), F32),
        ],
        compiler_params=pltpu.CompilerParams(
            dimension_semantics=("arbitrary", "arbitrary"), vmem_limit_bytes=VMEM
        ),
        name="mixer_backward",
    )(mask, projected, projected, projected, d_y, d_gate, states, taps, heads, skip)


def pad_last(array, size):
    extra = size - array.shape[-1]
    if extra == 0:
        return array
    return jnp.pad(array, [(0, 0)] * (array.ndim - 1) + [(0, extra)])


def pad_rows(array, size):
    return jnp.pad(array, [(0, size - array.shape[0]), (0, 0)])


def on_device(
    inputs, cotangent, widths, norm_gain, in_weight, conv_weight, conv_bias, step_bias, rate_log,
    skip_gain, out_gain, out_weight,
):
    mp, dp = lax.axis_size("mp"), lax.axis_size("dp")
    mp_place, dp_place = lax.axis_index("mp"), lax.axis_index("dp")
    heads, inner, channels = step_bias.shape[0], out_gain.shape[0], conv_bias.shape[0]
    head_dim, state_dim = inner // heads, (channels - inner) // 2
    own_heads = heads // mp
    own = own_heads * head_dim
    width = -(-own // LANES) * LANES
    joint = 2 * state_dim + width
    columns = joint + width + LANES
    tokens, depth = inputs.shape
    rows = depth // mp
    part = rows // dp
    seqs = widths.shape[0]
    all_tokens = tokens * mp

    slab = lax.dynamic_slice_in_dim(in_weight, dp_place * part, part, 0)
    by_place = lambda piece, size: pad_last(
        piece.reshape(part, mp, piece.shape[1] // mp).transpose(1, 0, 2), size
    )
    send = jnp.concatenate(
        [
            jnp.broadcast_to(slab[None, :, 2 * inner : 2 * inner + 2 * state_dim], (mp, part, 2 * state_dim)),
            by_place(slab[:, inner : 2 * inner], width),
            by_place(slab[:, :inner], width),
            by_place(slab[:, inner + channels :], LANES),
        ],
        axis=2,
    )
    got = lax.all_to_all(send, "mp", split_axis=0, concat_axis=0, tiled=True)
    weight = lax.all_gather(got.reshape(mp * part, columns), "dp", axis=0, tiled=True)

    reorder = lambda array: array.reshape(-1, mp, dp, part).transpose(0, 2, 1, 3).reshape(-1, depth)
    restore = lambda array: array.reshape(-1, dp, mp, part).transpose(0, 2, 1, 3).reshape(-1, depth)
    inputs_f = inputs.astype(F32)
    rms_scale = lax.rsqrt(jnp.mean(inputs_f * inputs_f, axis=-1, keepdims=True) + EPS)
    normed = inputs_f * rms_scale
    hidden_own = reorder((normed * norm_gain[None, :]).astype(BF16))
    hidden = lax.all_gather(hidden_own, "mp", axis=0, tiled=True)
    cot_all = lax.all_gather(cotangent, "mp", axis=0, tiled=True)

    first_chan, first_head = mp_place * own, mp_place * own_heads
    cut = lambda array, first, size: lax.dynamic_slice_in_dim(array, first, size, array.ndim - 1)
    taps_all = jnp.concatenate([conv_weight, conv_bias[None, :]], axis=0)
    taps = pad_rows(
        jnp.concatenate([taps_all[:, inner:], pad_last(cut(taps_all, first_chan, own), width)], axis=1), 8
    )
    head_rows = jnp.stack([step_bias, -jnp.exp(rate_log)])
    head_params = pad_rows(pad_last(cut(head_rows, first_head, own_heads), LANES), 8)
    skip = jnp.repeat(cut(skip_gain, first_head, own_heads), head_dim)[None, :]
    skip = pad_rows(pad_last(skip, width), 8)
    active_heads = heads // 8 * jnp.left_shift(jnp.int32(1), widths)
    head_mask = (first_head + jnp.arange(own_heads, dtype=jnp.int32))[None, :] < active_heads[:, None]
    chan_mask = jnp.repeat(head_mask.astype(F32), head_dim, axis=1)
    mask = pad_last(chan_mask, width)[:, None, :]
    per_token = lambda array: jnp.repeat(array, all_tokens // seqs, axis=0)
    mask_tok = chan_mask if seqs == 1 else per_token(chan_mask)
    active_count = (active_heads * head_dim).astype(F32)[:, None]
    if seqs > 1:
        active_count = per_token(active_count)

    projected, y_all, states, squares = mixer_forward(
        mask, hidden, weight, taps, head_params, skip, state_dim, width
    )
    total_square = lax.psum(squares[:, 0, :].reshape(all_tokens), "mp")[:, None]
    gate = projected[:, joint : joint + own].astype(F32)
    y_f = y_all[:, :own].astype(F32)
    gate_sig = jax.nn.sigmoid(gate)
    silu_z = gate * gate_sig
    gated = y_f * silu_z
    gain = cut(out_gain, first_chan, own)[None, :]
    out_root = lax.rsqrt(total_square / active_count + EPS)
    normed_out = (gated * out_root * gain * mask_tok).astype(BF16)
    share = jnp.dot(normed_out, out_weight, preferred_element_type=F32).astype(BF16)
    summed = lax.psum_scatter(share, "mp", scatter_dimension=0, tiled=True)
    outputs = (inputs_f + summed.astype(F32)).astype(BF16)

    d_normed = mm(cot_all, out_weight, NT)
    upstream = d_normed * gain * mask_tok
    inner_dot = lax.psum(jnp.sum(upstream * gated, axis=-1), "mp")[:, None]
    out_weight_grad = lax.psum(mm(normed_out, cot_all, TN), "dp")
    out_gain_grad = jnp.sum(d_normed * gated * out_root * mask_tok, axis=0)
    d_gated = out_root * upstream - out_root * out_root * out_root * mask_tok * gated * inner_dot / active_count
    d_y = pad_last((d_gated * silu_z).astype(BF16), width)
    d_gate = pad_last((d_gated * y_f * gate_sig * (1.0 + gate * (1.0 - gate_sig))).astype(BF16), width)
    d_proj, conv_grads, head_grads = mixer_backward(
        mask, projected, d_y, d_gate, states, taps, head_params, skip, state_dim, width
    )

    d_share = mm(d_proj, weight, NT).astype(BF16)
    d_hidden = lax.psum_scatter(d_share, "mp", scatter_dimension=0, tiled=True)
    d_hidden = restore(d_hidden.astype(F32))
    norm_gain_grad = jnp.sum(d_hidden * normed, axis=0)
    d_normed_in = d_hidden * norm_gain[None, :]
    input_back = rms_scale * (d_normed_in - normed * jnp.mean(d_normed_in * normed, axis=-1, keepdims=True))
    input_grad = (cotangent.astype(F32) + input_back).astype(BF16)

    weight_part = mm(hidden, d_proj, TN)
    mine = lax.psum_scatter(weight_part, "dp", scatter_dimension=0, tiled=True)
    blocks = lax.all_to_all(mine.reshape(mp, part, columns), "mp", split_axis=0, concat_axis=0, tiled=True)
    flat = lambda piece: piece.transpose(1, 0, 2).reshape(part, -1)
    grad_rows = jnp.concatenate(
        [
            flat(blocks[:, :, joint : joint + own]),
            flat(blocks[:, :, 2 * state_dim : 2 * state_dim + own]),
            jnp.sum(blocks[:, :, : 2 * state_dim], axis=0),
            flat(blocks[:, :, joint + width : joint + width + own_heads]),
        ],
        axis=1,
    )
    in_weight_grad = lax.all_gather(grad_rows, "dp", axis=0, tiled=True)

    def place_in(array, first, size):
        return lax.dynamic_update_slice_in_dim(
            jnp.zeros(array.shape[:-1] + (size,), F32), array, first, array.ndim - 1
        )

    conv_own = place_in(conv_grads[:5, 2 * state_dim : 2 * state_dim + own], first_chan, inner)
    conv_full = jnp.concatenate([conv_own, conv_grads[:5, : 2 * state_dim]], axis=1)
    head_full = place_in(head_grads[:3, :own_heads], first_head, heads)
    gain_full = place_in(out_gain_grad, first_chan, inner)
    conv_total, head_total, gain_total, norm_total = lax.psum(
        (conv_full, head_full, gain_full, norm_gain_grad), ("dp", "mp")
    )
    return (
        outputs,
        input_grad,
        norm_total,
        in_weight_grad,
        conv_total[:4],
        conv_total[4],
        head_total[0],
        head_total[1],
        head_total[2],
        gain_total,
        out_weight_grad,
    )


def solution(mesh):
    rows = P(("dp", "mp"), None)
    return jax.shard_map(
        on_device,
        mesh=mesh,
        in_specs=(rows, rows, P("dp"), P(), P("mp", None), P(), P(), P(), P(), P(), P(), P("mp", None)),
        out_specs=(rows, rows, P(), P("mp", None), P(), P(), P(), P(), P(), P(), P("mp", None)),
        check_vma=False,
    )
```

```python
import jax
import jax.numpy as jnp
from jax import lax
from jax.experimental import pallas as pl
from jax.experimental.pallas import tpu as pltpu
from jax.sharding import PartitionSpec as P

SEQ = 2048
BLOCK = 256
EPS = 1e-05
LANES = 128
VMEM = 56 * 2**20
FREE = pl.CostEstimate(flops=1, bytes_accessed=1, transcendentals=0)

F32 = jnp.float32
BF16 = jnp.bfloat16
NN = (((1,), (0,)), ((), ()))
NT = (((1,), (1,)), ((), ()))
TN = (((0,), (0,)), ((), ()))


def mm(left, right, dims=NN):
    return lax.dot_general(left, right, dims, preferred_element_type=F32)


def halves(value):
    high = value.astype(BF16)
    return high, (value - high.astype(F32)).astype(BF16)


def mm3(left, right, dims=NN):
    return mm(left[0], right[0], dims) + (mm(left[0], right[1], dims) + mm(left[1], right[0], dims))


def mm_exact(ones, value, dims=NN):
    first, rest = value.astype(BF16), None
    rest = value - first.astype(F32)
    second = rest.astype(BF16)
    third = (rest - second.astype(F32)).astype(BF16)
    return mm(ones, first, dims) + (mm(ones, second, dims) + mm(ones, third, dims))


def spread(per_head, width):
    rows = per_head.shape[0]
    low_half = lax.broadcasted_iota(jnp.int32, (rows, LANES), 1) < LANES // 2
    parts = []
    for pair in range(width // LANES):
        parts.append(
            jnp.where(
                low_half, per_head[:, 2 * pair : 2 * pair + 1], per_head[:, 2 * pair + 1 : 2 * pair + 2]
            )
        )
    return parts[0] if len(parts) == 1 else jnp.concatenate(parts, axis=1)


def head_ones(width):
    chan = lax.broadcasted_iota(jnp.int32, (width, LANES), 0)
    head = lax.broadcasted_iota(jnp.int32, (width, LANES), 1)
    return (chan // (LANES // 2) == head).astype(BF16)


def head_sum(per_chan, ones):
    high, low = halves(per_chan)
    return mm(high, ones) + mm(low, ones)


def conv_block(ext_ref, taps_ref):
    span = 4
    pre = taps_ref[span : span + 1, :] + ext_ref[5 : 5 + BLOCK, :] * taps_ref[0:1, :]
    for tap in range(1, span):
        pre = pre + ext_ref[5 + tap : 5 + tap + BLOCK, :] * taps_ref[tap : tap + 1, :]
    return pre


def step_rates(step_raw, heads_ref):
    biased = step_raw + heads_ref[0:1, :]
    step_size = jnp.maximum(biased, 0.0) + jnp.log1p(jnp.exp(-jnp.abs(biased)))
    decay = heads_ref[1:2, :] * step_size
    return biased, step_size, decay


def triangle(keep):
    row = lax.broadcasted_iota(jnp.int32, (BLOCK, BLOCK), 0)
    col = lax.broadcasted_iota(jnp.int32, (BLOCK, BLOCK), 1)
    return keep(row, col)


def forward_kernel(
    mask_ref, hidden_ref, weight_ref, taps_ref, heads_ref, skip_ref,
    proj_ref, y_ref, state_ref, square_ref, pre_ref,
    ext, state, *, state_dim, width,
):
    joint = 2 * state_dim + width

    @pl.when(pl.program_id(1) == 0)
    def _():
        ext[0:8, :] = jnp.zeros((8, joint), F32)
        state[...] = jnp.zeros_like(state)

    projected = mm(hidden_ref[...], weight_ref[...]).astype(BF16)
    proj_ref[...] = projected
    ext[8 : 8 + BLOCK, :] = projected[:, width : width + joint].astype(F32)
    pre = conv_block(ext, taps_ref)
    pre_ref[...] = pre
    ext[0:8, :] = ext[BLOCK : BLOCK + 8, :]
    conv_out = pre * jax.nn.sigmoid(pre)
    values = conv_out[:, 2 * state_dim :] * mask_ref[0]
    b_coef = halves(conv_out[:, :state_dim])
    c_coef = halves(conv_out[:, state_dim : 2 * state_dim])
    _, step_size, decay = step_rates(projected[:, joint + width :].astype(F32), heads_ref)
    causal = triangle(lambda row, col: row >= col)
    cumulative = mm_exact(causal.astype(BF16), decay)
    across = cumulative.T
    last = cumulative[BLOCK - 1 : BLOCK, :]
    scaled = values * spread(step_size, width)
    scaled_parts = halves(scaled)
    scores = mm3(c_coef, b_coef, NT)
    low_half = lax.broadcasted_iota(jnp.int32, (BLOCK, LANES), 1) < LANES // 2
    old = state[...]
    state_ref[0] = old
    mixed = spread(jnp.exp(cumulative), width) * mm3(c_coef, halves(old))
    within = []
    for pair in range(width // LANES):
        lanes = slice(pair * LANES, (pair + 1) * LANES)
        rhs = (scaled_parts[0][:, lanes], scaled_parts[1][:, lanes])
        sides = []
        for head in (2 * pair, 2 * pair + 1):
            gap = jnp.where(causal, cumulative[:, head : head + 1] - across[head : head + 1, :], -1e30)
            sides.append(mm3(halves(scores * jnp.exp(gap)), rhs))
        within.append(jnp.where(low_half, sides[0], sides[1]))
    mixed = mixed + (within[0] if len(within) == 1 else jnp.concatenate(within, axis=1))
    tail = halves(scaled * spread(jnp.exp(last - cumulative), width))
    state[...] = old * spread(jnp.exp(last), width) + mm3(b_coef, tail, TN)
    y_low = (mixed + skip_ref[0:1, :] * values).astype(BF16)
    y_ref[...] = y_low
    gate = projected[:, :width].astype(F32)
    gated = y_low.astype(F32) * (gate * jax.nn.sigmoid(gate))
    square = halves(gated * gated * mask_ref[0])
    ones = jnp.ones((8, width), BF16)
    square_ref[0] = mm(ones, square[0], NT) + mm(ones, square[1], NT)


def backward_kernel(
    gain_ref, proj_ref, pre_ref, y_ref, d_normed_ref, tokens_ref, state_ref, taps_ref, heads_ref, skip_ref,
    dproj_ref, conv_grad_ref, head_grad_ref, gain_grad_ref,
    dext, dstate, rows, *, state_dim, width,
):
    joint = 2 * state_dim + width

    @pl.when((pl.program_id(0) == 0) & (pl.program_id(1) == 0))
    def _():
        conv_grad_ref[...] = jnp.zeros_like(conv_grad_ref)
        head_grad_ref[...] = jnp.zeros_like(head_grad_ref)
        gain_grad_ref[...] = jnp.zeros_like(gain_grad_ref)
        rows[...] = jnp.zeros_like(rows)

    @pl.when(pl.program_id(1) == 0)
    def _():
        dext[0:8, :] = jnp.zeros((8, joint), F32)
        dstate[...] = jnp.zeros_like(dstate)

    per_token = tokens_ref[0].T
    count = gain_ref[0, 2:3, 0:1]
    root = lax.rsqrt(per_token[:, 0:1] / count + EPS)
    pull = root * root * per_token[:, 1:2] / count
    gate = proj_ref[:, :width].astype(F32)
    y = y_ref[...].astype(F32)
    gate_sig = jax.nn.sigmoid(gate)
    silu = gate * gate_sig
    normed_gated = y * silu * root * gain_ref[0, 1:2, :]
    d_normed = d_normed_ref[...]
    gain_grad_ref[0:1, :] += jnp.sum(d_normed * normed_gated, axis=0, keepdims=True)
    d_gated = root * (d_normed * gain_ref[0, 0:1, :]) - normed_gated * pull
    dy_low = (d_gated * silu).astype(BF16)
    dproj_ref[:, :width] = (d_gated * y * gate_sig * (1.0 + gate * (1.0 - gate_sig))).astype(BF16)

    pre = pre_ref[...]
    sig = jax.nn.sigmoid(pre)
    conv_out = pre * sig
    mask = gain_ref[0, 1:2, :]
    values = conv_out[:, 2 * state_dim :] * mask
    b_coef = halves(conv_out[:, :state_dim])
    c_coef = halves(conv_out[:, state_dim : 2 * state_dim])
    biased, step_size, decay = step_rates(proj_ref[:, joint + width :].astype(F32), heads_ref)
    later = triangle(lambda row, col: col >= row)
    cumulative = mm_exact(triangle(lambda row, col: row >= col).astype(BF16), decay)
    across = cumulative.T
    last = cumulative[BLOCK - 1 : BLOCK, :]
    step_chan = spread(step_size, width)
    scaled = values * step_chan
    scaled_parts = halves(scaled)
    dy = dy_low.astype(F32)
    scores = mm3(b_coef, c_coef, NT)
    low_half = lax.broadcasted_iota(jnp.int32, (BLOCK, LANES), 1) < LANES // 2
    lane = lax.broadcasted_iota(jnp.int32, (BLOCK, LANES), 1)
    d_scores = jnp.zeros((BLOCK, BLOCK), F32)
    from_rows = jnp.zeros((BLOCK, LANES), F32)
    d_within = []
    for pair in range(width // LANES):
        lanes = slice(pair * LANES, (pair + 1) * LANES)
        dy_pair = dy_low[:, lanes]
        dy_twice = jnp.concatenate([dy_pair, dy_pair], axis=1)
        sides = []
        for side in range(2):
            head = 2 * pair + side
            own = low_half if side == 0 else jnp.logical_not(low_half)
            left = jnp.concatenate(
                [jnp.where(own, part[:, lanes], jnp.zeros((), BF16)) for part in scaled_parts], axis=1
            )
            d_mixing = mm(left, dy_twice, NT)
            gap = jnp.where(later, across[head : head + 1, :] - cumulative[:, head : head + 1], -1e30)
            weight = jnp.exp(gap)
            mixing = scores * weight
            d_scores = d_scores + d_mixing * weight
            product = d_mixing * mixing
            rows[head : head + 1, :] = jnp.sum(product, axis=0, keepdims=True)
            from_rows = jnp.where(lane == head, jnp.sum(product, axis=1, keepdims=True), from_rows)
            parts = halves(mixing)
            sides.append(mm(parts[0], dy_pair) + mm(parts[1], dy_pair))
        d_within.append(jnp.where(low_half, sides[0], sides[1]))
    ones = head_ones(width)
    old = state_ref[0]
    old_parts = halves(old)
    grown = dstate[...]
    grown_parts = halves(grown)
    ey = spread(jnp.exp(cumulative), width) * dy
    ey_parts = halves(ey)
    tail_chan = spread(jnp.exp(last - cumulative), width)
    tail = scaled * tail_chan
    tail_parts = halves(tail)
    last_chan = spread(jnp.exp(last), width)
    into_state = mm3(b_coef, grown_parts)
    d_scaled = (d_within[0] if len(d_within) == 1 else jnp.concatenate(d_within, axis=1)) + tail_chan * into_state
    d_parts = halves(d_scores)
    d_c = mm3(d_parts, b_coef, TN) + mm3(ey_parts, old_parts, NT)
    d_b = mm3(d_parts, c_coef) + mm3(tail_parts, grown_parts, NT)
    end_terms = head_sum(ey * mm3(c_coef, old_parts), ones)
    start_terms = head_sum(tail * into_state, ones)
    kept = jnp.sum(last_chan * grown * old, axis=0, keepdims=True)
    skip_part = jnp.sum(dy * values, axis=0, keepdims=True)
    kept_heads = mm_exact_left(jnp.concatenate([kept, skip_part, jnp.zeros((6, width), F32)], axis=0), ones)
    dstate[...] = last_chan * grown + mm3(c_coef, ey_parts, TN)
    gaps = rows[...].T - from_rows + end_terms
    d_decay = (
        mm_exact(later.astype(BF16), gaps)
        + mm_exact(triangle(lambda row, col: col < row).astype(BF16), start_terms)
        + kept_heads[0:1, :]
    )
    d_step = head_sum(d_scaled * values, ones) + d_decay * heads_ref[1:2, :]
    d_raw = d_step * jax.nn.sigmoid(biased)
    head_grad_ref[0:1, :] += jnp.sum(d_raw, axis=0, keepdims=True)
    head_grad_ref[1:2, :] += jnp.sum(d_decay * decay, axis=0, keepdims=True)
    head_grad_ref[2:3, :] += kept_heads[1:2, :]
    d_values = (d_scaled * step_chan + skip_ref[0:1, :] * dy) * mask
    d_conv = jnp.concatenate([d_b, d_c, d_values], axis=1)
    d_pre = d_conv * (sig * (1.0 + pre * (1.0 - sig)))
    conv_grad_ref[4:5, :] += jnp.sum(d_pre, axis=0, keepdims=True)
    dext[BLOCK : BLOCK + 8, :] = dext[0:8, :]
    dext[0:BLOCK, :] = d_pre
    conv_in = proj_ref[:, width : width + joint].astype(F32)
    d_in = None
    for tap in range(4):
        ahead = d_pre if tap == 3 else dext[3 - tap : 3 - tap + BLOCK, :]
        conv_grad_ref[tap : tap + 1, :] += jnp.sum(ahead * conv_in, axis=0, keepdims=True)
        d_in = ahead * taps_ref[tap : tap + 1, :] if tap == 0 else d_in + ahead * taps_ref[tap : tap + 1, :]
    dproj_ref[:, width : width + joint] = d_in.astype(BF16)
    dproj_ref[:, joint + width :] = d_raw.astype(BF16)


def mm_exact_left(value, ones):
    first = value.astype(BF16)
    rest = value - first.astype(F32)
    second = rest.astype(BF16)
    third = (rest - second.astype(F32)).astype(BF16)
    return mm(first, ones) + (mm(second, ones) + mm(third, ones))


def mixer_forward(mask, hidden, weight, taps, heads, skip, state_dim, width):
    seqs = mask.shape[0]
    tokens, depth = hidden.shape
    blocks = tokens // seqs // BLOCK
    columns = weight.shape[1]
    joint = 2 * state_dim + width
    row = lambda s, c: (s * blocks + c, 0)
    whole = lambda s, c: (0, 0)
    return pl.pallas_call(
        lambda *refs: forward_kernel(*refs, state_dim=state_dim, width=width),
        grid=(seqs, blocks),
        in_specs=[
            pl.BlockSpec((1, 1, width), lambda s, c: (s, 0, 0)),
            pl.BlockSpec((BLOCK, depth), row),
            pl.BlockSpec((depth, columns), whole),
            pl.BlockSpec((8, joint), whole),
            pl.BlockSpec((8, LANES), whole),
            pl.BlockSpec((8, width), whole),
        ],
        out_specs=[
            pl.BlockSpec((BLOCK, columns), row),
            pl.BlockSpec((BLOCK, width), row),
            pl.BlockSpec((1, state_dim, width), lambda s, c: (s * blocks + c, 0, 0)),
            pl.BlockSpec((1, 8, BLOCK), lambda s, c: (s * blocks + c, 0, 0)),
            pl.BlockSpec((BLOCK, joint), row),
        ],
        out_shape=[
            jax.ShapeDtypeStruct((tokens, columns), BF16),
            jax.ShapeDtypeStruct((tokens, width), BF16),
            jax.ShapeDtypeStruct((seqs * blocks, state_dim, width), F32),
            jax.ShapeDtypeStruct((seqs * blocks, 8, BLOCK), F32),
            jax.ShapeDtypeStruct((tokens, joint), F32),
        ],
        scratch_shapes=[
            pltpu.VMEM((BLOCK + 8, joint), F32),
            pltpu.VMEM((state_dim, width), F32),
        ],
        compiler_params=pltpu.CompilerParams(
            dimension_semantics=("arbitrary", "arbitrary"), vmem_limit_bytes=VMEM
        ),
        cost_estimate=FREE,
        name="mixer_forward",
    )(mask, hidden, weight, taps, heads, skip)


def mixer_backward(gains, projected, pre, y_all, d_normed, token_rows, states, taps, heads, skip, state_dim):
    seqs, _, width = gains.shape
    tokens, columns = projected.shape
    blocks = tokens // seqs // BLOCK
    joint = 2 * state_dim + width
    place = lambda s, c: s * blocks + blocks - 1 - c
    row = lambda s, c: (place(s, c), 0)
    block = lambda s, c: (place(s, c), 0, 0)
    whole = lambda s, c: (0, 0)
    return pl.pallas_call(
        lambda *refs: backward_kernel(*refs, state_dim=state_dim, width=width),
        grid=(seqs, blocks),
        in_specs=[
            pl.BlockSpec((1, 8, width), lambda s, c: (s, 0, 0)),
            pl.BlockSpec((BLOCK, columns), row),
            pl.BlockSpec((BLOCK, joint), row),
            pl.BlockSpec((BLOCK, width), row),
            pl.BlockSpec((BLOCK, width), row),
            pl.BlockSpec((1, 8, BLOCK), block),
            pl.BlockSpec((1, state_dim, width), block),
            pl.BlockSpec((8, joint), whole),
            pl.BlockSpec((8, LANES), whole),
            pl.BlockSpec((8, width), whole),
        ],
        out_specs=[
            pl.BlockSpec((BLOCK, columns), row),
            pl.BlockSpec((8, joint), whole),
            pl.BlockSpec((8, LANES), whole),
            pl.BlockSpec((8, width), whole),
        ],
        out_shape=[
            jax.ShapeDtypeStruct((tokens, columns), BF16),
            jax.ShapeDtypeStruct((8, joint), F32),
            jax.ShapeDtypeStruct((8, LANES), F32),
            jax.ShapeDtypeStruct((8, width), F32),
        ],
        scratch_shapes=[
            pltpu.VMEM((BLOCK + 8, joint), F32),
            pltpu.VMEM((state_dim, width), F32),
            pltpu.VMEM((LANES, BLOCK), F32),
        ],
        compiler_params=pltpu.CompilerParams(
            dimension_semantics=("arbitrary", "arbitrary"), vmem_limit_bytes=VMEM
        ),
        cost_estimate=FREE,
        name="mixer_backward",
    )(gains, projected, pre, y_all, d_normed, token_rows, states, taps, heads, skip)


def row_sum(value):
    ones = jnp.ones((8, value.shape[1]), BF16)
    high, low = halves(value)
    return mm(ones, high, NT) + mm(ones, low, NT)


def pull_kernel(cot_ref, weight_ref, gate_ref, y_ref, gain_ref, d_normed_ref, dot_ref):
    d_normed = mm(cot_ref[...], weight_ref[...], NT)
    d_normed_ref[...] = d_normed
    gate = gate_ref[...].astype(F32)
    gated = y_ref[...].astype(F32) * (gate * jax.nn.sigmoid(gate))
    dot_ref[0] = row_sum(d_normed * gain_ref[0, 0:1, :] * gated)


def pull_back(cot_all, weight, projected, y_all, gains, gate_place):
    seqs, _, width = gains.shape
    tokens, depth = cot_all.shape
    blocks = tokens // seqs // BLOCK
    row = lambda s, c: (s * blocks + c, 0)
    return pl.pallas_call(
        pull_kernel,
        grid=(seqs, blocks),
        in_specs=[
            pl.BlockSpec((BLOCK, depth), row),
            pl.BlockSpec((width, depth), lambda s, c: (0, 0)),
            pl.BlockSpec((BLOCK, width), lambda s, c: (s * blocks + c, gate_place)),
            pl.BlockSpec((BLOCK, width), row),
            pl.BlockSpec((1, 8, width), lambda s, c: (s, 0, 0)),
        ],
        out_specs=[
            pl.BlockSpec((BLOCK, width), row),
            pl.BlockSpec((1, 8, BLOCK), lambda s, c: (s * blocks + c, 0, 0)),
        ],
        out_shape=[
            jax.ShapeDtypeStruct((tokens, width), F32),
            jax.ShapeDtypeStruct((seqs * blocks, 8, BLOCK), F32),
        ],
        compiler_params=pltpu.CompilerParams(
            dimension_semantics=("arbitrary", "arbitrary"), vmem_limit_bytes=VMEM
        ),
        cost_estimate=FREE,
        name="pull_back",
    )(cot_all, weight, projected, y_all, gains)


def pad_last(array, size):
    extra = size - array.shape[-1]
    if extra == 0:
        return array
    return jnp.pad(array, [(0, 0)] * (array.ndim - 1) + [(0, extra)])


def pad_rows(array, size):
    return jnp.pad(array, [(0, size - array.shape[0]), (0, 0)])


def swap(value, axis, bit):
    size = lax.axis_size(axis)
    return lax.ppermute(value, axis, [(place, place ^ bit) for place in range(size)])


def all_sum(value, axis):
    bit = 1
    while bit < lax.axis_size(axis):
        value = value + swap(value, axis, bit)
        bit *= 2
    return value


NEAR_FAR = ((1, 2), (2, 1))


def reduce_cut(share, block, dtype):
    return [
        jnp.concatenate([block(share, near ^ far, half), block(share, near, half)], axis=0).astype(dtype)
        for half, (near, far) in enumerate(NEAR_FAR)
    ]


def reduce_near(cuts):
    return [swap(cut, "dp", near) for cut, (near, _) in zip(cuts, NEAR_FAR)]


def reduce_far(share, block, got):
    rows = got[0].shape[0] // 2
    kept = [
        (block(share, far, half) + got[half][:rows].astype(F32)).astype(got[half].dtype)
        for half, (_, far) in enumerate(NEAR_FAR)
    ]
    mine = [block(share, 0, half) + got[half][rows:].astype(F32) for half in range(2)]
    kept = lax.optimization_barrier(kept)
    far_got = [swap(piece, "dp", far) for piece, (_, far) in zip(kept, NEAR_FAR)]
    return jnp.concatenate([piece + other.astype(F32) for piece, other in zip(mine, far_got)], axis=0)


def dp_gather(own):
    rows = own.shape[0] // 2
    upper, lower = own[:rows], own[rows:]
    upper1, lower2 = swap(upper, "dp", 1), swap(lower, "dp", 2)
    uppers = swap(jnp.concatenate([upper, upper1], axis=0), "dp", 2)
    lowers = swap(jnp.concatenate([lower, lower2], axis=0), "dp", 1)
    return [(upper, lower), (upper1, lowers[:rows]), (uppers[:rows], lower2), (uppers[rows:], lowers[rows:])]


def line_permute(block, reach):
    chips = lax.axis_size("mp") // 2
    pairs = [(2 * z + c, 2 * ((z + reach) % chips) + c) for z in range(chips) for c in range(2)]
    return lax.ppermute(block, "mp", pairs)


def line_send(shares):
    groups = [list(range(core, lax.axis_size("mp"), 2)) for core in range(2)]
    return lax.all_to_all(shares, "mp", split_axis=0, concat_axis=0, axis_index_groups=groups, tiled=True)


def pair_kernel(place_ref, own_ref, sibling_ref, own_weight_ref, sibling_weight_ref, *out_refs, dims):
    share = mm(own_ref[...], own_weight_ref[...], dims) + mm(sibling_ref[...], sibling_weight_ref[...], dims)
    share = share.astype(BF16)
    if len(out_refs) == 1:
        out_refs[0][0] = share
        return
    for reach, out_ref in enumerate(out_refs):

        @pl.when(pl.program_id(0) == reach)
        def _(out_ref=out_ref):
            out_ref[...] = share


def pair_product(left, theirs, own_weight, sibling_weight, dims, depth, tokens, stacked):
    chips = lax.axis_size("mp") // 2
    inner = left.shape[1]
    whole = lambda i, place: (0, 0)
    place = lax.axis_index("mp").astype(jnp.int32)
    there = lambda i, place: lax.rem(place[0] + i, chips)
    return pl.pallas_call(
        lambda *refs: pair_kernel(*refs, dims=dims),
        grid_spec=pltpu.PrefetchScalarGridSpec(
            num_scalar_prefetch=1,
            grid=(chips,),
            in_specs=[
                pl.BlockSpec((tokens, inner), lambda i, place: (2 * there(i, place) + place[1], 0)),
                pl.BlockSpec((tokens, inner), lambda i, place: (there(i, place), 0)),
                pl.BlockSpec(own_weight.shape, whole),
                pl.BlockSpec(sibling_weight.shape, whole),
            ],
            out_specs=[pl.BlockSpec((1, tokens, depth), lambda i, place: (there(i, place), 0, 0))]
            if stacked
            else [pl.BlockSpec((tokens, depth), whole)] * chips,
        ),
        out_shape=[jax.ShapeDtypeStruct((chips, tokens, depth), BF16)]
        if stacked
        else [jax.ShapeDtypeStruct((tokens, depth), BF16)] * chips,
        compiler_params=pltpu.CompilerParams(dimension_semantics=("arbitrary",), vmem_limit_bytes=VMEM),
        cost_estimate=FREE,
        name="pair_product",
    )(jnp.stack([place // 2, place % 2]), left, theirs, own_weight, sibling_weight)


def for_sibling(left, tokens):
    mp = lax.axis_size("mp")
    by_core = left.reshape(mp // 2, 2, tokens, left.shape[1])
    other = 1 - lax.axis_index("mp") % 2
    return lax.dynamic_index_in_dim(by_core, other, 1, keepdims=False).reshape(-1, left.shape[1])


def in_place_order(pieces):
    place = lax.axis_index("dp")
    pieces = [jnp.concatenate(pair, axis=0) for pair in pieces]
    odd, high = place % 2 == 1, place // 2 == 1
    lows = [jnp.where(odd, pieces[k ^ 1], pieces[k]) for k in range(4)]
    return jnp.concatenate([jnp.where(high, lows[k ^ 2], lows[k]).astype(F32) for k in range(4)], axis=0)


def assemble_kernel(place_ref, *refs):
    out_ref = refs[-1]
    for own in range(4):

        @pl.when(place_ref[0] == own)
        def _(own=own):
            order = [refs[2 * (own ^ p) + half][...].astype(F32) for p in range(4) for half in range(2)]
            out_ref[...] = jnp.concatenate(order, axis=0).T


def assemble(gathered):
    pieces = [half for pair in gathered for half in pair]
    half_rows, columns = pieces[0].shape
    chunk = 512
    return pl.pallas_call(
        assemble_kernel,
        grid=(pl.cdiv(columns, chunk),),
        in_specs=[pl.BlockSpec(memory_space=pltpu.SMEM)]
        + [pl.BlockSpec((half_rows, chunk), lambda i: (0, i)) for _ in pieces],
        out_specs=pl.BlockSpec((chunk, 8 * half_rows), lambda i: (i, 0)),
        out_shape=jax.ShapeDtypeStruct((columns, 8 * half_rows), F32),
        compiler_params=pltpu.CompilerParams(dimension_semantics=("arbitrary",), vmem_limit_bytes=VMEM),
        cost_estimate=FREE,
        name="assemble",
    )(lax.axis_index("dp").astype(jnp.int32)[None], *pieces).T


def total(blocks):
    result = blocks[0].astype(F32)
    for index in range(1, len(blocks)):
        result = result + blocks[index].astype(F32)
    return result


def on_device(
    inputs, cotangent, widths, norm_gain, in_weight, conv_weight, conv_bias, step_bias, rate_log,
    skip_gain, out_gain, out_weight,
):
    mp, dp = lax.axis_size("mp"), lax.axis_size("dp")
    mp_place, dp_place = lax.axis_index("mp"), lax.axis_index("dp")
    heads, inner, channels = step_bias.shape[0], out_gain.shape[0], conv_bias.shape[0]
    head_dim, state_dim = inner // heads, (channels - inner) // 2
    own_heads = heads // mp
    own = own_heads * head_dim
    width = -(-own // LANES) * LANES
    joint = 2 * state_dim + width
    columns = joint + width + LANES
    tokens, depth = inputs.shape
    rows = depth // mp
    part = rows // dp
    seqs = widths.shape[0]
    all_tokens = tokens * mp

    slab = lax.dynamic_slice_in_dim(in_weight, dp_place * part, part, 0)
    by_place = lambda piece, size: pad_last(
        piece.reshape(part, mp, piece.shape[1] // mp).transpose(1, 0, 2), size
    )
    send = jnp.concatenate(
        [
            by_place(slab[:, :inner], width),
            jnp.broadcast_to(slab[None, :, 2 * inner : 2 * inner + 2 * state_dim], (mp, part, 2 * state_dim)),
            by_place(slab[:, inner : 2 * inner], width),
            by_place(slab[:, inner + channels :], LANES),
        ],
        axis=2,
    )
    got = lax.all_to_all(send, "mp", split_axis=0, concat_axis=0, tiled=True)

    def reorder(array):
        apart = array.reshape(-1, mp, dp, part)
        return jnp.concatenate(
            [
                lax.dynamic_index_in_dim(apart, dp_place ^ k, 2, keepdims=False).reshape(-1, mp * part)
                for k in range(dp)
            ],
            axis=1,
        )

    def restore(array):
        apart = array.reshape(-1, dp, mp, part)
        return jnp.stack(
            [lax.dynamic_index_in_dim(apart, dp_place ^ k, 1, keepdims=False) for k in range(dp)], axis=2
        ).reshape(-1, depth)

    line = mp <= 16
    inputs_f = inputs.astype(F32)
    rms_scale = lax.rsqrt(jnp.mean(inputs_f * inputs_f, axis=-1, keepdims=True) + EPS)
    normed = inputs_f * rms_scale
    hidden_own = reorder((normed * norm_gain[None, :]).astype(BF16))
    hidden_own, got = lax.optimization_barrier((hidden_own, got))
    weight = jnp.concatenate(sum(dp_gather(got.reshape(mp * part, columns)), ()), axis=0)
    hidden = lax.all_gather(hidden_own, "mp", axis=0, tiled=True)

    first_chan, first_head = mp_place * own, mp_place * own_heads
    cut = lambda array, first, size: lax.dynamic_slice_in_dim(array, first, size, array.ndim - 1)
    taps_all = jnp.concatenate([conv_weight, conv_bias[None, :]], axis=0)
    taps = pad_rows(
        jnp.concatenate([taps_all[:, inner:], pad_last(cut(taps_all, first_chan, own), width)], axis=1), 8
    )
    head_rows = jnp.stack([step_bias, -jnp.exp(rate_log)])
    head_params = pad_rows(pad_last(cut(head_rows, first_head, own_heads), LANES), 8)
    skip = jnp.repeat(cut(skip_gain, first_head, own_heads), head_dim)[None, :]
    skip = pad_rows(pad_last(skip, width), 8)
    active_heads = heads // 8 * jnp.left_shift(jnp.int32(1), widths)
    head_mask = (first_head + jnp.arange(own_heads, dtype=jnp.int32))[None, :] < active_heads[:, None]
    chan_mask = jnp.repeat(head_mask.astype(F32), head_dim, axis=1)
    mask = pad_last(chan_mask, width)[:, None, :]
    per_token = lambda array: jnp.repeat(array, all_tokens // seqs, axis=0)
    mask_tok = chan_mask if seqs == 1 else per_token(chan_mask)
    active_count = (active_heads * head_dim).astype(F32)[:, None]
    if seqs > 1:
        active_count = per_token(active_count)

    if line:
        sibling_out, sibling_weight = swap(out_weight, "mp", 1), swap(weight, "mp", 1)
        weight, sibling_out, sibling_weight = lax.optimization_barrier((weight, sibling_out, sibling_weight))
    projected, y_all, states, squares, pre = mixer_forward(
        mask, hidden, weight, taps, head_params, skip, state_dim, width
    )
    square_rows = all_sum(squares[:, 0, :], "mp")
    total_square = square_rows.reshape(all_tokens)[:, None]
    gate = projected[:, :own].astype(F32)
    y_f = y_all[:, :own].astype(F32)
    gate_sig = jax.nn.sigmoid(gate)
    silu_z = gate * gate_sig
    gated = y_f * silu_z
    gain = cut(out_gain, first_chan, own)[None, :]
    out_root = lax.rsqrt(total_square / active_count + EPS)
    normed_out = (gated * out_root * gain * mask_tok).astype(BF16)
    if line:
        theirs = swap(for_sibling(normed_out, tokens), "mp", 1)
        shares = pair_product(normed_out, theirs, out_weight, sibling_out, NN, depth, tokens, True)[0]
        cot_all = lax.all_gather(cotangent, "mp", axis=0, tiled=True)
        cot_all, shares = lax.optimization_barrier((cot_all, shares))
    else:
        shares = mm(normed_out, out_weight).astype(BF16)
        sent = [lax.psum_scatter(shares, "mp", scatter_dimension=0, tiled=True)]
        late_cot, sent = lax.optimization_barrier((cotangent, sent))
        cot_all = lax.all_gather(late_cot, "mp", axis=0, tiled=True)

    gain_rows = pad_last(cut(out_gain, first_chan, own), width)
    gains = jnp.concatenate(
        [
            gain_rows[None, None, :] * mask,
            mask,
            jnp.broadcast_to((active_heads * head_dim).astype(F32)[:, None, None], mask.shape),
            jnp.zeros((seqs, 5, width), F32),
        ],
        axis=1,
    )
    out_padded = pad_rows(out_weight, width)
    d_normed, dots = pull_back(cot_all, out_padded, projected, y_all, gains, 0)
    dot_rows = all_sum(dots[:, 0, :], "mp")
    out_part = mm(normed_out, cot_all, TN)
    if line:
        dot_rows, shares = lax.optimization_barrier((dot_rows, shares))
        sent = line_send(shares)
    token_rows = jnp.stack([square_rows, dot_rows] + [jnp.zeros_like(dot_rows)] * 6, axis=1)
    quarter = depth // dp

    def in_block(share, k, half):
        return share[k * quarter + half * (quarter // 2) : k * quarter + (half + 1) * (quarter // 2)]

    def to_rows(mine):
        return lax.all_to_all(mine.astype(BF16).reshape(mp, part, -1), "mp", split_axis=0, concat_axis=0, tiled=True)

    token_rows, out_part = lax.optimization_barrier((token_rows, out_part))
    out_mine = lax.psum_scatter(out_part, "dp", scatter_dimension=0, tiled=True)
    d_proj, conv_grads, head_grads, gain_grads = mixer_backward(
        gains, projected, pre, y_all, d_normed, token_rows, states, taps, head_params, skip, state_dim
    )
    def place_in(array, first, size):
        return lax.dynamic_update_slice_in_dim(
            jnp.zeros(array.shape[:-1] + (size,), F32), array, first, array.ndim - 1
        )

    conv_own = place_in(conv_grads[:5, 2 * state_dim : 2 * state_dim + own], first_chan, inner)
    conv_full = jnp.concatenate([conv_own, conv_grads[:5, : 2 * state_dim]], axis=1)
    head_full = place_in(head_grads[:3, :own_heads], first_head, heads)
    gain_full = place_in(gain_grads[0, :own], first_chan, inner)
    small = [conv_full.reshape(-1), head_full.reshape(-1), gain_full]
    sizes = [piece.shape[0] for piece in small]
    packed = jnp.concatenate(small)
    count = -(-packed.shape[0] // 1024) * 1024
    packed = jnp.pad(packed, (0, count - packed.shape[0])).reshape(-1, LANES)

    if line:
        d_proj, out_mine = lax.optimization_barrier((d_proj, out_mine))
        theirs = swap(for_sibling(d_proj, tokens), "mp", 1)
        share = mm(hidden, d_proj, TN)
        near_cut = reduce_cut(share, in_block, BF16)
        near_cut, theirs = lax.optimization_barrier((near_cut, theirs))
        near_got = reduce_near(near_cut)
        d_shares = pair_product(d_proj, theirs, weight, sibling_weight, NT, depth, tokens, False)
        near_got, d_shares, sent = lax.optimization_barrier((near_got, d_shares, sent))
        d_blocks = [d_shares[0], line_permute(d_shares[1], 1)]
        mine = reduce_far(share, in_block, near_got)
        mine, d_blocks, out_mine, packed = lax.optimization_barrier((mine, d_blocks, out_mine, packed))
        out_weight_grad = lax.all_gather(out_mine, "dp", axis=0, tiled=True)
        blocks = to_rows(mine)
        d_blocks += [line_permute(d_shares[reach], reach) for reach in range(2, min(3, mp // 2))]
        blocks, d_blocks, d_shares, packed, out_weight_grad = lax.optimization_barrier(
            (blocks, d_blocks, d_shares, all_sum(packed, "dp"), out_weight_grad)
        )
        d_blocks += [line_permute(d_shares[reach], reach) for reach in range(3, mp // 2)]
        d_hidden = total(d_blocks)
    else:
        packed = all_sum(packed, "dp")
        out_weight_grad = lax.all_gather(out_mine, "dp", axis=0, tiled=True)
        share = mm(hidden, d_proj, TN)
        d_proj, share = lax.optimization_barrier((d_proj, share))
        blocks = to_rows(reduce_far(share, in_block, reduce_near(reduce_cut(share, in_block, BF16))))
        d_shares = mm(d_proj, weight, NT).astype(BF16)
        d_hidden = lax.psum_scatter(d_shares, "mp", scatter_dimension=0, tiled=True).astype(F32)
    outputs = (inputs_f + total(sent)).astype(BF16)
    d_hidden = restore(d_hidden)
    norm_gain_grad = jnp.sum(d_hidden * normed, axis=0)
    norm_part = all_sum(norm_gain_grad.reshape(-1, LANES), "dp")
    everything = all_sum(jnp.concatenate([packed, norm_part], axis=0), "mp")
    norm_total = everything[packed.shape[0] :].reshape(depth)
    packed = everything.reshape(-1)
    conv_total = packed[: sizes[0]].reshape(conv_full.shape)
    head_total = packed[sizes[0] : sizes[0] + sizes[1]].reshape(head_full.shape)
    gain_total = packed[sizes[0] + sizes[1] : sum(sizes)]

    d_normed_in = d_hidden * norm_gain[None, :]
    input_back = rms_scale * (d_normed_in - normed * jnp.mean(d_normed_in * normed, axis=-1, keepdims=True))
    input_grad = (cotangent.astype(F32) + input_back).astype(BF16)

    flat = lambda first, size: blocks[:, :, first : first + size].transpose(1, 0, 2).reshape(part, -1)
    shared = jnp.sum(blocks[:, :, width : width + 2 * state_dim].astype(F32), axis=0).astype(BF16)
    grad_rows = jnp.concatenate(
        [flat(0, own), flat(width + 2 * state_dim, own), shared, flat(width + joint, own_heads)], axis=1
    )
    gathered = dp_gather(grad_rows)
    in_weight_grad = assemble(gathered) if line else in_place_order(gathered)

    return (
        outputs,
        input_grad,
        norm_total,
        in_weight_grad,
        conv_total[:4],
        conv_total[4],
        head_total[0],
        head_total[1],
        head_total[2],
        gain_total,
        out_weight_grad,
    )


def solution(mesh):
    rows = P(("dp", "mp"), None)
    return jax.shard_map(
        on_device,
        mesh=mesh,
        in_specs=(rows, rows, P("dp"), P(), P("mp", None), P(), P(), P(), P(), P(), P(), P("mp", None)),
        out_specs=(rows, rows, P(), P("mp", None), P(), P(), P(), P(), P(), P(), P("mp", None)),
        check_vma=False,
    )
```

```python
import jax
import jax.numpy as jnp
from jax import lax
from jax.experimental import pallas as pl
from jax.experimental.pallas import tpu as pltpu
from jax.sharding import PartitionSpec as P

SEQ = 2048
BLOCK = 256
EPS = 1e-05
LANES = 128
VMEM = 56 * 2**20
FREE = pl.CostEstimate(flops=1, bytes_accessed=1, transcendentals=0)

F32 = jnp.float32
BF16 = jnp.bfloat16
NN = (((1,), (0,)), ((), ()))
NT = (((1,), (1,)), ((), ()))
TN = (((0,), (0,)), ((), ()))


def mm(left, right, dims=NN):
    return lax.dot_general(left, right, dims, preferred_element_type=F32)


def halves(value):
    high = value.astype(BF16)
    return high, (value - high.astype(F32)).astype(BF16)


def mm3(left, right, dims=NN):
    return mm(left[0], right[0], dims) + (mm(left[0], right[1], dims) + mm(left[1], right[0], dims))


def mm_exact(ones, value, dims=NN):
    first, rest = value.astype(BF16), None
    rest = value - first.astype(F32)
    second = rest.astype(BF16)
    third = (rest - second.astype(F32)).astype(BF16)
    return mm(ones, first, dims) + (mm(ones, second, dims) + mm(ones, third, dims))


def spread(per_head, width):
    rows = per_head.shape[0]
    low_half = lax.broadcasted_iota(jnp.int32, (rows, LANES), 1) < LANES // 2
    parts = []
    for pair in range(width // LANES):
        parts.append(
            jnp.where(
                low_half, per_head[:, 2 * pair : 2 * pair + 1], per_head[:, 2 * pair + 1 : 2 * pair + 2]
            )
        )
    return parts[0] if len(parts) == 1 else jnp.concatenate(parts, axis=1)


def head_ones(width):
    chan = lax.broadcasted_iota(jnp.int32, (width, LANES), 0)
    head = lax.broadcasted_iota(jnp.int32, (width, LANES), 1)
    return (chan // (LANES // 2) == head).astype(BF16)


def head_sum(per_chan, ones):
    high, low = halves(per_chan)
    return mm(high, ones) + mm(low, ones)


def conv_block(ext_ref, taps_ref):
    span = 4
    pre = taps_ref[span : span + 1, :] + ext_ref[5 : 5 + BLOCK, :] * taps_ref[0:1, :]
    for tap in range(1, span):
        pre = pre + ext_ref[5 + tap : 5 + tap + BLOCK, :] * taps_ref[tap : tap + 1, :]
    return pre


def step_rates(step_raw, heads_ref):
    biased = step_raw + heads_ref[0:1, :]
    step_size = jnp.maximum(biased, 0.0) + jnp.log1p(jnp.exp(-jnp.abs(biased)))
    decay = heads_ref[1:2, :] * step_size
    return biased, step_size, decay


def triangle(keep):
    row = lax.broadcasted_iota(jnp.int32, (BLOCK, BLOCK), 0)
    col = lax.broadcasted_iota(jnp.int32, (BLOCK, BLOCK), 1)
    return keep(row, col)


def forward_kernel(
    mask_ref, hidden_ref, weight_ref, taps_ref, heads_ref, skip_ref,
    proj_ref, y_ref, state_ref, square_ref, pre_ref,
    ext, state, *, state_dim, width,
):
    joint = 2 * state_dim + width

    @pl.when(pl.program_id(1) == 0)
    def _():
        ext[0:8, :] = jnp.zeros((8, joint), F32)
        state[...] = jnp.zeros_like(state)

    projected = mm(hidden_ref[...], weight_ref[...]).astype(BF16)
    proj_ref[...] = projected
    ext[8 : 8 + BLOCK, :] = projected[:, width : width + joint].astype(F32)
    pre = conv_block(ext, taps_ref)
    pre_ref[...] = pre
    ext[0:8, :] = ext[BLOCK : BLOCK + 8, :]
    conv_out = pre * jax.nn.sigmoid(pre)
    values = conv_out[:, 2 * state_dim :] * mask_ref[0]
    b_coef = halves(conv_out[:, :state_dim])
    c_coef = halves(conv_out[:, state_dim : 2 * state_dim])
    _, step_size, decay = step_rates(projected[:, joint + width :].astype(F32), heads_ref)
    causal = triangle(lambda row, col: row >= col)
    cumulative = mm_exact(causal.astype(BF16), decay)
    across = cumulative.T
    last = cumulative[BLOCK - 1 : BLOCK, :]
    scaled = values * spread(step_size, width)
    scaled_parts = halves(scaled)
    scores = mm3(c_coef, b_coef, NT)
    low_half = lax.broadcasted_iota(jnp.int32, (BLOCK, LANES), 1) < LANES // 2
    old = state[...]
    state_ref[0] = old
    mixed = spread(jnp.exp(cumulative), width) * mm3(c_coef, halves(old))
    within = []
    for pair in range(width // LANES):
        lanes = slice(pair * LANES, (pair + 1) * LANES)
        rhs = (scaled_parts[0][:, lanes], scaled_parts[1][:, lanes])
        sides = []
        for head in (2 * pair, 2 * pair + 1):
            gap = jnp.where(causal, cumulative[:, head : head + 1] - across[head : head + 1, :], -1e30)
            sides.append(mm3(halves(scores * jnp.exp(gap)), rhs))
        within.append(jnp.where(low_half, sides[0], sides[1]))
    mixed = mixed + (within[0] if len(within) == 1 else jnp.concatenate(within, axis=1))
    tail = halves(scaled * spread(jnp.exp(last - cumulative), width))
    state[...] = old * spread(jnp.exp(last), width) + mm3(b_coef, tail, TN)
    y_low = (mixed + skip_ref[0:1, :] * values).astype(BF16)
    y_ref[...] = y_low
    gate = projected[:, :width].astype(F32)
    gated = y_low.astype(F32) * (gate * jax.nn.sigmoid(gate))
    square = halves(gated * gated * mask_ref[0])
    ones = jnp.ones((8, width), BF16)
    square_ref[0] = mm(ones, square[0], NT) + mm(ones, square[1], NT)


def backward_kernel(
    gain_ref, proj_ref, pre_ref, y_ref, d_normed_ref, tokens_ref, state_ref, taps_ref, heads_ref, skip_ref,
    dproj_ref, conv_grad_ref, head_grad_ref, gain_grad_ref,
    dext, dstate, rows, *, state_dim, width,
):
    joint = 2 * state_dim + width

    @pl.when((pl.program_id(0) == 0) & (pl.program_id(1) == 0))
    def _():
        conv_grad_ref[...] = jnp.zeros_like(conv_grad_ref)
        head_grad_ref[...] = jnp.zeros_like(head_grad_ref)
        gain_grad_ref[...] = jnp.zeros_like(gain_grad_ref)
        rows[...] = jnp.zeros_like(rows)

    @pl.when(pl.program_id(1) == 0)
    def _():
        dext[0:8, :] = jnp.zeros((8, joint), F32)
        dstate[...] = jnp.zeros_like(dstate)

    per_token = tokens_ref[0].T
    count = gain_ref[0, 2:3, 0:1]
    root = lax.rsqrt(per_token[:, 0:1] / count + EPS)
    pull = root * root * per_token[:, 1:2] / count
    gate = proj_ref[:, :width].astype(F32)
    y = y_ref[...].astype(F32)
    gate_sig = jax.nn.sigmoid(gate)
    silu = gate * gate_sig
    normed_gated = y * silu * root * gain_ref[0, 1:2, :]
    d_normed = d_normed_ref[...]
    gain_grad_ref[0:1, :] += jnp.sum(d_normed * normed_gated, axis=0, keepdims=True)
    d_gated = root * (d_normed * gain_ref[0, 0:1, :]) - normed_gated * pull
    dy_low = (d_gated * silu).astype(BF16)
    dproj_ref[:, :width] = (d_gated * y * gate_sig * (1.0 + gate * (1.0 - gate_sig))).astype(BF16)

    pre = pre_ref[...]
    sig = jax.nn.sigmoid(pre)
    conv_out = pre * sig
    mask = gain_ref[0, 1:2, :]
    values = conv_out[:, 2 * state_dim :] * mask
    b_coef = halves(conv_out[:, :state_dim])
    c_coef = halves(conv_out[:, state_dim : 2 * state_dim])
    biased, step_size, decay = step_rates(proj_ref[:, joint + width :].astype(F32), heads_ref)
    later = triangle(lambda row, col: col >= row)
    cumulative = mm_exact(triangle(lambda row, col: row >= col).astype(BF16), decay)
    across = cumulative.T
    last = cumulative[BLOCK - 1 : BLOCK, :]
    step_chan = spread(step_size, width)
    scaled = values * step_chan
    scaled_parts = halves(scaled)
    dy = dy_low.astype(F32)
    scores = mm3(b_coef, c_coef, NT)
    low_half = lax.broadcasted_iota(jnp.int32, (BLOCK, LANES), 1) < LANES // 2
    lane = lax.broadcasted_iota(jnp.int32, (BLOCK, LANES), 1)
    d_scores = jnp.zeros((BLOCK, BLOCK), F32)
    from_rows = jnp.zeros((BLOCK, LANES), F32)
    d_within = []
    for pair in range(width // LANES):
        lanes = slice(pair * LANES, (pair + 1) * LANES)
        dy_pair = dy_low[:, lanes]
        dy_twice = jnp.concatenate([dy_pair, dy_pair], axis=1)
        sides = []
        for side in range(2):
            head = 2 * pair + side
            own = low_half if side == 0 else jnp.logical_not(low_half)
            left = jnp.concatenate(
                [jnp.where(own, part[:, lanes], jnp.zeros((), BF16)) for part in scaled_parts], axis=1
            )
            d_mixing = mm(left, dy_twice, NT)
            gap = jnp.where(later, across[head : head + 1, :] - cumulative[:, head : head + 1], -1e30)
            weight = jnp.exp(gap)
            mixing = scores * weight
            d_scores = d_scores + d_mixing * weight
            product = d_mixing * mixing
            rows[head : head + 1, :] = jnp.sum(product, axis=0, keepdims=True)
            from_rows = jnp.where(lane == head, jnp.sum(product, axis=1, keepdims=True), from_rows)
            parts = halves(mixing)
            sides.append(mm(parts[0], dy_pair) + mm(parts[1], dy_pair))
        d_within.append(jnp.where(low_half, sides[0], sides[1]))
    ones = head_ones(width)
    old = state_ref[0]
    old_parts = halves(old)
    grown = dstate[...]
    grown_parts = halves(grown)
    ey = spread(jnp.exp(cumulative), width) * dy
    ey_parts = halves(ey)
    tail_chan = spread(jnp.exp(last - cumulative), width)
    tail = scaled * tail_chan
    tail_parts = halves(tail)
    last_chan = spread(jnp.exp(last), width)
    into_state = mm3(b_coef, grown_parts)
    d_scaled = (d_within[0] if len(d_within) == 1 else jnp.concatenate(d_within, axis=1)) + tail_chan * into_state
    d_parts = halves(d_scores)
    d_c = mm3(d_parts, b_coef, TN) + mm3(ey_parts, old_parts, NT)
    d_b = mm3(d_parts, c_coef) + mm3(tail_parts, grown_parts, NT)
    end_terms = head_sum(ey * mm3(c_coef, old_parts), ones)
    start_terms = head_sum(tail * into_state, ones)
    kept = jnp.sum(last_chan * grown * old, axis=0, keepdims=True)
    skip_part = jnp.sum(dy * values, axis=0, keepdims=True)
    kept_heads = mm_exact_left(jnp.concatenate([kept, skip_part, jnp.zeros((6, width), F32)], axis=0), ones)
    dstate[...] = last_chan * grown + mm3(c_coef, ey_parts, TN)
    gaps = rows[...].T - from_rows + end_terms
    d_decay = (
        mm_exact(later.astype(BF16), gaps)
        + mm_exact(triangle(lambda row, col: col < row).astype(BF16), start_terms)
        + kept_heads[0:1, :]
    )
    d_step = head_sum(d_scaled * values, ones) + d_decay * heads_ref[1:2, :]
    d_raw = d_step * jax.nn.sigmoid(biased)
    head_grad_ref[0:1, :] += jnp.sum(d_raw, axis=0, keepdims=True)
    head_grad_ref[1:2, :] += jnp.sum(d_decay * decay, axis=0, keepdims=True)
    head_grad_ref[2:3, :] += kept_heads[1:2, :]
    d_values = (d_scaled * step_chan + skip_ref[0:1, :] * dy) * mask
    d_conv = jnp.concatenate([d_b, d_c, d_values], axis=1)
    d_pre = d_conv * (sig * (1.0 + pre * (1.0 - sig)))
    conv_grad_ref[4:5, :] += jnp.sum(d_pre, axis=0, keepdims=True)
    dext[BLOCK : BLOCK + 8, :] = dext[0:8, :]
    dext[0:BLOCK, :] = d_pre
    conv_in = proj_ref[:, width : width + joint].astype(F32)
    d_in = None
    for tap in range(4):
        ahead = d_pre if tap == 3 else dext[3 - tap : 3 - tap + BLOCK, :]
        conv_grad_ref[tap : tap + 1, :] += jnp.sum(ahead * conv_in, axis=0, keepdims=True)
        d_in = ahead * taps_ref[tap : tap + 1, :] if tap == 0 else d_in + ahead * taps_ref[tap : tap + 1, :]
    dproj_ref[:, width : width + joint] = d_in.astype(BF16)
    dproj_ref[:, joint + width :] = d_raw.astype(BF16)


def mm_exact_left(value, ones):
    first = value.astype(BF16)
    rest = value - first.astype(F32)
    second = rest.astype(BF16)
    third = (rest - second.astype(F32)).astype(BF16)
    return mm(first, ones) + (mm(second, ones) + mm(third, ones))


def mixer_forward(mask, hidden, weight, taps, heads, skip, state_dim, width):
    seqs = mask.shape[0]
    tokens, depth = hidden.shape
    blocks = tokens // seqs // BLOCK
    columns = weight.shape[1]
    joint = 2 * state_dim + width
    row = lambda s, c: (s * blocks + c, 0)
    whole = lambda s, c: (0, 0)
    return pl.pallas_call(
        lambda *refs: forward_kernel(*refs, state_dim=state_dim, width=width),
        grid=(seqs, blocks),
        in_specs=[
            pl.BlockSpec((1, 1, width), lambda s, c: (s, 0, 0)),
            pl.BlockSpec((BLOCK, depth), row),
            pl.BlockSpec((depth, columns), whole),
            pl.BlockSpec((8, joint), whole),
            pl.BlockSpec((8, LANES), whole),
            pl.BlockSpec((8, width), whole),
        ],
        out_specs=[
            pl.BlockSpec((BLOCK, columns), row),
            pl.BlockSpec((BLOCK, width), row),
            pl.BlockSpec((1, state_dim, width), lambda s, c: (s * blocks + c, 0, 0)),
            pl.BlockSpec((1, 8, BLOCK), lambda s, c: (s * blocks + c, 0, 0)),
            pl.BlockSpec((BLOCK, joint), row),
        ],
        out_shape=[
            jax.ShapeDtypeStruct((tokens, columns), BF16),
            jax.ShapeDtypeStruct((tokens, width), BF16),
            jax.ShapeDtypeStruct((seqs * blocks, state_dim, width), F32),
            jax.ShapeDtypeStruct((seqs * blocks, 8, BLOCK), F32),
            jax.ShapeDtypeStruct((tokens, joint), F32),
        ],
        scratch_shapes=[
            pltpu.VMEM((BLOCK + 8, joint), F32),
            pltpu.VMEM((state_dim, width), F32),
        ],
        compiler_params=pltpu.CompilerParams(
            dimension_semantics=("arbitrary", "arbitrary"), vmem_limit_bytes=VMEM
        ),
        cost_estimate=FREE,
        name="mixer_forward",
    )(mask, hidden, weight, taps, heads, skip)


def mixer_backward(gains, projected, pre, y_all, d_normed, token_rows, states, taps, heads, skip, state_dim):
    seqs, _, width = gains.shape
    tokens, columns = projected.shape
    blocks = tokens // seqs // BLOCK
    joint = 2 * state_dim + width
    place = lambda s, c: s * blocks + blocks - 1 - c
    row = lambda s, c: (place(s, c), 0)
    block = lambda s, c: (place(s, c), 0, 0)
    whole = lambda s, c: (0, 0)
    return pl.pallas_call(
        lambda *refs: backward_kernel(*refs, state_dim=state_dim, width=width),
        grid=(seqs, blocks),
        in_specs=[
            pl.BlockSpec((1, 8, width), lambda s, c: (s, 0, 0)),
            pl.BlockSpec((BLOCK, columns), row),
            pl.BlockSpec((BLOCK, joint), row),
            pl.BlockSpec((BLOCK, width), row),
            pl.BlockSpec((BLOCK, width), row),
            pl.BlockSpec((1, 8, BLOCK), block),
            pl.BlockSpec((1, state_dim, width), block),
            pl.BlockSpec((8, joint), whole),
            pl.BlockSpec((8, LANES), whole),
            pl.BlockSpec((8, width), whole),
        ],
        out_specs=[
            pl.BlockSpec((BLOCK, columns), row),
            pl.BlockSpec((8, joint), whole),
            pl.BlockSpec((8, LANES), whole),
            pl.BlockSpec((8, width), whole),
        ],
        out_shape=[
            jax.ShapeDtypeStruct((tokens, columns), BF16),
            jax.ShapeDtypeStruct((8, joint), F32),
            jax.ShapeDtypeStruct((8, LANES), F32),
            jax.ShapeDtypeStruct((8, width), F32),
        ],
        scratch_shapes=[
            pltpu.VMEM((BLOCK + 8, joint), F32),
            pltpu.VMEM((state_dim, width), F32),
            pltpu.VMEM((LANES, BLOCK), F32),
        ],
        compiler_params=pltpu.CompilerParams(
            dimension_semantics=("arbitrary", "arbitrary"), vmem_limit_bytes=VMEM
        ),
        cost_estimate=FREE,
        name="mixer_backward",
    )(gains, projected, pre, y_all, d_normed, token_rows, states, taps, heads, skip)


def row_sum(value):
    ones = jnp.ones((8, value.shape[1]), BF16)
    high, low = halves(value)
    return mm(ones, high, NT) + mm(ones, low, NT)


def pull_kernel(cot_ref, weight_ref, gate_ref, y_ref, gain_ref, d_normed_ref, dot_ref):
    d_normed = mm(cot_ref[...], weight_ref[...], NT)
    d_normed_ref[...] = d_normed
    gate = gate_ref[...].astype(F32)
    gated = y_ref[...].astype(F32) * (gate * jax.nn.sigmoid(gate))
    dot_ref[0] = row_sum(d_normed * gain_ref[0, 0:1, :] * gated)


def pull_back(cot_all, weight, projected, y_all, gains, gate_place):
    seqs, _, width = gains.shape
    tokens, depth = cot_all.shape
    blocks = tokens // seqs // BLOCK
    row = lambda s, c: (s * blocks + c, 0)
    return pl.pallas_call(
        pull_kernel,
        grid=(seqs, blocks),
        in_specs=[
            pl.BlockSpec((BLOCK, depth), row),
            pl.BlockSpec((width, depth), lambda s, c: (0, 0)),
            pl.BlockSpec((BLOCK, width), lambda s, c: (s * blocks + c, gate_place)),
            pl.BlockSpec((BLOCK, width), row),
            pl.BlockSpec((1, 8, width), lambda s, c: (s, 0, 0)),
        ],
        out_specs=[
            pl.BlockSpec((BLOCK, width), row),
            pl.BlockSpec((1, 8, BLOCK), lambda s, c: (s * blocks + c, 0, 0)),
        ],
        out_shape=[
            jax.ShapeDtypeStruct((tokens, width), F32),
            jax.ShapeDtypeStruct((seqs * blocks, 8, BLOCK), F32),
        ],
        compiler_params=pltpu.CompilerParams(
            dimension_semantics=("arbitrary", "arbitrary"), vmem_limit_bytes=VMEM
        ),
        cost_estimate=FREE,
        name="pull_back",
    )(cot_all, weight, projected, y_all, gains)


def pad_last(array, size):
    extra = size - array.shape[-1]
    if extra == 0:
        return array
    return jnp.pad(array, [(0, 0)] * (array.ndim - 1) + [(0, extra)])


def pad_rows(array, size):
    return jnp.pad(array, [(0, size - array.shape[0]), (0, 0)])


def swap(value, axis, bit):
    size = lax.axis_size(axis)
    return lax.ppermute(value, axis, [(place, place ^ bit) for place in range(size)])


def all_sum(value, axis):
    bit = 1
    while bit < lax.axis_size(axis):
        value = value + swap(value, axis, bit)
        bit *= 2
    return value


NEAR_FAR = ((1, 2), (2, 1))


def reduce_cut(share, block, dtype):
    return [
        jnp.concatenate([block(share, near ^ far, half), block(share, near, half)], axis=0).astype(dtype)
        for half, (near, far) in enumerate(NEAR_FAR)
    ]


def reduce_near(cuts):
    return [swap(cut, "dp", near) for cut, (near, _) in zip(cuts, NEAR_FAR)]


def reduce_far(share, block, got):
    rows = got[0].shape[0] // 2
    kept = [
        (block(share, far, half) + got[half][:rows].astype(F32)).astype(got[half].dtype)
        for half, (_, far) in enumerate(NEAR_FAR)
    ]
    mine = [block(share, 0, half) + got[half][rows:].astype(F32) for half in range(2)]
    kept = lax.optimization_barrier(kept)
    far_got = [swap(piece, "dp", far) for piece, (_, far) in zip(kept, NEAR_FAR)]
    return jnp.concatenate([piece + other.astype(F32) for piece, other in zip(mine, far_got)], axis=0)


def gather_near(own):
    rows = own.shape[0] // 2
    upper, lower = own[:rows], own[rows:]
    return upper, lower, swap(upper, "dp", 1), swap(lower, "dp", 2)


def gather_far(first):
    upper, lower, upper1, lower2 = first
    rows = upper.shape[0]
    uppers = swap(jnp.concatenate([upper, upper1], axis=0), "dp", 2)
    lowers = swap(jnp.concatenate([lower, lower2], axis=0), "dp", 1)
    return [(upper, lower), (upper1, lowers[:rows]), (uppers[:rows], lower2), (uppers[rows:], lowers[rows:])]


def line_permute(block, reach):
    chips = lax.axis_size("mp") // 2
    pairs = [(2 * z + c, 2 * ((z + reach) % chips) + c) for z in range(chips) for c in range(2)]
    return lax.ppermute(block, "mp", pairs)


def line_send(shares):
    groups = [list(range(core, lax.axis_size("mp"), 2)) for core in range(2)]
    return lax.all_to_all(shares, "mp", split_axis=0, concat_axis=0, axis_index_groups=groups, tiled=True)


def pair_kernel(place_ref, own_ref, sibling_ref, own_weight_ref, sibling_weight_ref, *out_refs, dims):
    share = mm(own_ref[...], own_weight_ref[...], dims) + mm(sibling_ref[...], sibling_weight_ref[...], dims)
    share = share.astype(BF16)
    if len(out_refs) == 1:
        out_refs[0][0] = share
        return
    for reach, out_ref in enumerate(out_refs):

        @pl.when(pl.program_id(0) == reach)
        def _(out_ref=out_ref):
            out_ref[...] = share


def pair_product(left, theirs, own_weight, sibling_weight, dims, depth, tokens, stacked):
    chips = lax.axis_size("mp") // 2
    inner = left.shape[1]
    whole = lambda i, place: (0, 0)
    place = lax.axis_index("mp").astype(jnp.int32)
    there = lambda i, place: lax.rem(place[0] + i, chips)
    return pl.pallas_call(
        lambda *refs: pair_kernel(*refs, dims=dims),
        grid_spec=pltpu.PrefetchScalarGridSpec(
            num_scalar_prefetch=1,
            grid=(chips,),
            in_specs=[
                pl.BlockSpec((tokens, inner), lambda i, place: (2 * there(i, place) + place[1], 0)),
                pl.BlockSpec((tokens, inner), lambda i, place: (there(i, place), 0)),
                pl.BlockSpec(own_weight.shape, whole),
                pl.BlockSpec(sibling_weight.shape, whole),
            ],
            out_specs=[pl.BlockSpec((1, tokens, depth), lambda i, place: (there(i, place), 0, 0))]
            if stacked
            else [pl.BlockSpec((tokens, depth), whole)] * chips,
        ),
        out_shape=[jax.ShapeDtypeStruct((chips, tokens, depth), BF16)]
        if stacked
        else [jax.ShapeDtypeStruct((tokens, depth), BF16)] * chips,
        compiler_params=pltpu.CompilerParams(dimension_semantics=("arbitrary",), vmem_limit_bytes=VMEM),
        cost_estimate=FREE,
        name="pair_product",
    )(jnp.stack([place // 2, place % 2]), left, theirs, own_weight, sibling_weight)


def for_sibling(left, tokens):
    mp = lax.axis_size("mp")
    by_core = left.reshape(mp // 2, 2, tokens, left.shape[1])
    other = 1 - lax.axis_index("mp") % 2
    return lax.dynamic_index_in_dim(by_core, other, 1, keepdims=False).reshape(-1, left.shape[1])


def in_place_order(pieces):
    place = lax.axis_index("dp")
    pieces = [jnp.concatenate(pair, axis=0) for pair in pieces]
    odd, high = place % 2 == 1, place // 2 == 1
    lows = [jnp.where(odd, pieces[k ^ 1], pieces[k]) for k in range(4)]
    return jnp.concatenate([jnp.where(high, lows[k ^ 2], lows[k]).astype(F32) for k in range(4)], axis=0)


def assemble_kernel(place_ref, *refs):
    out_ref = refs[-1]
    for own in range(4):

        @pl.when(place_ref[0] == own)
        def _(own=own):
            order = [refs[2 * (own ^ p) + half][...].astype(F32) for p in range(4) for half in range(2)]
            out_ref[...] = jnp.concatenate(order, axis=0).T


def assemble(gathered):
    pieces = [half for pair in gathered for half in pair]
    half_rows, columns = pieces[0].shape
    chunk = 512
    return pl.pallas_call(
        assemble_kernel,
        grid=(pl.cdiv(columns, chunk),),
        in_specs=[pl.BlockSpec(memory_space=pltpu.SMEM)]
        + [pl.BlockSpec((half_rows, chunk), lambda i: (0, i)) for _ in pieces],
        out_specs=pl.BlockSpec((chunk, 8 * half_rows), lambda i: (i, 0)),
        out_shape=jax.ShapeDtypeStruct((columns, 8 * half_rows), F32),
        compiler_params=pltpu.CompilerParams(dimension_semantics=("arbitrary",), vmem_limit_bytes=VMEM),
        cost_estimate=FREE,
        name="assemble",
    )(lax.axis_index("dp").astype(jnp.int32)[None], *pieces).T


def total(blocks):
    result = blocks[0].astype(F32)
    for index in range(1, len(blocks)):
        result = result + blocks[index].astype(F32)
    return result


def on_device(
    inputs, cotangent, widths, norm_gain, in_weight, conv_weight, conv_bias, step_bias, rate_log,
    skip_gain, out_gain, out_weight,
):
    mp, dp = lax.axis_size("mp"), lax.axis_size("dp")
    mp_place, dp_place = lax.axis_index("mp"), lax.axis_index("dp")
    heads, inner, channels = step_bias.shape[0], out_gain.shape[0], conv_bias.shape[0]
    head_dim, state_dim = inner // heads, (channels - inner) // 2
    own_heads = heads // mp
    own = own_heads * head_dim
    width = -(-own // LANES) * LANES
    joint = 2 * state_dim + width
    columns = joint + width + LANES
    tokens, depth = inputs.shape
    rows = depth // mp
    part = rows // dp
    seqs = widths.shape[0]
    all_tokens = tokens * mp

    slab = lax.dynamic_slice_in_dim(in_weight, dp_place * part, part, 0)
    by_place = lambda piece, size: pad_last(
        piece.reshape(part, mp, piece.shape[1] // mp).transpose(1, 0, 2), size
    )
    send = jnp.concatenate(
        [
            by_place(slab[:, :inner], width),
            jnp.broadcast_to(slab[None, :, 2 * inner : 2 * inner + 2 * state_dim], (mp, part, 2 * state_dim)),
            by_place(slab[:, inner : 2 * inner], width),
            by_place(slab[:, inner + channels :], LANES),
        ],
        axis=2,
    )
    got = lax.all_to_all(send, "mp", split_axis=0, concat_axis=0, tiled=True)

    def reorder(array):
        apart = array.reshape(-1, mp, dp, part)
        return jnp.concatenate(
            [
                lax.dynamic_index_in_dim(apart, dp_place ^ k, 2, keepdims=False).reshape(-1, mp * part)
                for k in range(dp)
            ],
            axis=1,
        )

    def restore(array):
        apart = array.reshape(-1, dp, mp, part)
        return jnp.stack(
            [lax.dynamic_index_in_dim(apart, dp_place ^ k, 1, keepdims=False) for k in range(dp)], axis=2
        ).reshape(-1, depth)

    line = mp <= 16
    inputs_f = inputs.astype(F32)
    rms_scale = lax.rsqrt(jnp.mean(inputs_f * inputs_f, axis=-1, keepdims=True) + EPS)
    normed = inputs_f * rms_scale
    hidden_own = reorder((normed * norm_gain[None, :]).astype(BF16))
    hidden_own, got = lax.optimization_barrier((hidden_own, got))
    weight = jnp.concatenate(sum(gather_far(gather_near(got.reshape(mp * part, columns))), ()), axis=0)
    hidden = lax.all_gather(hidden_own, "mp", axis=0, tiled=True)

    first_chan, first_head = mp_place * own, mp_place * own_heads
    cut = lambda array, first, size: lax.dynamic_slice_in_dim(array, first, size, array.ndim - 1)
    taps_all = jnp.concatenate([conv_weight, conv_bias[None, :]], axis=0)
    taps = pad_rows(
        jnp.concatenate([taps_all[:, inner:], pad_last(cut(taps_all, first_chan, own), width)], axis=1), 8
    )
    head_rows = jnp.stack([step_bias, -jnp.exp(rate_log)])
    head_params = pad_rows(pad_last(cut(head_rows, first_head, own_heads), LANES), 8)
    skip = jnp.repeat(cut(skip_gain, first_head, own_heads), head_dim)[None, :]
    skip = pad_rows(pad_last(skip, width), 8)
    active_heads = heads // 8 * jnp.left_shift(jnp.int32(1), widths)
    head_mask = (first_head + jnp.arange(own_heads, dtype=jnp.int32))[None, :] < active_heads[:, None]
    chan_mask = jnp.repeat(head_mask.astype(F32), head_dim, axis=1)
    mask = pad_last(chan_mask, width)[:, None, :]
    per_token = lambda array: jnp.repeat(array, all_tokens // seqs, axis=0)
    mask_tok = chan_mask if seqs == 1 else per_token(chan_mask)
    active_count = (active_heads * head_dim).astype(F32)[:, None]
    if seqs > 1:
        active_count = per_token(active_count)

    if line:
        sibling_out, sibling_weight = swap(out_weight, "mp", 1), swap(weight, "mp", 1)
        weight, sibling_out, sibling_weight = lax.optimization_barrier((weight, sibling_out, sibling_weight))
    projected, y_all, states, squares, pre = mixer_forward(
        mask, hidden, weight, taps, head_params, skip, state_dim, width
    )
    square_rows = all_sum(squares[:, 0, :], "mp")
    total_square = square_rows.reshape(all_tokens)[:, None]
    gate = projected[:, :own].astype(F32)
    y_f = y_all[:, :own].astype(F32)
    gate_sig = jax.nn.sigmoid(gate)
    silu_z = gate * gate_sig
    gated = y_f * silu_z
    gain = cut(out_gain, first_chan, own)[None, :]
    out_root = lax.rsqrt(total_square / active_count + EPS)
    normed_out = (gated * out_root * gain * mask_tok).astype(BF16)
    if line:
        theirs = swap(for_sibling(normed_out, tokens), "mp", 1)
        shares = pair_product(normed_out, theirs, out_weight, sibling_out, NN, depth, tokens, True)[0]
        cot_all = lax.all_gather(cotangent, "mp", axis=0, tiled=True)
        cot_all, shares = lax.optimization_barrier((cot_all, shares))
    else:
        shares = mm(normed_out, out_weight).astype(BF16)
        sent = [lax.psum_scatter(shares, "mp", scatter_dimension=0, tiled=True)]
        late_cot, sent = lax.optimization_barrier((cotangent, sent))
        cot_all = lax.all_gather(late_cot, "mp", axis=0, tiled=True)

    gain_rows = pad_last(cut(out_gain, first_chan, own), width)
    gains = jnp.concatenate(
        [
            gain_rows[None, None, :] * mask,
            mask,
            jnp.broadcast_to((active_heads * head_dim).astype(F32)[:, None, None], mask.shape),
            jnp.zeros((seqs, 5, width), F32),
        ],
        axis=1,
    )
    out_padded = pad_rows(out_weight, width)
    d_normed, dots = pull_back(cot_all, out_padded, projected, y_all, gains, 0)
    dot_rows = all_sum(dots[:, 0, :], "mp")
    out_part = mm(normed_out, cot_all, TN)
    if line:
        dot_rows, shares = lax.optimization_barrier((dot_rows, shares))
        sent = line_send(shares)
    token_rows = jnp.stack([square_rows, dot_rows] + [jnp.zeros_like(dot_rows)] * 6, axis=1)
    quarter = depth // dp

    def in_block(share, k, half):
        return share[k * quarter + half * (quarter // 2) : k * quarter + (half + 1) * (quarter // 2)]

    def to_rows(mine):
        return lax.all_to_all(mine.astype(BF16).reshape(mp, part, -1), "mp", split_axis=0, concat_axis=0, tiled=True)

    token_rows, out_part = lax.optimization_barrier((token_rows, out_part))
    out_mine = lax.psum_scatter(out_part, "dp", scatter_dimension=0, tiled=True)
    def rows_of(blocks):
        flat = lambda first, size: blocks[:, :, first : first + size].transpose(1, 0, 2).reshape(part, -1)
        shared = jnp.sum(blocks[:, :, width : width + 2 * state_dim].astype(F32), axis=0).astype(BF16)
        return jnp.concatenate(
            [flat(0, own), flat(width + 2 * state_dim, own), shared, flat(width + joint, own_heads)], axis=1
        )

    d_proj, conv_grads, head_grads, gain_grads = mixer_backward(
        gains, projected, pre, y_all, d_normed, token_rows, states, taps, head_params, skip, state_dim
    )
    d_proj, out_mine = lax.optimization_barrier((d_proj, out_mine))
    out_weight_grad = lax.all_gather(out_mine, "dp", axis=0, tiled=True)

    def place_in(array, first, size):
        return lax.dynamic_update_slice_in_dim(
            jnp.zeros(array.shape[:-1] + (size,), F32), array, first, array.ndim - 1
        )

    conv_own = place_in(conv_grads[:5, 2 * state_dim : 2 * state_dim + own], first_chan, inner)
    conv_full = jnp.concatenate([conv_own, conv_grads[:5, : 2 * state_dim]], axis=1)
    head_full = place_in(head_grads[:3, :own_heads], first_head, heads)
    gain_full = place_in(gain_grads[0, :own], first_chan, inner)
    small = [conv_full.reshape(-1), head_full.reshape(-1), gain_full]
    sizes = [piece.shape[0] for piece in small]
    packed = jnp.concatenate(small)
    count = -(-packed.shape[0] // 1024) * 1024
    packed = jnp.pad(packed, (0, count - packed.shape[0])).reshape(-1, LANES)

    if line:
        theirs = swap(for_sibling(d_proj, tokens), "mp", 1)
        d_shares = pair_product(d_proj, theirs, weight, sibling_weight, NT, depth, tokens, False)
        d_shares, d_proj, sent = lax.optimization_barrier((d_shares, d_proj, sent))
        reaches = [1] + list(range(mp // 2 - 1, 1, -1))
        d_blocks = [d_shares[0], line_permute(d_shares[1], 1)]
        share = mm(hidden, d_proj, TN)
        near_cut = reduce_cut(share, in_block, BF16)
        near_cut, d_blocks, out_weight_grad = lax.optimization_barrier((near_cut, d_blocks, out_weight_grad))
        near_got = reduce_near(near_cut)
        d_blocks += [line_permute(d_shares[reach], reach) for reach in reaches[1:2]]
        near_got, d_blocks = lax.optimization_barrier((near_got, d_blocks))
        mine = reduce_far(share, in_block, near_got)
        mine, packed = lax.optimization_barrier((mine, packed))
        blocks = to_rows(mine)
        blocks, d_shares, packed = lax.optimization_barrier((blocks, d_shares, all_sum(packed, "dp")))
        d_blocks += [line_permute(d_shares[reach], reach) for reach in reaches[2:]]
        gathered = gather_far(gather_near(rows_of(blocks)))
        in_weight_grad, d_blocks = lax.optimization_barrier((assemble(gathered), d_blocks))
        d_hidden = total(d_blocks)
    else:
        packed = all_sum(packed, "dp")
        share = mm(hidden, d_proj, TN)
        d_proj, share = lax.optimization_barrier((d_proj, share))
        blocks = to_rows(reduce_far(share, in_block, reduce_near(reduce_cut(share, in_block, BF16))))
        d_shares = mm(d_proj, weight, NT).astype(BF16)
        d_hidden = lax.psum_scatter(d_shares, "mp", scatter_dimension=0, tiled=True).astype(F32)
        in_weight_grad = in_place_order(gather_far(gather_near(rows_of(blocks))))
    outputs = (inputs_f + total(sent)).astype(BF16)
    d_hidden = restore(d_hidden)
    norm_gain_grad = jnp.sum(d_hidden * normed, axis=0)
    norm_part = all_sum(norm_gain_grad.reshape(-1, LANES), "dp")
    everything = all_sum(jnp.concatenate([packed, norm_part], axis=0), "mp")
    norm_total = everything[packed.shape[0] :].reshape(depth)
    packed = everything.reshape(-1)
    conv_total = packed[: sizes[0]].reshape(conv_full.shape)
    head_total = packed[sizes[0] : sizes[0] + sizes[1]].reshape(head_full.shape)
    gain_total = packed[sizes[0] + sizes[1] : sum(sizes)]

    d_normed_in = d_hidden * norm_gain[None, :]
    input_back = rms_scale * (d_normed_in - normed * jnp.mean(d_normed_in * normed, axis=-1, keepdims=True))
    input_grad = (cotangent.astype(F32) + input_back).astype(BF16)

    return (
        outputs,
        input_grad,
        norm_total,
        in_weight_grad,
        conv_total[:4],
        conv_total[4],
        head_total[0],
        head_total[1],
        head_total[2],
        gain_total,
        out_weight_grad,
    )


def solution(mesh):
    rows = P(("dp", "mp"), None)
    return jax.shard_map(
        on_device,
        mesh=mesh,
        in_specs=(rows, rows, P("dp"), P(), P("mp", None), P(), P(), P(), P(), P(), P(), P("mp", None)),
        out_specs=(rows, rows, P(), P("mp", None), P(), P(), P(), P(), P(), P(), P("mp", None)),
        check_vma=False,
    )
```

```python
import jax
import jax.numpy as jnp
from jax import lax
from jax.experimental import pallas as pl
from jax.experimental.pallas import tpu as pltpu
from jax.sharding import PartitionSpec as P

SEQ = 2048
BLOCK = 256
EPS = 1e-05
LANES = 128
VMEM = 56 * 2**20
FREE = pl.CostEstimate(flops=1, bytes_accessed=1, transcendentals=0)

F32 = jnp.float32
BF16 = jnp.bfloat16
NN = (((1,), (0,)), ((), ()))
NT = (((1,), (1,)), ((), ()))
TN = (((0,), (0,)), ((), ()))


def mm(left, right, dims=NN):
    return lax.dot_general(left, right, dims, preferred_element_type=F32)


def halves(value):
    high = value.astype(BF16)
    return high, (value - high.astype(F32)).astype(BF16)


def mm3(left, right, dims=NN):
    return mm(left[0], right[0], dims) + (mm(left[0], right[1], dims) + mm(left[1], right[0], dims))


def mm_exact(ones, value, dims=NN):
    first, rest = value.astype(BF16), None
    rest = value - first.astype(F32)
    second = rest.astype(BF16)
    third = (rest - second.astype(F32)).astype(BF16)
    return mm(ones, first, dims) + (mm(ones, second, dims) + mm(ones, third, dims))


def spread(per_head, width):
    rows = per_head.shape[0]
    low_half = lax.broadcasted_iota(jnp.int32, (rows, LANES), 1) < LANES // 2
    parts = []
    for pair in range(width // LANES):
        parts.append(
            jnp.where(
                low_half, per_head[:, 2 * pair : 2 * pair + 1], per_head[:, 2 * pair + 1 : 2 * pair + 2]
            )
        )
    return parts[0] if len(parts) == 1 else jnp.concatenate(parts, axis=1)


def head_ones(width):
    chan = lax.broadcasted_iota(jnp.int32, (width, LANES), 0)
    head = lax.broadcasted_iota(jnp.int32, (width, LANES), 1)
    return (chan // (LANES // 2) == head).astype(BF16)


def head_sum(per_chan, ones):
    high, low = halves(per_chan)
    return mm(high, ones) + mm(low, ones)


def conv_block(ext_ref, taps_ref):
    span = 4
    pre = taps_ref[span : span + 1, :] + ext_ref[5 : 5 + BLOCK, :] * taps_ref[0:1, :]
    for tap in range(1, span):
        pre = pre + ext_ref[5 + tap : 5 + tap + BLOCK, :] * taps_ref[tap : tap + 1, :]
    return pre


def step_rates(step_raw, heads_ref):
    biased = step_raw + heads_ref[0:1, :]
    step_size = jnp.maximum(biased, 0.0) + jnp.log1p(jnp.exp(-jnp.abs(biased)))
    decay = heads_ref[1:2, :] * step_size
    return biased, step_size, decay


def triangle(keep):
    row = lax.broadcasted_iota(jnp.int32, (BLOCK, BLOCK), 0)
    col = lax.broadcasted_iota(jnp.int32, (BLOCK, BLOCK), 1)
    return keep(row, col)


def forward_kernel(
    mask_ref, hidden_ref, weight_ref, taps_ref, heads_ref, skip_ref,
    proj_ref, y_ref, state_ref, square_ref, pre_ref,
    ext, state, *, state_dim, width,
):
    joint = 2 * state_dim + width

    @pl.when(pl.program_id(1) == 0)
    def _():
        ext[0:8, :] = jnp.zeros((8, joint), F32)
        state[...] = jnp.zeros_like(state)

    projected = mm(hidden_ref[...], weight_ref[...]).astype(BF16)
    proj_ref[...] = projected
    ext[8 : 8 + BLOCK, :] = projected[:, width : width + joint].astype(F32)
    pre = conv_block(ext, taps_ref)
    pre_ref[...] = pre
    ext[0:8, :] = ext[BLOCK : BLOCK + 8, :]
    conv_out = pre * jax.nn.sigmoid(pre)
    values = conv_out[:, 2 * state_dim :] * mask_ref[0]
    b_coef = halves(conv_out[:, :state_dim])
    c_coef = halves(conv_out[:, state_dim : 2 * state_dim])
    _, step_size, decay = step_rates(projected[:, joint + width :].astype(F32), heads_ref)
    causal = triangle(lambda row, col: row >= col)
    cumulative = mm_exact(causal.astype(BF16), decay)
    across = cumulative.T
    last = cumulative[BLOCK - 1 : BLOCK, :]
    scaled = values * spread(step_size, width)
    scaled_parts = halves(scaled)
    scores = mm3(c_coef, b_coef, NT)
    low_half = lax.broadcasted_iota(jnp.int32, (BLOCK, LANES), 1) < LANES // 2
    old = state[...]
    state_ref[0] = old
    mixed = spread(jnp.exp(cumulative), width) * mm3(c_coef, halves(old))
    within = []
    for pair in range(width // LANES):
        lanes = slice(pair * LANES, (pair + 1) * LANES)
        rhs = (scaled_parts[0][:, lanes], scaled_parts[1][:, lanes])
        sides = []
        for head in (2 * pair, 2 * pair + 1):
            gap = jnp.where(causal, cumulative[:, head : head + 1] - across[head : head + 1, :], -1e30)
            sides.append(mm3(halves(scores * jnp.exp(gap)), rhs))
        within.append(jnp.where(low_half, sides[0], sides[1]))
    mixed = mixed + (within[0] if len(within) == 1 else jnp.concatenate(within, axis=1))
    tail = halves(scaled * spread(jnp.exp(last - cumulative), width))
    state[...] = old * spread(jnp.exp(last), width) + mm3(b_coef, tail, TN)
    y_low = (mixed + skip_ref[0:1, :] * values).astype(BF16)
    y_ref[...] = y_low
    gate = projected[:, :width].astype(F32)
    gated = y_low.astype(F32) * (gate * jax.nn.sigmoid(gate))
    square = halves(gated * gated * mask_ref[0])
    ones = jnp.ones((8, width), BF16)
    square_ref[0] = mm(ones, square[0], NT) + mm(ones, square[1], NT)


def backward_kernel(
    gain_ref, proj_ref, pre_ref, y_ref, d_normed_ref, tokens_ref, state_ref, taps_ref, heads_ref, skip_ref,
    dproj_ref, conv_grad_ref, head_grad_ref, gain_grad_ref,
    dext, dstate, rows, *, state_dim, width,
):
    joint = 2 * state_dim + width

    @pl.when((pl.program_id(0) == 0) & (pl.program_id(1) == 0))
    def _():
        conv_grad_ref[...] = jnp.zeros_like(conv_grad_ref)
        head_grad_ref[...] = jnp.zeros_like(head_grad_ref)
        gain_grad_ref[...] = jnp.zeros_like(gain_grad_ref)
        rows[...] = jnp.zeros_like(rows)

    @pl.when(pl.program_id(1) == 0)
    def _():
        dext[0:8, :] = jnp.zeros((8, joint), F32)
        dstate[...] = jnp.zeros_like(dstate)

    per_token = tokens_ref[0].T
    count = gain_ref[0, 2:3, 0:1]
    root = lax.rsqrt(per_token[:, 0:1] / count + EPS)
    pull = root * root * per_token[:, 1:2] / count
    gate = proj_ref[:, :width].astype(F32)
    y = y_ref[...].astype(F32)
    gate_sig = jax.nn.sigmoid(gate)
    silu = gate * gate_sig
    normed_gated = y * silu * root * gain_ref[0, 1:2, :]
    d_normed = d_normed_ref[...]
    gain_grad_ref[0:1, :] += jnp.sum(d_normed * normed_gated, axis=0, keepdims=True)
    d_gated = root * (d_normed * gain_ref[0, 0:1, :]) - normed_gated * pull
    dy_low = (d_gated * silu).astype(BF16)
    dproj_ref[:, :width] = (d_gated * y * gate_sig * (1.0 + gate * (1.0 - gate_sig))).astype(BF16)

    pre = pre_ref[...]
    sig = jax.nn.sigmoid(pre)
    conv_out = pre * sig
    mask = gain_ref[0, 1:2, :]
    values = conv_out[:, 2 * state_dim :] * mask
    b_coef = halves(conv_out[:, :state_dim])
    c_coef = halves(conv_out[:, state_dim : 2 * state_dim])
    biased, step_size, decay = step_rates(proj_ref[:, joint + width :].astype(F32), heads_ref)
    later = triangle(lambda row, col: col >= row)
    cumulative = mm_exact(triangle(lambda row, col: row >= col).astype(BF16), decay)
    across = cumulative.T
    last = cumulative[BLOCK - 1 : BLOCK, :]
    step_chan = spread(step_size, width)
    scaled = values * step_chan
    scaled_parts = halves(scaled)
    dy = dy_low.astype(F32)
    scores = mm3(b_coef, c_coef, NT)
    low_half = lax.broadcasted_iota(jnp.int32, (BLOCK, LANES), 1) < LANES // 2
    lane = lax.broadcasted_iota(jnp.int32, (BLOCK, LANES), 1)
    d_scores = jnp.zeros((BLOCK, BLOCK), F32)
    from_rows = jnp.zeros((BLOCK, LANES), F32)
    d_within = []
    for pair in range(width // LANES):
        lanes = slice(pair * LANES, (pair + 1) * LANES)
        dy_pair = dy_low[:, lanes]
        dy_twice = jnp.concatenate([dy_pair, dy_pair], axis=1)
        sides = []
        for side in range(2):
            head = 2 * pair + side
            own = low_half if side == 0 else jnp.logical_not(low_half)
            left = jnp.concatenate(
                [jnp.where(own, part[:, lanes], jnp.zeros((), BF16)) for part in scaled_parts], axis=1
            )
            d_mixing = mm(left, dy_twice, NT)
            gap = jnp.where(later, across[head : head + 1, :] - cumulative[:, head : head + 1], -1e30)
            weight = jnp.exp(gap)
            mixing = scores * weight
            d_scores = d_scores + d_mixing * weight
            product = d_mixing * mixing
            rows[head : head + 1, :] = jnp.sum(product, axis=0, keepdims=True)
            from_rows = jnp.where(lane == head, jnp.sum(product, axis=1, keepdims=True), from_rows)
            parts = halves(mixing)
            sides.append(mm(parts[0], dy_pair) + mm(parts[1], dy_pair))
        d_within.append(jnp.where(low_half, sides[0], sides[1]))
    ones = head_ones(width)
    old = state_ref[0]
    old_parts = halves(old)
    grown = dstate[...]
    grown_parts = halves(grown)
    ey = spread(jnp.exp(cumulative), width) * dy
    ey_parts = halves(ey)
    tail_chan = spread(jnp.exp(last - cumulative), width)
    tail = scaled * tail_chan
    tail_parts = halves(tail)
    last_chan = spread(jnp.exp(last), width)
    into_state = mm3(b_coef, grown_parts)
    d_scaled = (d_within[0] if len(d_within) == 1 else jnp.concatenate(d_within, axis=1)) + tail_chan * into_state
    d_parts = halves(d_scores)
    d_c = mm3(d_parts, b_coef, TN) + mm3(ey_parts, old_parts, NT)
    d_b = mm3(d_parts, c_coef) + mm3(tail_parts, grown_parts, NT)
    end_terms = head_sum(ey * mm3(c_coef, old_parts), ones)
    start_terms = head_sum(tail * into_state, ones)
    kept = jnp.sum(last_chan * grown * old, axis=0, keepdims=True)
    skip_part = jnp.sum(dy * values, axis=0, keepdims=True)
    kept_heads = mm_exact_left(jnp.concatenate([kept, skip_part, jnp.zeros((6, width), F32)], axis=0), ones)
    dstate[...] = last_chan * grown + mm3(c_coef, ey_parts, TN)
    gaps = rows[...].T - from_rows + end_terms
    d_decay = (
        mm_exact(later.astype(BF16), gaps)
        + mm_exact(triangle(lambda row, col: col < row).astype(BF16), start_terms)
        + kept_heads[0:1, :]
    )
    d_step = head_sum(d_scaled * values, ones) + d_decay * heads_ref[1:2, :]
    d_raw = d_step * jax.nn.sigmoid(biased)
    head_grad_ref[0:1, :] += jnp.sum(d_raw, axis=0, keepdims=True)
    head_grad_ref[1:2, :] += jnp.sum(d_decay * decay, axis=0, keepdims=True)
    head_grad_ref[2:3, :] += kept_heads[1:2, :]
    d_values = (d_scaled * step_chan + skip_ref[0:1, :] * dy) * mask
    d_conv = jnp.concatenate([d_b, d_c, d_values], axis=1)
    d_pre = d_conv * (sig * (1.0 + pre * (1.0 - sig)))
    conv_grad_ref[4:5, :] += jnp.sum(d_pre, axis=0, keepdims=True)
    dext[BLOCK : BLOCK + 8, :] = dext[0:8, :]
    dext[0:BLOCK, :] = d_pre
    conv_in = proj_ref[:, width : width + joint].astype(F32)
    d_in = None
    for tap in range(4):
        ahead = d_pre if tap == 3 else dext[3 - tap : 3 - tap + BLOCK, :]
        conv_grad_ref[tap : tap + 1, :] += jnp.sum(ahead * conv_in, axis=0, keepdims=True)
        d_in = ahead * taps_ref[tap : tap + 1, :] if tap == 0 else d_in + ahead * taps_ref[tap : tap + 1, :]
    dproj_ref[:, width : width + joint] = d_in.astype(BF16)
    dproj_ref[:, joint + width :] = d_raw.astype(BF16)


def mm_exact_left(value, ones):
    first = value.astype(BF16)
    rest = value - first.astype(F32)
    second = rest.astype(BF16)
    third = (rest - second.astype(F32)).astype(BF16)
    return mm(first, ones) + (mm(second, ones) + mm(third, ones))


def mixer_forward(mask, hidden, weight, taps, heads, skip, state_dim, width):
    seqs = mask.shape[0]
    tokens, depth = hidden.shape
    blocks = tokens // seqs // BLOCK
    columns = weight.shape[1]
    joint = 2 * state_dim + width
    row = lambda s, c: (s * blocks + c, 0)
    whole = lambda s, c: (0, 0)
    return pl.pallas_call(
        lambda *refs: forward_kernel(*refs, state_dim=state_dim, width=width),
        grid=(seqs, blocks),
        in_specs=[
            pl.BlockSpec((1, 1, width), lambda s, c: (s, 0, 0)),
            pl.BlockSpec((BLOCK, depth), row),
            pl.BlockSpec((depth, columns), whole),
            pl.BlockSpec((8, joint), whole),
            pl.BlockSpec((8, LANES), whole),
            pl.BlockSpec((8, width), whole),
        ],
        out_specs=[
            pl.BlockSpec((BLOCK, columns), row),
            pl.BlockSpec((BLOCK, width), row),
            pl.BlockSpec((1, state_dim, width), lambda s, c: (s * blocks + c, 0, 0)),
            pl.BlockSpec((1, 8, BLOCK), lambda s, c: (s * blocks + c, 0, 0)),
            pl.BlockSpec((BLOCK, joint), row),
        ],
        out_shape=[
            jax.ShapeDtypeStruct((tokens, columns), BF16),
            jax.ShapeDtypeStruct((tokens, width), BF16),
            jax.ShapeDtypeStruct((seqs * blocks, state_dim, width), F32),
            jax.ShapeDtypeStruct((seqs * blocks, 8, BLOCK), F32),
            jax.ShapeDtypeStruct((tokens, joint), F32),
        ],
        scratch_shapes=[
            pltpu.VMEM((BLOCK + 8, joint), F32),
            pltpu.VMEM((state_dim, width), F32),
        ],
        compiler_params=pltpu.CompilerParams(
            dimension_semantics=("arbitrary", "arbitrary"), vmem_limit_bytes=VMEM
        ),
        cost_estimate=FREE,
        name="mixer_forward",
    )(mask, hidden, weight, taps, heads, skip)


def mixer_backward(gains, projected, pre, y_all, d_normed, token_rows, states, taps, heads, skip, state_dim):
    seqs, _, width = gains.shape
    tokens, columns = projected.shape
    blocks = tokens // seqs // BLOCK
    joint = 2 * state_dim + width
    place = lambda s, c: s * blocks + blocks - 1 - c
    row = lambda s, c: (place(s, c), 0)
    block = lambda s, c: (place(s, c), 0, 0)
    whole = lambda s, c: (0, 0)
    return pl.pallas_call(
        lambda *refs: backward_kernel(*refs, state_dim=state_dim, width=width),
        grid=(seqs, blocks),
        in_specs=[
            pl.BlockSpec((1, 8, width), lambda s, c: (s, 0, 0)),
            pl.BlockSpec((BLOCK, columns), row),
            pl.BlockSpec((BLOCK, joint), row),
            pl.BlockSpec((BLOCK, width), row),
            pl.BlockSpec((BLOCK, width), row),
            pl.BlockSpec((1, 8, BLOCK), block),
            pl.BlockSpec((1, state_dim, width), block),
            pl.BlockSpec((8, joint), whole),
            pl.BlockSpec((8, LANES), whole),
            pl.BlockSpec((8, width), whole),
        ],
        out_specs=[
            pl.BlockSpec((BLOCK, columns), row),
            pl.BlockSpec((8, joint), whole),
            pl.BlockSpec((8, LANES), whole),
            pl.BlockSpec((8, width), whole),
        ],
        out_shape=[
            jax.ShapeDtypeStruct((tokens, columns), BF16),
            jax.ShapeDtypeStruct((8, joint), F32),
            jax.ShapeDtypeStruct((8, LANES), F32),
            jax.ShapeDtypeStruct((8, width), F32),
        ],
        scratch_shapes=[
            pltpu.VMEM((BLOCK + 8, joint), F32),
            pltpu.VMEM((state_dim, width), F32),
            pltpu.VMEM((LANES, BLOCK), F32),
        ],
        compiler_params=pltpu.CompilerParams(
            dimension_semantics=("arbitrary", "arbitrary"), vmem_limit_bytes=VMEM
        ),
        cost_estimate=FREE,
        name="mixer_backward",
    )(gains, projected, pre, y_all, d_normed, token_rows, states, taps, heads, skip)


def row_sum(value):
    ones = jnp.ones((8, value.shape[1]), BF16)
    high, low = halves(value)
    return mm(ones, high, NT) + mm(ones, low, NT)


def pull_kernel(cot_ref, weight_ref, gate_ref, y_ref, gain_ref, d_normed_ref, dot_ref):
    d_normed = mm(cot_ref[...], weight_ref[...], NT)
    d_normed_ref[...] = d_normed
    gate = gate_ref[...].astype(F32)
    gated = y_ref[...].astype(F32) * (gate * jax.nn.sigmoid(gate))
    dot_ref[0] = row_sum(d_normed * gain_ref[0, 0:1, :] * gated)


def pull_back(cot_all, weight, projected, y_all, gains, gate_place):
    seqs, _, width = gains.shape
    tokens, depth = cot_all.shape
    blocks = tokens // seqs // BLOCK
    row = lambda s, c: (s * blocks + c, 0)
    return pl.pallas_call(
        pull_kernel,
        grid=(seqs, blocks),
        in_specs=[
            pl.BlockSpec((BLOCK, depth), row),
            pl.BlockSpec((width, depth), lambda s, c: (0, 0)),
            pl.BlockSpec((BLOCK, width), lambda s, c: (s * blocks + c, gate_place)),
            pl.BlockSpec((BLOCK, width), row),
            pl.BlockSpec((1, 8, width), lambda s, c: (s, 0, 0)),
        ],
        out_specs=[
            pl.BlockSpec((BLOCK, width), row),
            pl.BlockSpec((1, 8, BLOCK), lambda s, c: (s * blocks + c, 0, 0)),
        ],
        out_shape=[
            jax.ShapeDtypeStruct((tokens, width), F32),
            jax.ShapeDtypeStruct((seqs * blocks, 8, BLOCK), F32),
        ],
        compiler_params=pltpu.CompilerParams(
            dimension_semantics=("arbitrary", "arbitrary"), vmem_limit_bytes=VMEM
        ),
        cost_estimate=FREE,
        name="pull_back",
    )(cot_all, weight, projected, y_all, gains)


def pad_last(array, size):
    extra = size - array.shape[-1]
    if extra == 0:
        return array
    return jnp.pad(array, [(0, 0)] * (array.ndim - 1) + [(0, extra)])


def pad_rows(array, size):
    return jnp.pad(array, [(0, size - array.shape[0]), (0, 0)])


def swap(value, axis, bit):
    size = lax.axis_size(axis)
    return lax.ppermute(value, axis, [(place, place ^ bit) for place in range(size)])


def all_sum(value, axis):
    bit = 1
    while bit < lax.axis_size(axis):
        value = value + swap(value, axis, bit)
        bit *= 2
    return value


NEAR_FAR = ((1, 2), (2, 1))


def reduce_cut(share, block, dtype):
    return [
        jnp.concatenate([block(share, near ^ far, half), block(share, near, half)], axis=0).astype(dtype)
        for half, (near, far) in enumerate(NEAR_FAR)
    ]


def reduce_near(cuts):
    return [swap(cut, "dp", near) for cut, (near, _) in zip(cuts, NEAR_FAR)]


def reduce_far(share, block, got):
    rows = got[0].shape[0] // 2
    kept = [
        (block(share, far, half) + got[half][:rows].astype(F32)).astype(got[half].dtype)
        for half, (_, far) in enumerate(NEAR_FAR)
    ]
    mine = [block(share, 0, half) + got[half][rows:].astype(F32) for half in range(2)]
    kept = lax.optimization_barrier(kept)
    far_got = [swap(piece, "dp", far) for piece, (_, far) in zip(kept, NEAR_FAR)]
    return jnp.concatenate([piece + other.astype(F32) for piece, other in zip(mine, far_got)], axis=0)


def gather_near(own):
    rows = own.shape[0] // 2
    upper, lower = own[:rows], own[rows:]
    upper1, lower2 = swap(upper, "dp", 1), swap(lower, "dp", 2)
    upper2, lower1 = swap(upper, "dp", 2), swap(lower, "dp", 1)
    return [(upper, lower), (upper1, lower1), (upper2, lower2)]


def gather_far(first):
    return first + [(swap(first[1][0], "dp", 2), swap(first[2][1], "dp", 1))]


def line_permute(block, reach):
    chips = lax.axis_size("mp") // 2
    pairs = [(2 * z + c, 2 * ((z + reach) % chips) + c) for z in range(chips) for c in range(2)]
    return lax.ppermute(block, "mp", pairs)


def line_send(shares):
    groups = [list(range(core, lax.axis_size("mp"), 2)) for core in range(2)]
    return lax.all_to_all(shares, "mp", split_axis=0, concat_axis=0, axis_index_groups=groups, tiled=True)


def pair_kernel(place_ref, own_ref, sibling_ref, own_weight_ref, sibling_weight_ref, *out_refs, dims):
    share = mm(own_ref[...], own_weight_ref[...], dims) + mm(sibling_ref[...], sibling_weight_ref[...], dims)
    share = share.astype(BF16)
    if len(out_refs) == 1:
        out_refs[0][0] = share
        return
    for reach, out_ref in enumerate(out_refs):

        @pl.when(pl.program_id(0) == reach)
        def _(out_ref=out_ref):
            out_ref[...] = share


def pair_product(left, theirs, own_weight, sibling_weight, dims, depth, tokens, stacked):
    chips = lax.axis_size("mp") // 2
    inner = left.shape[1]
    whole = lambda i, place: (0, 0)
    place = lax.axis_index("mp").astype(jnp.int32)
    there = lambda i, place: lax.rem(place[0] + i, chips)
    return pl.pallas_call(
        lambda *refs: pair_kernel(*refs, dims=dims),
        grid_spec=pltpu.PrefetchScalarGridSpec(
            num_scalar_prefetch=1,
            grid=(chips,),
            in_specs=[
                pl.BlockSpec((tokens, inner), lambda i, place: (2 * there(i, place) + place[1], 0)),
                pl.BlockSpec((tokens, inner), lambda i, place: (there(i, place), 0)),
                pl.BlockSpec(own_weight.shape, whole),
                pl.BlockSpec(sibling_weight.shape, whole),
            ],
            out_specs=[pl.BlockSpec((1, tokens, depth), lambda i, place: (there(i, place), 0, 0))]
            if stacked
            else [pl.BlockSpec((tokens, depth), whole)] * chips,
        ),
        out_shape=[jax.ShapeDtypeStruct((chips, tokens, depth), BF16)]
        if stacked
        else [jax.ShapeDtypeStruct((tokens, depth), BF16)] * chips,
        compiler_params=pltpu.CompilerParams(dimension_semantics=("arbitrary",), vmem_limit_bytes=VMEM),
        cost_estimate=FREE,
        name="pair_product",
    )(jnp.stack([place // 2, place % 2]), left, theirs, own_weight, sibling_weight)


def for_sibling(left, tokens):
    mp = lax.axis_size("mp")
    by_core = left.reshape(mp // 2, 2, tokens, left.shape[1])
    other = 1 - lax.axis_index("mp") % 2
    return lax.dynamic_index_in_dim(by_core, other, 1, keepdims=False).reshape(-1, left.shape[1])


def in_place_order(pieces):
    place = lax.axis_index("dp")
    pieces = [jnp.concatenate(pair, axis=0) for pair in pieces]
    odd, high = place % 2 == 1, place // 2 == 1
    lows = [jnp.where(odd, pieces[k ^ 1], pieces[k]) for k in range(4)]
    return jnp.concatenate([jnp.where(high, lows[k ^ 2], lows[k]).astype(F32) for k in range(4)], axis=0)


def keep_kernel(in_ref, out_ref):
    out_ref[...] = in_ref[...]


def keep(array):
    rows = 64
    spec = pl.BlockSpec((rows, array.shape[1]), lambda i: (i, 0))
    return pl.pallas_call(
        keep_kernel,
        grid=(array.shape[0] // rows,),
        in_specs=[spec],
        out_specs=spec,
        out_shape=jax.ShapeDtypeStruct(array.shape, array.dtype),
        cost_estimate=FREE,
        name="keep",
    )(array)


def assemble_kernel(place_ref, *refs):
    out_ref = refs[-1]
    for own in range(4):

        @pl.when(place_ref[0] == own)
        def _(own=own):
            order = [refs[2 * (own ^ p) + half][...].astype(F32) for p in range(4) for half in range(2)]
            out_ref[...] = jnp.concatenate(order, axis=0).T


def assemble(gathered):
    pieces = [half for pair in gathered for half in pair]
    half_rows, columns = pieces[0].shape
    chunk = 1280
    return pl.pallas_call(
        assemble_kernel,
        grid=(pl.cdiv(columns, chunk),),
        in_specs=[pl.BlockSpec(memory_space=pltpu.SMEM)]
        + [pl.BlockSpec((half_rows, chunk), lambda i: (0, i)) for _ in pieces],
        out_specs=pl.BlockSpec((chunk, 8 * half_rows), lambda i: (i, 0)),
        out_shape=jax.ShapeDtypeStruct((columns, 8 * half_rows), F32),
        compiler_params=pltpu.CompilerParams(dimension_semantics=("arbitrary",), vmem_limit_bytes=VMEM),
        cost_estimate=pl.CostEstimate(flops=1, bytes_accessed=30 * 2**20, transcendentals=0),
        name="assemble",
    )(lax.axis_index("dp").astype(jnp.int32)[None], *pieces).T


def total(blocks):
    result = blocks[0].astype(F32)
    for index in range(1, len(blocks)):
        result = result + blocks[index].astype(F32)
    return result


def on_device(
    inputs, cotangent, widths, norm_gain, in_weight, conv_weight, conv_bias, step_bias, rate_log,
    skip_gain, out_gain, out_weight,
):
    mp, dp = lax.axis_size("mp"), lax.axis_size("dp")
    mp_place, dp_place = lax.axis_index("mp"), lax.axis_index("dp")
    heads, inner, channels = step_bias.shape[0], out_gain.shape[0], conv_bias.shape[0]
    head_dim, state_dim = inner // heads, (channels - inner) // 2
    own_heads = heads // mp
    own = own_heads * head_dim
    width = -(-own // LANES) * LANES
    joint = 2 * state_dim + width
    columns = joint + width + LANES
    tokens, depth = inputs.shape
    rows = depth // mp
    part = rows // dp
    seqs = widths.shape[0]
    all_tokens = tokens * mp

    slab = lax.dynamic_slice_in_dim(in_weight, dp_place * part, part, 0)
    by_place = lambda piece, size: pad_last(
        piece.reshape(part, mp, piece.shape[1] // mp).transpose(1, 0, 2), size
    )
    send = jnp.concatenate(
        [
            by_place(slab[:, :inner], width),
            jnp.broadcast_to(slab[None, :, 2 * inner : 2 * inner + 2 * state_dim], (mp, part, 2 * state_dim)),
            by_place(slab[:, inner : 2 * inner], width),
            by_place(slab[:, inner + channels :], LANES),
        ],
        axis=2,
    )
    got = lax.all_to_all(send, "mp", split_axis=0, concat_axis=0, tiled=True)

    def reorder(array):
        apart = array.reshape(-1, mp, dp, part)
        return jnp.concatenate(
            [
                lax.dynamic_index_in_dim(apart, dp_place ^ k, 2, keepdims=False).reshape(-1, mp * part)
                for k in range(dp)
            ],
            axis=1,
        )

    def restore(array):
        apart = array.reshape(-1, dp, mp, part)
        return jnp.stack(
            [lax.dynamic_index_in_dim(apart, dp_place ^ k, 1, keepdims=False) for k in range(dp)], axis=2
        ).reshape(-1, depth)

    line = mp <= 16
    inputs_f = inputs.astype(F32)
    rms_scale = lax.rsqrt(jnp.mean(inputs_f * inputs_f, axis=-1, keepdims=True) + EPS)
    gain_in = reorder(norm_gain[None, :])
    normed = reorder(inputs).astype(F32) * rms_scale
    hidden_own = (normed * gain_in).astype(BF16)
    hidden_own, got = lax.optimization_barrier((hidden_own, got))
    weight = jnp.concatenate(sum(gather_far(gather_near(got.reshape(mp * part, columns))), ()), axis=0)
    hidden = lax.all_gather(hidden_own, "mp", axis=0, tiled=True)

    first_chan, first_head = mp_place * own, mp_place * own_heads
    cut = lambda array, first, size: lax.dynamic_slice_in_dim(array, first, size, array.ndim - 1)
    taps_all = jnp.concatenate([conv_weight, conv_bias[None, :]], axis=0)
    taps = pad_rows(
        jnp.concatenate([taps_all[:, inner:], pad_last(cut(taps_all, first_chan, own), width)], axis=1), 8
    )
    head_rows = jnp.stack([step_bias, -jnp.exp(rate_log)])
    head_params = pad_rows(pad_last(cut(head_rows, first_head, own_heads), LANES), 8)
    skip = jnp.repeat(cut(skip_gain, first_head, own_heads), head_dim)[None, :]
    skip = pad_rows(pad_last(skip, width), 8)
    active_heads = heads // 8 * jnp.left_shift(jnp.int32(1), widths)
    head_mask = (first_head + jnp.arange(own_heads, dtype=jnp.int32))[None, :] < active_heads[:, None]
    chan_mask = jnp.repeat(head_mask.astype(F32), head_dim, axis=1)
    mask = pad_last(chan_mask, width)[:, None, :]
    per_token = lambda array: jnp.repeat(array, all_tokens // seqs, axis=0)
    mask_tok = chan_mask if seqs == 1 else per_token(chan_mask)
    active_count = (active_heads * head_dim).astype(F32)[:, None]
    if seqs > 1:
        active_count = per_token(active_count)

    if line:
        sibling_out, sibling_weight = swap(out_weight, "mp", 1), swap(weight, "mp", 1)
        weight, sibling_out, sibling_weight = lax.optimization_barrier((weight, sibling_out, sibling_weight))
    projected, y_all, states, squares, pre = mixer_forward(
        mask, hidden, weight, taps, head_params, skip, state_dim, width
    )
    square_rows = all_sum(squares[:, 0, :], "mp")
    total_square = square_rows.reshape(all_tokens)[:, None]
    gate = projected[:, :own].astype(F32)
    y_f = y_all[:, :own].astype(F32)
    gate_sig = jax.nn.sigmoid(gate)
    silu_z = gate * gate_sig
    gated = y_f * silu_z
    gain = cut(out_gain, first_chan, own)[None, :]
    out_root = lax.rsqrt(total_square / active_count + EPS)
    normed_out = (gated * out_root * gain * mask_tok).astype(BF16)
    if line:
        theirs = swap(for_sibling(normed_out, tokens), "mp", 1)
        shares = pair_product(normed_out, theirs, out_weight, sibling_out, NN, depth, tokens, True)[0]
        cot_all = lax.all_gather(cotangent, "mp", axis=0, tiled=True)
        cot_all, shares = lax.optimization_barrier((cot_all, shares))
    else:
        shares = mm(normed_out, out_weight).astype(BF16)
        sent = [lax.psum_scatter(shares, "mp", scatter_dimension=0, tiled=True)]
        late_cot, sent = lax.optimization_barrier((cotangent, sent))
        cot_all = lax.all_gather(late_cot, "mp", axis=0, tiled=True)

    gain_rows = pad_last(cut(out_gain, first_chan, own), width)
    gains = jnp.concatenate(
        [
            gain_rows[None, None, :] * mask,
            mask,
            jnp.broadcast_to((active_heads * head_dim).astype(F32)[:, None, None], mask.shape),
            jnp.zeros((seqs, 5, width), F32),
        ],
        axis=1,
    )
    out_padded = pad_rows(out_weight, width)
    d_normed, dots = pull_back(cot_all, out_padded, projected, y_all, gains, 0)
    dot_rows = all_sum(dots[:, 0, :], "mp")
    out_part = mm(normed_out, cot_all, TN)
    if line:
        dot_rows, shares = lax.optimization_barrier((dot_rows, shares))
        sent = line_send(shares)
    token_rows = jnp.stack([square_rows, dot_rows] + [jnp.zeros_like(dot_rows)] * 6, axis=1)
    quarter = depth // dp

    def in_block(share, k, half):
        return share[k * quarter + half * (quarter // 2) : k * quarter + (half + 1) * (quarter // 2)]

    def to_rows(mine):
        return lax.all_to_all(mine.astype(BF16).reshape(mp, part, -1), "mp", split_axis=0, concat_axis=0, tiled=True)

    token_rows, out_part = lax.optimization_barrier((token_rows, out_part))
    out_mine = lax.psum_scatter(out_part, "dp", scatter_dimension=0, tiled=True)
    def norm_share(d_hidden):
        share = restore(jnp.sum(d_hidden * normed, axis=0)[None, :])
        return all_sum(share.reshape(-1, LANES), "dp")

    def rows_of(blocks):
        flat = lambda first, size: blocks[:, :, first : first + size].transpose(1, 0, 2).reshape(part, -1)
        shared = jnp.sum(blocks[:, :, width : width + 2 * state_dim].astype(F32), axis=0).astype(BF16)
        return jnp.concatenate(
            [flat(0, own), flat(width + 2 * state_dim, own), shared, flat(width + joint, own_heads)], axis=1
        )

    d_proj, conv_grads, head_grads, gain_grads = mixer_backward(
        gains, projected, pre, y_all, d_normed, token_rows, states, taps, head_params, skip, state_dim
    )
    d_proj, out_mine = lax.optimization_barrier((d_proj, out_mine))
    out_weight_grad = lax.all_gather(out_mine, "dp", axis=0, tiled=True)

    def place_in(array, first, size):
        return lax.dynamic_update_slice_in_dim(
            jnp.zeros(array.shape[:-1] + (size,), F32), array, first, array.ndim - 1
        )

    conv_own = place_in(conv_grads[:5, 2 * state_dim : 2 * state_dim + own], first_chan, inner)
    conv_full = jnp.concatenate([conv_own, conv_grads[:5, : 2 * state_dim]], axis=1)
    head_full = place_in(head_grads[:3, :own_heads], first_head, heads)
    gain_full = place_in(gain_grads[0, :own], first_chan, inner)
    small = [conv_full.reshape(-1), head_full.reshape(-1), gain_full]
    sizes = [piece.shape[0] for piece in small]
    packed = jnp.concatenate(small)
    count = -(-packed.shape[0] // 1024) * 1024
    packed = jnp.pad(packed, (0, count - packed.shape[0])).reshape(-1, LANES)

    if line:
        theirs = swap(for_sibling(d_proj, tokens), "mp", 1)
        d_shares = pair_product(d_proj, theirs, weight, sibling_weight, NT, depth, tokens, False)
        d_shares, d_proj, sent = lax.optimization_barrier((d_shares, d_proj, sent))
        reaches = [1] + list(range(mp // 2 - 1, 1, -1))
        d_blocks = [d_shares[0], line_permute(d_shares[1], 1)]
        share = mm(hidden, d_proj, TN)
        near_cut = reduce_cut(share, in_block, BF16)
        near_cut, d_blocks, out_weight_grad = lax.optimization_barrier((near_cut, d_blocks, out_weight_grad))
        near_got = reduce_near(near_cut)
        d_blocks += [line_permute(d_shares[reach], reach) for reach in reaches[1:2]]
        near_got, d_blocks = lax.optimization_barrier((near_got, d_blocks))
        mine = reduce_far(share, in_block, near_got)
        d_blocks += [line_permute(d_shares[reach], reach) for reach in reaches[2:]]
        mine, packed, d_blocks = lax.optimization_barrier((mine, packed, d_blocks))
        blocks = to_rows(mine)
        d_hidden = total(d_blocks)
        norm_part = norm_share(d_hidden)
        blocks, packed, out_weight_grad, norm_part = lax.optimization_barrier(
            (blocks, all_sum(packed, "dp"), keep(out_weight_grad), norm_part)
        )
        in_weight_grad = assemble(gather_far(gather_near(rows_of(blocks))))
    else:
        packed = all_sum(packed, "dp")
        share = mm(hidden, d_proj, TN)
        d_proj, share = lax.optimization_barrier((d_proj, share))
        blocks = to_rows(reduce_far(share, in_block, reduce_near(reduce_cut(share, in_block, BF16))))
        d_shares = mm(d_proj, weight, NT).astype(BF16)
        d_hidden = lax.psum_scatter(d_shares, "mp", scatter_dimension=0, tiled=True).astype(F32)
        in_weight_grad = in_place_order(gather_far(gather_near(rows_of(blocks))))
    outputs = (inputs_f + total(sent)).astype(BF16)
    if not line:
        norm_part = norm_share(d_hidden)
    everything = all_sum(jnp.concatenate([packed, norm_part], axis=0), "mp")
    norm_total = everything[packed.shape[0] :].reshape(depth)
    packed = everything.reshape(-1)
    conv_total = packed[: sizes[0]].reshape(conv_full.shape)
    head_total = packed[sizes[0] : sizes[0] + sizes[1]].reshape(head_full.shape)
    gain_total = packed[sizes[0] + sizes[1] : sum(sizes)]

    d_normed_in = d_hidden * gain_in
    input_back = rms_scale * (d_normed_in - normed * jnp.mean(d_normed_in * normed, axis=-1, keepdims=True))
    input_grad = restore((reorder(cotangent).astype(F32) + input_back).astype(BF16))

    return (
        outputs,
        input_grad,
        norm_total,
        in_weight_grad,
        conv_total[:4],
        conv_total[4],
        head_total[0],
        head_total[1],
        head_total[2],
        gain_total,
        out_weight_grad,
    )


def solution(mesh):
    rows = P(("dp", "mp"), None)
    return jax.shard_map(
        on_device,
        mesh=mesh,
        in_specs=(rows, rows, P("dp"), P(), P("mp", None), P(), P(), P(), P(), P(), P(), P("mp", None)),
        out_specs=(rows, rows, P(), P("mp", None), P(), P(), P(), P(), P(), P(), P("mp", None)),
        check_vma=False,
    )
```

```python
import jax
import jax.numpy as jnp
from jax import lax
from jax.experimental import pallas as pl
from jax.experimental.pallas import tpu as pltpu
from jax.sharding import PartitionSpec as P

SEQ = 2048
BLOCK = 256
EPS = 1e-05
LANES = 128
VMEM = 56 * 2**20
FREE = pl.CostEstimate(flops=1, bytes_accessed=1, transcendentals=0)

F32 = jnp.float32
BF16 = jnp.bfloat16
NN = (((1,), (0,)), ((), ()))
NT = (((1,), (1,)), ((), ()))
TN = (((0,), (0,)), ((), ()))


def mm(left, right, dims=NN):
    return lax.dot_general(left, right, dims, preferred_element_type=F32)


def halves(value):
    high = value.astype(BF16)
    return high, (value - high.astype(F32)).astype(BF16)


def mm3(left, right, dims=NN):
    return mm(left[0], right[0], dims) + (mm(left[0], right[1], dims) + mm(left[1], right[0], dims))


def mm_exact(ones, value, dims=NN):
    first, rest = value.astype(BF16), None
    rest = value - first.astype(F32)
    second = rest.astype(BF16)
    third = (rest - second.astype(F32)).astype(BF16)
    return mm(ones, first, dims) + (mm(ones, second, dims) + mm(ones, third, dims))


def spread(per_head, width):
    rows = per_head.shape[0]
    low_half = lax.broadcasted_iota(jnp.int32, (rows, LANES), 1) < LANES // 2
    parts = []
    for pair in range(width // LANES):
        parts.append(
            jnp.where(
                low_half, per_head[:, 2 * pair : 2 * pair + 1], per_head[:, 2 * pair + 1 : 2 * pair + 2]
            )
        )
    return parts[0] if len(parts) == 1 else jnp.concatenate(parts, axis=1)


def head_ones(width):
    chan = lax.broadcasted_iota(jnp.int32, (width, LANES), 0)
    head = lax.broadcasted_iota(jnp.int32, (width, LANES), 1)
    return (chan // (LANES // 2) == head).astype(BF16)


def head_sum(per_chan, ones):
    high, low = halves(per_chan)
    return mm(high, ones) + mm(low, ones)


def conv_block(ext_ref, taps_ref):
    span = 4
    pre = taps_ref[span : span + 1, :] + ext_ref[5 : 5 + BLOCK, :] * taps_ref[0:1, :]
    for tap in range(1, span):
        pre = pre + ext_ref[5 + tap : 5 + tap + BLOCK, :] * taps_ref[tap : tap + 1, :]
    return pre


def step_rates(step_raw, heads_ref):
    biased = step_raw + heads_ref[0:1, :]
    step_size = jnp.maximum(biased, 0.0) + jnp.log1p(jnp.exp(-jnp.abs(biased)))
    decay = heads_ref[1:2, :] * step_size
    return biased, step_size, decay


def triangle(keep):
    row = lax.broadcasted_iota(jnp.int32, (BLOCK, BLOCK), 0)
    col = lax.broadcasted_iota(jnp.int32, (BLOCK, BLOCK), 1)
    return keep(row, col)


def forward_kernel(
    mask_ref, hidden_ref, weight_ref, taps_ref, heads_ref, skip_ref,
    proj_ref, y_ref, state_ref, square_ref, pre_ref,
    ext, state, *, state_dim, width,
):
    joint = 2 * state_dim + width

    @pl.when(pl.program_id(1) == 0)
    def _():
        ext[0:8, :] = jnp.zeros((8, joint), F32)
        state[...] = jnp.zeros_like(state)

    projected = mm(hidden_ref[...], weight_ref[...]).astype(BF16)
    proj_ref[...] = projected
    ext[8 : 8 + BLOCK, :] = projected[:, width : width + joint].astype(F32)
    pre = conv_block(ext, taps_ref)
    pre_ref[...] = pre
    ext[0:8, :] = ext[BLOCK : BLOCK + 8, :]
    conv_out = pre * jax.nn.sigmoid(pre)
    values = conv_out[:, 2 * state_dim :] * mask_ref[0]
    b_coef = halves(conv_out[:, :state_dim])
    c_coef = halves(conv_out[:, state_dim : 2 * state_dim])
    _, step_size, decay = step_rates(projected[:, joint + width :].astype(F32), heads_ref)
    causal = triangle(lambda row, col: row >= col)
    cumulative = mm_exact(causal.astype(BF16), decay)
    across = cumulative.T
    last = cumulative[BLOCK - 1 : BLOCK, :]
    scaled = values * spread(step_size, width)
    scaled_parts = halves(scaled)
    scores = mm3(c_coef, b_coef, NT)
    low_half = lax.broadcasted_iota(jnp.int32, (BLOCK, LANES), 1) < LANES // 2
    old = state[...]
    state_ref[0] = old
    mixed = spread(jnp.exp(cumulative), width) * mm3(c_coef, halves(old))
    within = []
    for pair in range(width // LANES):
        lanes = slice(pair * LANES, (pair + 1) * LANES)
        rhs = (scaled_parts[0][:, lanes], scaled_parts[1][:, lanes])
        sides = []
        for head in (2 * pair, 2 * pair + 1):
            gap = jnp.where(causal, cumulative[:, head : head + 1] - across[head : head + 1, :], -1e30)
            sides.append(mm3(halves(scores * jnp.exp(gap)), rhs))
        within.append(jnp.where(low_half, sides[0], sides[1]))
    mixed = mixed + (within[0] if len(within) == 1 else jnp.concatenate(within, axis=1))
    tail = halves(scaled * spread(jnp.exp(last - cumulative), width))
    state[...] = old * spread(jnp.exp(last), width) + mm3(b_coef, tail, TN)
    y_low = (mixed + skip_ref[0:1, :] * values).astype(BF16)
    y_ref[...] = y_low
    gate = projected[:, :width].astype(F32)
    gated = y_low.astype(F32) * (gate * jax.nn.sigmoid(gate))
    square = halves(gated * gated * mask_ref[0])
    ones = jnp.ones((8, width), BF16)
    square_ref[0] = mm(ones, square[0], NT) + mm(ones, square[1], NT)


def backward_kernel(
    gain_ref, proj_ref, pre_ref, y_ref, d_normed_ref, tokens_ref, state_ref, taps_ref, heads_ref, skip_ref,
    dproj_ref, conv_grad_ref, head_grad_ref, gain_grad_ref,
    dext, dstate, rows, *, state_dim, width,
):
    joint = 2 * state_dim + width

    @pl.when((pl.program_id(0) == 0) & (pl.program_id(1) == 0))
    def _():
        conv_grad_ref[...] = jnp.zeros_like(conv_grad_ref)
        head_grad_ref[...] = jnp.zeros_like(head_grad_ref)
        gain_grad_ref[...] = jnp.zeros_like(gain_grad_ref)
        rows[...] = jnp.zeros_like(rows)

    @pl.when(pl.program_id(1) == 0)
    def _():
        dext[0:8, :] = jnp.zeros((8, joint), F32)
        dstate[...] = jnp.zeros_like(dstate)

    per_token = tokens_ref[0].T
    count = gain_ref[0, 2:3, 0:1]
    root = lax.rsqrt(per_token[:, 0:1] / count + EPS)
    pull = root * root * per_token[:, 1:2] / count
    gate = proj_ref[:, :width].astype(F32)
    y = y_ref[...].astype(F32)
    gate_sig = jax.nn.sigmoid(gate)
    silu = gate * gate_sig
    normed_gated = y * silu * root * gain_ref[0, 1:2, :]
    d_normed = d_normed_ref[...]
    gain_grad_ref[0:1, :] += jnp.sum(d_normed * normed_gated, axis=0, keepdims=True)
    d_gated = root * (d_normed * gain_ref[0, 0:1, :]) - normed_gated * pull
    dy_low = (d_gated * silu).astype(BF16)
    dproj_ref[:, :width] = (d_gated * y * gate_sig * (1.0 + gate * (1.0 - gate_sig))).astype(BF16)

    pre = pre_ref[...]
    sig = jax.nn.sigmoid(pre)
    conv_out = pre * sig
    mask = gain_ref[0, 1:2, :]
    values = conv_out[:, 2 * state_dim :] * mask
    b_coef = halves(conv_out[:, :state_dim])
    c_coef = halves(conv_out[:, state_dim : 2 * state_dim])
    biased, step_size, decay = step_rates(proj_ref[:, joint + width :].astype(F32), heads_ref)
    later = triangle(lambda row, col: col >= row)
    cumulative = mm_exact(triangle(lambda row, col: row >= col).astype(BF16), decay)
    across = cumulative.T
    last = cumulative[BLOCK - 1 : BLOCK, :]
    step_chan = spread(step_size, width)
    scaled = values * step_chan
    scaled_parts = halves(scaled)
    dy = dy_low.astype(F32)
    scores = mm3(b_coef, c_coef, NT)
    low_half = lax.broadcasted_iota(jnp.int32, (BLOCK, LANES), 1) < LANES // 2
    lane = lax.broadcasted_iota(jnp.int32, (BLOCK, LANES), 1)
    d_scores = jnp.zeros((BLOCK, BLOCK), F32)
    from_rows = jnp.zeros((BLOCK, LANES), F32)
    d_within = []
    for pair in range(width // LANES):
        lanes = slice(pair * LANES, (pair + 1) * LANES)
        dy_pair = dy_low[:, lanes]
        dy_twice = jnp.concatenate([dy_pair, dy_pair], axis=1)
        sides = []
        for side in range(2):
            head = 2 * pair + side
            own = low_half if side == 0 else jnp.logical_not(low_half)
            left = jnp.concatenate(
                [jnp.where(own, part[:, lanes], jnp.zeros((), BF16)) for part in scaled_parts], axis=1
            )
            d_mixing = mm(left, dy_twice, NT)
            gap = jnp.where(later, across[head : head + 1, :] - cumulative[:, head : head + 1], -1e30)
            weight = jnp.exp(gap)
            mixing = scores * weight
            d_scores = d_scores + d_mixing * weight
            product = d_mixing * mixing
            rows[head : head + 1, :] = jnp.sum(product, axis=0, keepdims=True)
            from_rows = jnp.where(lane == head, jnp.sum(product, axis=1, keepdims=True), from_rows)
            parts = halves(mixing)
            sides.append(mm(parts[0], dy_pair) + mm(parts[1], dy_pair))
        d_within.append(jnp.where(low_half, sides[0], sides[1]))
    ones = head_ones(width)
    old = state_ref[0]
    old_parts = halves(old)
    grown = dstate[...]
    grown_parts = halves(grown)
    ey = spread(jnp.exp(cumulative), width) * dy
    ey_parts = halves(ey)
    tail_chan = spread(jnp.exp(last - cumulative), width)
    tail = scaled * tail_chan
    tail_parts = halves(tail)
    last_chan = spread(jnp.exp(last), width)
    into_state = mm3(b_coef, grown_parts)
    d_scaled = (d_within[0] if len(d_within) == 1 else jnp.concatenate(d_within, axis=1)) + tail_chan * into_state
    d_parts = halves(d_scores)
    d_c = mm3(d_parts, b_coef, TN) + mm3(ey_parts, old_parts, NT)
    d_b = mm3(d_parts, c_coef) + mm3(tail_parts, grown_parts, NT)
    end_terms = mm((ey * mm3(c_coef, old_parts)).astype(BF16), ones)
    start_terms = mm((tail * into_state).astype(BF16), ones)
    kept = jnp.sum(last_chan * grown * old, axis=0, keepdims=True)
    skip_part = jnp.sum(dy * values, axis=0, keepdims=True)
    kept_heads = mm_exact_left(jnp.concatenate([kept, skip_part, jnp.zeros((6, width), F32)], axis=0), ones)
    dstate[...] = last_chan * grown + mm3(c_coef, ey_parts, TN)
    gaps = rows[...].T - from_rows + end_terms
    d_decay = (
        mm_exact(later.astype(BF16), gaps)
        + mm_exact(triangle(lambda row, col: col < row).astype(BF16), start_terms)
        + kept_heads[0:1, :]
    )
    d_step = head_sum(d_scaled * values, ones) + d_decay * heads_ref[1:2, :]
    d_raw = d_step * jax.nn.sigmoid(biased)
    head_grad_ref[0:1, :] += jnp.sum(d_raw, axis=0, keepdims=True)
    head_grad_ref[1:2, :] += jnp.sum(d_decay * decay, axis=0, keepdims=True)
    head_grad_ref[2:3, :] += kept_heads[1:2, :]
    d_values = (d_scaled * step_chan + skip_ref[0:1, :] * dy) * mask
    d_conv = jnp.concatenate([d_b, d_c, d_values], axis=1)
    d_pre = d_conv * (sig * (1.0 + pre * (1.0 - sig)))
    conv_grad_ref[4:5, :] += jnp.sum(d_pre, axis=0, keepdims=True)
    dext[BLOCK : BLOCK + 8, :] = dext[0:8, :]
    dext[0:BLOCK, :] = d_pre
    conv_in = proj_ref[:, width : width + joint].astype(F32)
    d_in = None
    for tap in range(4):
        ahead = d_pre if tap == 3 else dext[3 - tap : 3 - tap + BLOCK, :]
        conv_grad_ref[tap : tap + 1, :] += jnp.sum(ahead * conv_in, axis=0, keepdims=True)
        d_in = ahead * taps_ref[tap : tap + 1, :] if tap == 0 else d_in + ahead * taps_ref[tap : tap + 1, :]
    dproj_ref[:, width : width + joint] = d_in.astype(BF16)
    dproj_ref[:, joint + width :] = d_raw.astype(BF16)


def mm_exact_left(value, ones):
    first = value.astype(BF16)
    rest = value - first.astype(F32)
    second = rest.astype(BF16)
    third = (rest - second.astype(F32)).astype(BF16)
    return mm(first, ones) + (mm(second, ones) + mm(third, ones))


def mixer_forward(mask, hidden, weight, taps, heads, skip, state_dim, width):
    seqs = mask.shape[0]
    tokens, depth = hidden.shape
    blocks = tokens // seqs // BLOCK
    columns = weight.shape[1]
    joint = 2 * state_dim + width
    row = lambda s, c: (s * blocks + c, 0)
    whole = lambda s, c: (0, 0)
    return pl.pallas_call(
        lambda *refs: forward_kernel(*refs, state_dim=state_dim, width=width),
        grid=(seqs, blocks),
        in_specs=[
            pl.BlockSpec((1, 1, width), lambda s, c: (s, 0, 0)),
            pl.BlockSpec((BLOCK, depth), row),
            pl.BlockSpec((depth, columns), whole),
            pl.BlockSpec((8, joint), whole),
            pl.BlockSpec((8, LANES), whole),
            pl.BlockSpec((8, width), whole),
        ],
        out_specs=[
            pl.BlockSpec((BLOCK, columns), row),
            pl.BlockSpec((BLOCK, width), row),
            pl.BlockSpec((1, state_dim, width), lambda s, c: (s * blocks + c, 0, 0)),
            pl.BlockSpec((1, 8, BLOCK), lambda s, c: (s * blocks + c, 0, 0)),
            pl.BlockSpec((BLOCK, joint), row),
        ],
        out_shape=[
            jax.ShapeDtypeStruct((tokens, columns), BF16),
            jax.ShapeDtypeStruct((tokens, width), BF16),
            jax.ShapeDtypeStruct((seqs * blocks, state_dim, width), F32),
            jax.ShapeDtypeStruct((seqs * blocks, 8, BLOCK), F32),
            jax.ShapeDtypeStruct((tokens, joint), F32),
        ],
        scratch_shapes=[
            pltpu.VMEM((BLOCK + 8, joint), F32),
            pltpu.VMEM((state_dim, width), F32),
        ],
        compiler_params=pltpu.CompilerParams(
            dimension_semantics=("arbitrary", "arbitrary"), vmem_limit_bytes=VMEM
        ),
        cost_estimate=FREE,
        name="mixer_forward",
    )(mask, hidden, weight, taps, heads, skip)


def mixer_backward(gains, projected, pre, y_all, d_normed, token_rows, states, taps, heads, skip, state_dim):
    seqs, _, width = gains.shape
    tokens, columns = projected.shape
    blocks = tokens // seqs // BLOCK
    joint = 2 * state_dim + width
    place = lambda s, c: s * blocks + blocks - 1 - c
    row = lambda s, c: (place(s, c), 0)
    block = lambda s, c: (place(s, c), 0, 0)
    whole = lambda s, c: (0, 0)
    return pl.pallas_call(
        lambda *refs: backward_kernel(*refs, state_dim=state_dim, width=width),
        grid=(seqs, blocks),
        in_specs=[
            pl.BlockSpec((1, 8, width), lambda s, c: (s, 0, 0)),
            pl.BlockSpec((BLOCK, columns), row),
            pl.BlockSpec((BLOCK, joint), row),
            pl.BlockSpec((BLOCK, width), row),
            pl.BlockSpec((BLOCK, width), row),
            pl.BlockSpec((1, 8, BLOCK), block),
            pl.BlockSpec((1, state_dim, width), block),
            pl.BlockSpec((8, joint), whole),
            pl.BlockSpec((8, LANES), whole),
            pl.BlockSpec((8, width), whole),
        ],
        out_specs=[
            pl.BlockSpec((BLOCK, columns), row),
            pl.BlockSpec((8, joint), whole),
            pl.BlockSpec((8, LANES), whole),
            pl.BlockSpec((8, width), whole),
        ],
        out_shape=[
            jax.ShapeDtypeStruct((tokens, columns), BF16),
            jax.ShapeDtypeStruct((8, joint), F32),
            jax.ShapeDtypeStruct((8, LANES), F32),
            jax.ShapeDtypeStruct((8, width), F32),
        ],
        scratch_shapes=[
            pltpu.VMEM((BLOCK + 8, joint), F32),
            pltpu.VMEM((state_dim, width), F32),
            pltpu.VMEM((LANES, BLOCK), F32),
        ],
        compiler_params=pltpu.CompilerParams(
            dimension_semantics=("arbitrary", "arbitrary"), vmem_limit_bytes=VMEM
        ),
        cost_estimate=FREE,
        name="mixer_backward",
    )(gains, projected, pre, y_all, d_normed, token_rows, states, taps, heads, skip)


def row_sum(value):
    ones = jnp.ones((8, value.shape[1]), BF16)
    high, low = halves(value)
    return mm(ones, high, NT) + mm(ones, low, NT)


def pull_kernel(cot_ref, weight_ref, gate_ref, y_ref, gain_ref, d_normed_ref, dot_ref):
    d_normed = mm(cot_ref[...], weight_ref[...], NT)
    d_normed_ref[...] = d_normed
    gate = gate_ref[...].astype(F32)
    gated = y_ref[...].astype(F32) * (gate * jax.nn.sigmoid(gate))
    dot_ref[0] = row_sum(d_normed * gain_ref[0, 0:1, :] * gated)


def pull_back(cot_all, weight, projected, y_all, gains, gate_place):
    seqs, _, width = gains.shape
    tokens, depth = cot_all.shape
    blocks = tokens // seqs // BLOCK
    row = lambda s, c: (s * blocks + c, 0)
    return pl.pallas_call(
        pull_kernel,
        grid=(seqs, blocks),
        in_specs=[
            pl.BlockSpec((BLOCK, depth), row),
            pl.BlockSpec((width, depth), lambda s, c: (0, 0)),
            pl.BlockSpec((BLOCK, width), lambda s, c: (s * blocks + c, gate_place)),
            pl.BlockSpec((BLOCK, width), row),
            pl.BlockSpec((1, 8, width), lambda s, c: (s, 0, 0)),
        ],
        out_specs=[
            pl.BlockSpec((BLOCK, width), row),
            pl.BlockSpec((1, 8, BLOCK), lambda s, c: (s * blocks + c, 0, 0)),
        ],
        out_shape=[
            jax.ShapeDtypeStruct((tokens, width), F32),
            jax.ShapeDtypeStruct((seqs * blocks, 8, BLOCK), F32),
        ],
        compiler_params=pltpu.CompilerParams(
            dimension_semantics=("arbitrary", "arbitrary"), vmem_limit_bytes=VMEM
        ),
        cost_estimate=FREE,
        name="pull_back",
    )(cot_all, weight, projected, y_all, gains)


def pad_last(array, size):
    extra = size - array.shape[-1]
    if extra == 0:
        return array
    return jnp.pad(array, [(0, 0)] * (array.ndim - 1) + [(0, extra)])


def pad_rows(array, size):
    return jnp.pad(array, [(0, size - array.shape[0]), (0, 0)])


def swap(value, axis, bit):
    size = lax.axis_size(axis)
    return lax.ppermute(value, axis, [(place, place ^ bit) for place in range(size)])


def all_sum(value, axis):
    bit = 1
    while bit < lax.axis_size(axis):
        value = value + swap(value, axis, bit)
        bit *= 2
    return value


NEAR_FAR = ((1, 2), (2, 1))


def reduce_cut(share, block, dtype):
    return [
        jnp.concatenate([block(share, near ^ far, half), block(share, near, half)], axis=0).astype(dtype)
        for half, (near, far) in enumerate(NEAR_FAR)
    ]


def reduce_near(cuts):
    return [swap(cut, "dp", near) for cut, (near, _) in zip(cuts, NEAR_FAR)]


def reduce_far(share, block, got):
    rows = got[0].shape[0] // 2
    kept = [
        (block(share, far, half) + got[half][:rows].astype(F32)).astype(got[half].dtype)
        for half, (_, far) in enumerate(NEAR_FAR)
    ]
    mine = [block(share, 0, half) + got[half][rows:].astype(F32) for half in range(2)]
    kept = lax.optimization_barrier(kept)
    far_got = [swap(piece, "dp", far) for piece, (_, far) in zip(kept, NEAR_FAR)]
    return jnp.concatenate([piece + other.astype(F32) for piece, other in zip(mine, far_got)], axis=0)


def gather_near(own):
    rows = own.shape[0] // 2
    upper, lower = own[:rows], own[rows:]
    upper1, lower2 = swap(upper, "dp", 1), swap(lower, "dp", 2)
    upper2, lower1 = swap(upper, "dp", 2), swap(lower, "dp", 1)
    return [(upper, lower), (upper1, lower1), (upper2, lower2)]


def gather_far(first):
    return first + [(swap(first[1][0], "dp", 2), swap(first[2][1], "dp", 1))]


def line_permute(block, reach):
    chips = lax.axis_size("mp") // 2
    pairs = [(2 * z + c, 2 * ((z + reach) % chips) + c) for z in range(chips) for c in range(2)]
    return lax.ppermute(block, "mp", pairs)


def line_send(shares):
    groups = [list(range(core, lax.axis_size("mp"), 2)) for core in range(2)]
    return lax.all_to_all(shares, "mp", split_axis=0, concat_axis=0, axis_index_groups=groups, tiled=True)


def pair_kernel(place_ref, own_ref, sibling_ref, own_weight_ref, sibling_weight_ref, *out_refs, dims):
    share = mm(own_ref[...], own_weight_ref[...], dims) + mm(sibling_ref[...], sibling_weight_ref[...], dims)
    share = share.astype(BF16)
    if len(out_refs) == 1:
        out_refs[0][0] = share
        return
    for reach, out_ref in enumerate(out_refs):

        @pl.when(pl.program_id(0) == reach)
        def _(out_ref=out_ref):
            out_ref[...] = share


def pair_product(left, theirs, own_weight, sibling_weight, dims, depth, tokens, stacked):
    chips = lax.axis_size("mp") // 2
    inner = left.shape[1]
    whole = lambda i, place: (0, 0)
    place = lax.axis_index("mp").astype(jnp.int32)
    there = lambda i, place: lax.rem(place[0] + i, chips)
    return pl.pallas_call(
        lambda *refs: pair_kernel(*refs, dims=dims),
        grid_spec=pltpu.PrefetchScalarGridSpec(
            num_scalar_prefetch=1,
            grid=(chips,),
            in_specs=[
                pl.BlockSpec((tokens, inner), lambda i, place: (2 * there(i, place) + place[1], 0)),
                pl.BlockSpec((tokens, inner), lambda i, place: (there(i, place), 0)),
                pl.BlockSpec(own_weight.shape, whole),
                pl.BlockSpec(sibling_weight.shape, whole),
            ],
            out_specs=[pl.BlockSpec((1, tokens, depth), lambda i, place: (there(i, place), 0, 0))]
            if stacked
            else [pl.BlockSpec((tokens, depth), whole)] * chips,
        ),
        out_shape=[jax.ShapeDtypeStruct((chips, tokens, depth), BF16)]
        if stacked
        else [jax.ShapeDtypeStruct((tokens, depth), BF16)] * chips,
        compiler_params=pltpu.CompilerParams(dimension_semantics=("arbitrary",), vmem_limit_bytes=VMEM),
        cost_estimate=FREE,
        name="pair_product",
    )(jnp.stack([place // 2, place % 2]), left, theirs, own_weight, sibling_weight)


def for_sibling(left, tokens):
    mp = lax.axis_size("mp")
    by_core = left.reshape(mp // 2, 2, tokens, left.shape[1])
    other = 1 - lax.axis_index("mp") % 2
    return lax.dynamic_index_in_dim(by_core, other, 1, keepdims=False).reshape(-1, left.shape[1])


def in_place_order(pieces):
    place = lax.axis_index("dp")
    pieces = [jnp.concatenate(pair, axis=0) for pair in pieces]
    odd, high = place % 2 == 1, place // 2 == 1
    lows = [jnp.where(odd, pieces[k ^ 1], pieces[k]) for k in range(4)]
    return jnp.concatenate([jnp.where(high, lows[k ^ 2], lows[k]).astype(F32) for k in range(4)], axis=0)


def keep_kernel(in_ref, out_ref):
    out_ref[...] = in_ref[...]


def keep(array):
    rows = 64
    spec = pl.BlockSpec((rows, array.shape[1]), lambda i: (i, 0))
    return pl.pallas_call(
        keep_kernel,
        grid=(array.shape[0] // rows,),
        in_specs=[spec],
        out_specs=spec,
        out_shape=jax.ShapeDtypeStruct(array.shape, array.dtype),
        cost_estimate=FREE,
        name="keep",
    )(array)


def assemble_kernel(place_ref, *refs):
    out_ref = refs[-1]
    for own in range(4):

        @pl.when(place_ref[0] == own)
        def _(own=own):
            order = [refs[2 * (own ^ p) + half][...].astype(F32) for p in range(4) for half in range(2)]
            out_ref[...] = jnp.concatenate(order, axis=0).T


def assemble(gathered):
    pieces = [half for pair in gathered for half in pair]
    half_rows, columns = pieces[0].shape
    chunk = 1280
    return pl.pallas_call(
        assemble_kernel,
        grid=(pl.cdiv(columns, chunk),),
        in_specs=[pl.BlockSpec(memory_space=pltpu.SMEM)]
        + [pl.BlockSpec((half_rows, chunk), lambda i: (0, i)) for _ in pieces],
        out_specs=pl.BlockSpec((chunk, 8 * half_rows), lambda i: (i, 0)),
        out_shape=jax.ShapeDtypeStruct((columns, 8 * half_rows), F32),
        compiler_params=pltpu.CompilerParams(dimension_semantics=("arbitrary",), vmem_limit_bytes=VMEM),
        cost_estimate=pl.CostEstimate(flops=1, bytes_accessed=30 * 2**20, transcendentals=0),
        name="assemble",
    )(lax.axis_index("dp").astype(jnp.int32)[None], *pieces).T


def total(blocks):
    result = blocks[0].astype(F32)
    for index in range(1, len(blocks)):
        result = result + blocks[index].astype(F32)
    return result


def on_device(
    inputs, cotangent, widths, norm_gain, in_weight, conv_weight, conv_bias, step_bias, rate_log,
    skip_gain, out_gain, out_weight,
):
    mp, dp = lax.axis_size("mp"), lax.axis_size("dp")
    mp_place, dp_place = lax.axis_index("mp"), lax.axis_index("dp")
    heads, inner, channels = step_bias.shape[0], out_gain.shape[0], conv_bias.shape[0]
    head_dim, state_dim = inner // heads, (channels - inner) // 2
    own_heads = heads // mp
    own = own_heads * head_dim
    width = -(-own // LANES) * LANES
    joint = 2 * state_dim + width
    columns = joint + width + LANES
    tokens, depth = inputs.shape
    rows = depth // mp
    part = rows // dp
    seqs = widths.shape[0]
    all_tokens = tokens * mp

    slab = lax.dynamic_slice_in_dim(in_weight, dp_place * part, part, 0)
    by_place = lambda piece, size: pad_last(
        piece.reshape(part, mp, piece.shape[1] // mp).transpose(1, 0, 2), size
    )
    send = jnp.concatenate(
        [
            by_place(slab[:, :inner], width),
            jnp.broadcast_to(slab[None, :, 2 * inner : 2 * inner + 2 * state_dim], (mp, part, 2 * state_dim)),
            by_place(slab[:, inner : 2 * inner], width),
            by_place(slab[:, inner + channels :], LANES),
        ],
        axis=2,
    )
    got = lax.all_to_all(send, "mp", split_axis=0, concat_axis=0, tiled=True)

    def reorder(array):
        apart = array.reshape(-1, mp, dp, part)
        return jnp.concatenate(
            [
                lax.dynamic_index_in_dim(apart, dp_place ^ k, 2, keepdims=False).reshape(-1, mp * part)
                for k in range(dp)
            ],
            axis=1,
        )

    def restore(array):
        apart = array.reshape(-1, dp, mp, part)
        return jnp.stack(
            [lax.dynamic_index_in_dim(apart, dp_place ^ k, 1, keepdims=False) for k in range(dp)], axis=2
        ).reshape(-1, depth)

    line = mp <= 16
    inputs_f = inputs.astype(F32)
    rms_scale = lax.rsqrt(jnp.mean(inputs_f * inputs_f, axis=-1, keepdims=True) + EPS)
    gain_in = reorder(norm_gain[None, :])
    normed = reorder(inputs).astype(F32) * rms_scale
    hidden_own = (normed * gain_in).astype(BF16)
    hidden_own, got = lax.optimization_barrier((hidden_own, got))
    weight = jnp.concatenate(sum(gather_far(gather_near(got.reshape(mp * part, columns))), ()), axis=0)
    hidden = lax.all_gather(hidden_own, "mp", axis=0, tiled=True)

    first_chan, first_head = mp_place * own, mp_place * own_heads
    cut = lambda array, first, size: lax.dynamic_slice_in_dim(array, first, size, array.ndim - 1)
    taps_all = jnp.concatenate([conv_weight, conv_bias[None, :]], axis=0)
    taps = pad_rows(
        jnp.concatenate([taps_all[:, inner:], pad_last(cut(taps_all, first_chan, own), width)], axis=1), 8
    )
    head_rows = jnp.stack([step_bias, -jnp.exp(rate_log)])
    head_params = pad_rows(pad_last(cut(head_rows, first_head, own_heads), LANES), 8)
    skip = jnp.repeat(cut(skip_gain, first_head, own_heads), head_dim)[None, :]
    skip = pad_rows(pad_last(skip, width), 8)
    active_heads = heads // 8 * jnp.left_shift(jnp.int32(1), widths)
    head_mask = (first_head + jnp.arange(own_heads, dtype=jnp.int32))[None, :] < active_heads[:, None]
    chan_mask = jnp.repeat(head_mask.astype(F32), head_dim, axis=1)
    mask = pad_last(chan_mask, width)[:, None, :]
    per_token = lambda array: jnp.repeat(array, all_tokens // seqs, axis=0)
    mask_tok = chan_mask if seqs == 1 else per_token(chan_mask)
    active_count = (active_heads * head_dim).astype(F32)[:, None]
    if seqs > 1:
        active_count = per_token(active_count)

    if line:
        sibling_out, sibling_weight = swap(out_weight, "mp", 1), swap(weight, "mp", 1)
        weight, sibling_out, sibling_weight = lax.optimization_barrier((weight, sibling_out, sibling_weight))
    projected, y_all, states, squares, pre = mixer_forward(
        mask, hidden, weight, taps, head_params, skip, state_dim, width
    )
    square_rows = all_sum(squares[:, 0, :], "mp")
    total_square = square_rows.reshape(all_tokens)[:, None]
    gate = projected[:, :own].astype(F32)
    y_f = y_all[:, :own].astype(F32)
    gate_sig = jax.nn.sigmoid(gate)
    silu_z = gate * gate_sig
    gated = y_f * silu_z
    gain = cut(out_gain, first_chan, own)[None, :]
    out_root = lax.rsqrt(total_square / active_count + EPS)
    normed_out = (gated * out_root * gain * mask_tok).astype(BF16)
    if line:
        theirs = swap(for_sibling(normed_out, tokens), "mp", 1)
        shares = pair_product(normed_out, theirs, out_weight, sibling_out, NN, depth, tokens, True)[0]
        cot_all = lax.all_gather(cotangent, "mp", axis=0, tiled=True)
        cot_all, shares = lax.optimization_barrier((cot_all, shares))
    else:
        shares = mm(normed_out, out_weight).astype(BF16)
        sent = [lax.psum_scatter(shares, "mp", scatter_dimension=0, tiled=True)]
        late_cot, sent = lax.optimization_barrier((cotangent, sent))
        cot_all = lax.all_gather(late_cot, "mp", axis=0, tiled=True)

    gain_rows = pad_last(cut(out_gain, first_chan, own), width)
    gains = jnp.concatenate(
        [
            gain_rows[None, None, :] * mask,
            mask,
            jnp.broadcast_to((active_heads * head_dim).astype(F32)[:, None, None], mask.shape),
            jnp.zeros((seqs, 5, width), F32),
        ],
        axis=1,
    )
    out_padded = pad_rows(out_weight, width)
    d_normed, dots = pull_back(cot_all, out_padded, projected, y_all, gains, 0)
    dot_rows = all_sum(dots[:, 0, :], "mp")
    out_part = mm(normed_out, cot_all, TN)
    if line:
        dot_rows, shares = lax.optimization_barrier((dot_rows, shares))
        sent = line_send(shares)
    token_rows = jnp.stack([square_rows, dot_rows] + [jnp.zeros_like(dot_rows)] * 6, axis=1)
    quarter = depth // dp

    def in_block(share, k, half):
        return share[k * quarter + half * (quarter // 2) : k * quarter + (half + 1) * (quarter // 2)]

    def to_rows(mine):
        return lax.all_to_all(mine.astype(BF16).reshape(mp, part, -1), "mp", split_axis=0, concat_axis=0, tiled=True)

    token_rows, out_part = lax.optimization_barrier((token_rows, out_part))
    out_mine = lax.psum_scatter(out_part, "dp", scatter_dimension=0, tiled=True)
    def norm_share(d_hidden):
        share = restore(jnp.sum(d_hidden * normed, axis=0)[None, :])
        return all_sum(share.reshape(-1, LANES), "dp")

    def rows_of(blocks):
        flat = lambda first, size: blocks[:, :, first : first + size].transpose(1, 0, 2).reshape(part, -1)
        shared = jnp.sum(blocks[:, :, width : width + 2 * state_dim].astype(F32), axis=0).astype(BF16)
        return jnp.concatenate(
            [flat(0, own), flat(width + 2 * state_dim, own), shared, flat(width + joint, own_heads)], axis=1
        )

    d_proj, conv_grads, head_grads, gain_grads = mixer_backward(
        gains, projected, pre, y_all, d_normed, token_rows, states, taps, head_params, skip, state_dim
    )
    d_proj, out_mine = lax.optimization_barrier((d_proj, out_mine))
    out_weight_grad = lax.all_gather(out_mine, "dp", axis=0, tiled=True)

    def place_in(array, first, size):
        return lax.dynamic_update_slice_in_dim(
            jnp.zeros(array.shape[:-1] + (size,), F32), array, first, array.ndim - 1
        )

    conv_own = place_in(conv_grads[:5, 2 * state_dim : 2 * state_dim + own], first_chan, inner)
    conv_full = jnp.concatenate([conv_own, conv_grads[:5, : 2 * state_dim]], axis=1)
    head_full = place_in(head_grads[:3, :own_heads], first_head, heads)
    gain_full = place_in(gain_grads[0, :own], first_chan, inner)
    small = [conv_full.reshape(-1), head_full.reshape(-1), gain_full]
    sizes = [piece.shape[0] for piece in small]
    packed = jnp.concatenate(small)
    count = -(-packed.shape[0] // 1024) * 1024
    packed = jnp.pad(packed, (0, count - packed.shape[0])).reshape(-1, LANES)

    if line:
        theirs = swap(for_sibling(d_proj, tokens), "mp", 1)
        d_shares = pair_product(d_proj, theirs, weight, sibling_weight, NT, depth, tokens, False)
        d_shares, d_proj, sent = lax.optimization_barrier((d_shares, d_proj, sent))
        reaches = list(range(1, mp // 2))
        d_blocks = [d_shares[0], line_permute(d_shares[1], 1)]
        share = mm(hidden, d_proj, TN)
        near_cut = reduce_cut(share, in_block, BF16)
        near_cut, d_blocks, out_weight_grad = lax.optimization_barrier((near_cut, d_blocks, out_weight_grad))
        near_got = reduce_near(near_cut)
        d_blocks += [line_permute(d_shares[reach], reach) for reach in reaches[1:2]]
        near_got, d_blocks = lax.optimization_barrier((near_got, d_blocks))
        mine = reduce_far(share, in_block, near_got)
        d_blocks += [line_permute(d_shares[reach], reach) for reach in reaches[2:]]
        mine, packed, d_blocks = lax.optimization_barrier((mine, packed, d_blocks))
        blocks = to_rows(mine)
        d_hidden = total(d_blocks)
        norm_part = norm_share(d_hidden)
        blocks, packed, out_weight_grad, norm_part = lax.optimization_barrier(
            (blocks, all_sum(packed, "dp"), keep(out_weight_grad), norm_part)
        )
        in_weight_grad = assemble(gather_far(gather_near(rows_of(blocks))))
    else:
        packed = all_sum(packed, "dp")
        share = mm(hidden, d_proj, TN)
        d_proj, share = lax.optimization_barrier((d_proj, share))
        blocks = to_rows(reduce_far(share, in_block, reduce_near(reduce_cut(share, in_block, BF16))))
        d_shares = mm(d_proj, weight, NT).astype(BF16)
        d_hidden = lax.psum_scatter(d_shares, "mp", scatter_dimension=0, tiled=True).astype(F32)
        in_weight_grad = in_place_order(gather_far(gather_near(rows_of(blocks))))
    outputs = (inputs_f + total(sent)).astype(BF16)
    if not line:
        norm_part = norm_share(d_hidden)
    everything = all_sum(jnp.concatenate([packed, norm_part], axis=0), "mp")
    norm_total = everything[packed.shape[0] :].reshape(depth)
    packed = everything.reshape(-1)
    conv_total = packed[: sizes[0]].reshape(conv_full.shape)
    head_total = packed[sizes[0] : sizes[0] + sizes[1]].reshape(head_full.shape)
    gain_total = packed[sizes[0] + sizes[1] : sum(sizes)]

    d_normed_in = d_hidden * gain_in
    input_back = rms_scale * (d_normed_in - normed * jnp.mean(d_normed_in * normed, axis=-1, keepdims=True))
    input_grad = restore((reorder(cotangent).astype(F32) + input_back).astype(BF16))

    return (
        outputs,
        input_grad,
        norm_total,
        in_weight_grad,
        conv_total[:4],
        conv_total[4],
        head_total[0],
        head_total[1],
        head_total[2],
        gain_total,
        out_weight_grad,
    )


def solution(mesh):
    rows = P(("dp", "mp"), None)
    return jax.shard_map(
        on_device,
        mesh=mesh,
        in_specs=(rows, rows, P("dp"), P(), P("mp", None), P(), P(), P(), P(), P(), P(), P("mp", None)),
        out_specs=(rows, rows, P(), P("mp", None), P(), P(), P(), P(), P(), P(), P("mp", None)),
        check_vma=False,
    )
```

```python
import jax
import jax.numpy as jnp
from jax import lax
from jax.experimental import pallas as pl
from jax.experimental.pallas import tpu as pltpu
from jax.sharding import PartitionSpec as P

SEQ = 2048
BLOCK = 256
EPS = 1e-05
LANES = 128
VMEM = 56 * 2**20
FREE = pl.CostEstimate(flops=1, bytes_accessed=1, transcendentals=0)

F32 = jnp.float32
BF16 = jnp.bfloat16
NN = (((1,), (0,)), ((), ()))
NT = (((1,), (1,)), ((), ()))
TN = (((0,), (0,)), ((), ()))


def mm(left, right, dims=NN):
    return lax.dot_general(left, right, dims, preferred_element_type=F32)


def halves(value):
    high = value.astype(BF16)
    return high, (value - high.astype(F32)).astype(BF16)


def mm3(left, right, dims=NN):
    return mm(left[0], right[0], dims) + (mm(left[0], right[1], dims) + mm(left[1], right[0], dims))


def mm_exact(ones, value, dims=NN):
    first, rest = value.astype(BF16), None
    rest = value - first.astype(F32)
    second = rest.astype(BF16)
    third = (rest - second.astype(F32)).astype(BF16)
    return mm(ones, first, dims) + (mm(ones, second, dims) + mm(ones, third, dims))


def spread(per_head, width):
    rows = per_head.shape[0]
    low_half = lax.broadcasted_iota(jnp.int32, (rows, LANES), 1) < LANES // 2
    parts = []
    for pair in range(width // LANES):
        parts.append(
            jnp.where(
                low_half, per_head[:, 2 * pair : 2 * pair + 1], per_head[:, 2 * pair + 1 : 2 * pair + 2]
            )
        )
    return parts[0] if len(parts) == 1 else jnp.concatenate(parts, axis=1)


def head_ones(width):
    chan = lax.broadcasted_iota(jnp.int32, (width, LANES), 0)
    head = lax.broadcasted_iota(jnp.int32, (width, LANES), 1)
    return (chan // (LANES // 2) == head).astype(BF16)


def head_sum(per_chan, ones):
    high, low = halves(per_chan)
    return mm(high, ones) + mm(low, ones)


def conv_block(ext_ref, taps_ref):
    span = 4
    pre = taps_ref[span : span + 1, :] + ext_ref[5 : 5 + BLOCK, :] * taps_ref[0:1, :]
    for tap in range(1, span):
        pre = pre + ext_ref[5 + tap : 5 + tap + BLOCK, :] * taps_ref[tap : tap + 1, :]
    return pre


def step_rates(step_raw, heads_ref):
    biased = step_raw + heads_ref[0:1, :]
    step_size = jnp.maximum(biased, 0.0) + jnp.log1p(jnp.exp(-jnp.abs(biased)))
    decay = heads_ref[1:2, :] * step_size
    return biased, step_size, decay


def triangle(keep):
    row = lax.broadcasted_iota(jnp.int32, (BLOCK, BLOCK), 0)
    col = lax.broadcasted_iota(jnp.int32, (BLOCK, BLOCK), 1)
    return keep(row, col)


def forward_kernel(
    mask_ref, hidden_ref, weight_ref, taps_ref, heads_ref, skip_ref,
    proj_ref, y_ref, state_ref, square_ref, pre_ref,
    ext, state, *, state_dim, width,
):
    joint = 2 * state_dim + width

    @pl.when(pl.program_id(1) == 0)
    def _():
        ext[0:8, :] = jnp.zeros((8, joint), F32)
        state[...] = jnp.zeros_like(state)

    projected = mm(hidden_ref[...], weight_ref[...]).astype(BF16)
    proj_ref[...] = projected
    ext[8 : 8 + BLOCK, :] = projected[:, width : width + joint].astype(F32)
    pre = conv_block(ext, taps_ref)
    pre_ref[...] = pre
    ext[0:8, :] = ext[BLOCK : BLOCK + 8, :]
    conv_out = pre * jax.nn.sigmoid(pre)
    values = conv_out[:, 2 * state_dim :] * mask_ref[0]
    b_coef = halves(conv_out[:, :state_dim])
    c_coef = halves(conv_out[:, state_dim : 2 * state_dim])
    _, step_size, decay = step_rates(projected[:, joint + width :].astype(F32), heads_ref)
    causal = triangle(lambda row, col: row >= col)
    cumulative = mm_exact(causal.astype(BF16), decay)
    across = cumulative.T
    last = cumulative[BLOCK - 1 : BLOCK, :]
    scaled = values * spread(step_size, width)
    scaled_parts = halves(scaled)
    scores = mm3(c_coef, b_coef, NT)
    low_half = lax.broadcasted_iota(jnp.int32, (BLOCK, LANES), 1) < LANES // 2
    old = state[...]
    state_ref[0] = old
    mixed = spread(jnp.exp(cumulative), width) * mm3(c_coef, halves(old))
    within = []
    for pair in range(width // LANES):
        lanes = slice(pair * LANES, (pair + 1) * LANES)
        rhs = (scaled_parts[0][:, lanes], scaled_parts[1][:, lanes])
        sides = []
        for head in (2 * pair, 2 * pair + 1):
            gap = jnp.where(causal, cumulative[:, head : head + 1] - across[head : head + 1, :], -1e30)
            sides.append(mm3(halves(scores * jnp.exp(gap)), rhs))
        within.append(jnp.where(low_half, sides[0], sides[1]))
    mixed = mixed + (within[0] if len(within) == 1 else jnp.concatenate(within, axis=1))
    tail = halves(scaled * spread(jnp.exp(last - cumulative), width))
    state[...] = old * spread(jnp.exp(last), width) + mm3(b_coef, tail, TN)
    y_low = (mixed + skip_ref[0:1, :] * values).astype(BF16)
    y_ref[...] = y_low
    gate = projected[:, :width].astype(F32)
    gated = y_low.astype(F32) * (gate * jax.nn.sigmoid(gate))
    square = halves(gated * gated * mask_ref[0])
    ones = jnp.ones((8, width), BF16)
    square_ref[0] = mm(ones, square[0], NT) + mm(ones, square[1], NT)


def backward_kernel(
    gain_ref, proj_ref, pre_ref, y_ref, d_normed_ref, tokens_ref, state_ref, taps_ref, heads_ref, skip_ref,
    dproj_ref, conv_grad_ref, head_grad_ref, gain_grad_ref,
    dext, dstate, rows, *, state_dim, width,
):
    joint = 2 * state_dim + width

    @pl.when((pl.program_id(0) == 0) & (pl.program_id(1) == 0))
    def _():
        conv_grad_ref[...] = jnp.zeros_like(conv_grad_ref)
        head_grad_ref[...] = jnp.zeros_like(head_grad_ref)
        gain_grad_ref[...] = jnp.zeros_like(gain_grad_ref)
        rows[...] = jnp.zeros_like(rows)

    @pl.when(pl.program_id(1) == 0)
    def _():
        dext[0:8, :] = jnp.zeros((8, joint), F32)
        dstate[...] = jnp.zeros_like(dstate)

    per_token = tokens_ref[0].T
    count = gain_ref[0, 2:3, 0:1]
    root = lax.rsqrt(per_token[:, 0:1] / count + EPS)
    pull = root * root * per_token[:, 1:2] / count
    gate = proj_ref[:, :width].astype(F32)
    y = y_ref[...].astype(F32)
    gate_sig = jax.nn.sigmoid(gate)
    silu = gate * gate_sig
    normed_gated = y * silu * root * gain_ref[0, 1:2, :]
    d_normed = d_normed_ref[...]
    gain_grad_ref[0:1, :] += jnp.sum(d_normed * normed_gated, axis=0, keepdims=True)
    d_gated = root * (d_normed * gain_ref[0, 0:1, :]) - normed_gated * pull
    dy_low = (d_gated * silu).astype(BF16)
    dproj_ref[:, :width] = (d_gated * y * gate_sig * (1.0 + gate * (1.0 - gate_sig))).astype(BF16)

    pre = pre_ref[...]
    sig = jax.nn.sigmoid(pre)
    conv_out = pre * sig
    mask = gain_ref[0, 1:2, :]
    values = conv_out[:, 2 * state_dim :] * mask
    b_coef = halves(conv_out[:, :state_dim])
    c_coef = halves(conv_out[:, state_dim : 2 * state_dim])
    biased, step_size, decay = step_rates(proj_ref[:, joint + width :].astype(F32), heads_ref)
    later = triangle(lambda row, col: col >= row)
    cumulative = mm_exact(triangle(lambda row, col: row >= col).astype(BF16), decay)
    across = cumulative.T
    last = cumulative[BLOCK - 1 : BLOCK, :]
    step_chan = spread(step_size, width)
    scaled = values * step_chan
    scaled_parts = halves(scaled)
    dy = dy_low.astype(F32)
    scores = mm3(b_coef, c_coef, NT)
    low_half = lax.broadcasted_iota(jnp.int32, (BLOCK, LANES), 1) < LANES // 2
    lane = lax.broadcasted_iota(jnp.int32, (BLOCK, LANES), 1)
    d_scores = jnp.zeros((BLOCK, BLOCK), F32)
    from_rows = jnp.zeros((BLOCK, LANES), F32)
    d_within = []
    for pair in range(width // LANES):
        lanes = slice(pair * LANES, (pair + 1) * LANES)
        dy_pair = dy_low[:, lanes]
        dy_twice = jnp.concatenate([dy_pair, dy_pair], axis=1)
        sides = []
        for side in range(2):
            head = 2 * pair + side
            own = low_half if side == 0 else jnp.logical_not(low_half)
            left = jnp.concatenate(
                [jnp.where(own, part[:, lanes], jnp.zeros((), BF16)) for part in scaled_parts], axis=1
            )
            d_mixing = mm(left, dy_twice, NT)
            gap = jnp.where(later, across[head : head + 1, :] - cumulative[:, head : head + 1], -1e30)
            weight = jnp.exp(gap)
            mixing = scores * weight
            d_scores = d_scores + d_mixing * weight
            product = d_mixing * mixing
            rows[head : head + 1, :] = jnp.sum(product, axis=0, keepdims=True)
            from_rows = jnp.where(lane == head, jnp.sum(product, axis=1, keepdims=True), from_rows)
            parts = halves(mixing)
            sides.append(mm(parts[0], dy_pair) + mm(parts[1], dy_pair))
        d_within.append(jnp.where(low_half, sides[0], sides[1]))
    ones = head_ones(width)
    old = state_ref[0]
    old_parts = halves(old)
    grown = dstate[...]
    grown_parts = halves(grown)
    ey = spread(jnp.exp(cumulative), width) * dy
    ey_parts = halves(ey)
    tail_chan = spread(jnp.exp(last - cumulative), width)
    tail = scaled * tail_chan
    tail_parts = halves(tail)
    last_chan = spread(jnp.exp(last), width)
    into_state = mm3(b_coef, grown_parts)
    d_scaled = (d_within[0] if len(d_within) == 1 else jnp.concatenate(d_within, axis=1)) + tail_chan * into_state
    d_parts = halves(d_scores)
    d_c = mm3(d_parts, b_coef, TN) + mm3(ey_parts, old_parts, NT)
    d_b = mm3(d_parts, c_coef) + mm3(tail_parts, grown_parts, NT)
    end_terms = mm((ey * mm3(c_coef, old_parts)).astype(BF16), ones)
    start_terms = mm((tail * into_state).astype(BF16), ones)
    kept = jnp.sum(last_chan * grown * old, axis=0, keepdims=True)
    skip_part = jnp.sum(dy * values, axis=0, keepdims=True)
    kept_heads = mm_exact_left(jnp.concatenate([kept, skip_part, jnp.zeros((6, width), F32)], axis=0), ones)
    dstate[...] = last_chan * grown + mm3(c_coef, ey_parts, TN)
    gaps = rows[...].T - from_rows + end_terms
    d_decay = (
        mm_exact(later.astype(BF16), gaps)
        + mm_exact(triangle(lambda row, col: col < row).astype(BF16), start_terms)
        + kept_heads[0:1, :]
    )
    d_step = head_sum(d_scaled * values, ones) + d_decay * heads_ref[1:2, :]
    d_raw = d_step * jax.nn.sigmoid(biased)
    head_grad_ref[0:1, :] += jnp.sum(d_raw, axis=0, keepdims=True)
    head_grad_ref[1:2, :] += jnp.sum(d_decay * decay, axis=0, keepdims=True)
    head_grad_ref[2:3, :] += kept_heads[1:2, :]
    d_values = (d_scaled * step_chan + skip_ref[0:1, :] * dy) * mask
    d_conv = jnp.concatenate([d_b, d_c, d_values], axis=1)
    d_pre = d_conv * (sig * (1.0 + pre * (1.0 - sig)))
    conv_grad_ref[4:5, :] += jnp.sum(d_pre, axis=0, keepdims=True)
    dext[BLOCK : BLOCK + 8, :] = dext[0:8, :]
    dext[0:BLOCK, :] = d_pre
    conv_in = proj_ref[:, width : width + joint].astype(F32)
    d_in = None
    for tap in range(4):
        ahead = d_pre if tap == 3 else dext[3 - tap : 3 - tap + BLOCK, :]
        conv_grad_ref[tap : tap + 1, :] += jnp.sum(ahead * conv_in, axis=0, keepdims=True)
        d_in = ahead * taps_ref[tap : tap + 1, :] if tap == 0 else d_in + ahead * taps_ref[tap : tap + 1, :]
    dproj_ref[:, width : width + joint] = d_in.astype(BF16)
    dproj_ref[:, joint + width :] = d_raw.astype(BF16)


def mm_exact_left(value, ones):
    first = value.astype(BF16)
    rest = value - first.astype(F32)
    second = rest.astype(BF16)
    third = (rest - second.astype(F32)).astype(BF16)
    return mm(first, ones) + (mm(second, ones) + mm(third, ones))


def mixer_forward(mask, hidden, weight, taps, heads, skip, state_dim, width):
    seqs = mask.shape[0]
    tokens, depth = hidden.shape
    blocks = tokens // seqs // BLOCK
    columns = weight.shape[1]
    joint = 2 * state_dim + width
    row = lambda s, c: (s * blocks + c, 0)
    whole = lambda s, c: (0, 0)
    return pl.pallas_call(
        lambda *refs: forward_kernel(*refs, state_dim=state_dim, width=width),
        grid=(seqs, blocks),
        in_specs=[
            pl.BlockSpec((1, 1, width), lambda s, c: (s, 0, 0)),
            pl.BlockSpec((BLOCK, depth), row),
            pl.BlockSpec((depth, columns), whole),
            pl.BlockSpec((8, joint), whole),
            pl.BlockSpec((8, LANES), whole),
            pl.BlockSpec((8, width), whole),
        ],
        out_specs=[
            pl.BlockSpec((BLOCK, columns), row),
            pl.BlockSpec((BLOCK, width), row),
            pl.BlockSpec((1, state_dim, width), lambda s, c: (s * blocks + c, 0, 0)),
            pl.BlockSpec((1, 8, BLOCK), lambda s, c: (s * blocks + c, 0, 0)),
            pl.BlockSpec((BLOCK, joint), row),
        ],
        out_shape=[
            jax.ShapeDtypeStruct((tokens, columns), BF16),
            jax.ShapeDtypeStruct((tokens, width), BF16),
            jax.ShapeDtypeStruct((seqs * blocks, state_dim, width), F32),
            jax.ShapeDtypeStruct((seqs * blocks, 8, BLOCK), F32),
            jax.ShapeDtypeStruct((tokens, joint), F32),
        ],
        scratch_shapes=[
            pltpu.VMEM((BLOCK + 8, joint), F32),
            pltpu.VMEM((state_dim, width), F32),
        ],
        compiler_params=pltpu.CompilerParams(
            dimension_semantics=("arbitrary", "arbitrary"), vmem_limit_bytes=VMEM
        ),
        cost_estimate=FREE,
        name="mixer_forward",
    )(mask, hidden, weight, taps, heads, skip)


def mixer_backward(gains, projected, pre, y_all, d_normed, token_rows, states, taps, heads, skip, state_dim):
    seqs, _, width = gains.shape
    tokens, columns = projected.shape
    blocks = tokens // seqs // BLOCK
    joint = 2 * state_dim + width
    place = lambda s, c: s * blocks + blocks - 1 - c
    row = lambda s, c: (place(s, c), 0)
    block = lambda s, c: (place(s, c), 0, 0)
    whole = lambda s, c: (0, 0)
    return pl.pallas_call(
        lambda *refs: backward_kernel(*refs, state_dim=state_dim, width=width),
        grid=(seqs, blocks),
        in_specs=[
            pl.BlockSpec((1, 8, width), lambda s, c: (s, 0, 0)),
            pl.BlockSpec((BLOCK, columns), row),
            pl.BlockSpec((BLOCK, joint), row),
            pl.BlockSpec((BLOCK, width), row),
            pl.BlockSpec((BLOCK, width), row),
            pl.BlockSpec((1, 8, BLOCK), block),
            pl.BlockSpec((1, state_dim, width), block),
            pl.BlockSpec((8, joint), whole),
            pl.BlockSpec((8, LANES), whole),
            pl.BlockSpec((8, width), whole),
        ],
        out_specs=[
            pl.BlockSpec((BLOCK, columns), row),
            pl.BlockSpec((8, joint), whole),
            pl.BlockSpec((8, LANES), whole),
            pl.BlockSpec((8, width), whole),
        ],
        out_shape=[
            jax.ShapeDtypeStruct((tokens, columns), BF16),
            jax.ShapeDtypeStruct((8, joint), F32),
            jax.ShapeDtypeStruct((8, LANES), F32),
            jax.ShapeDtypeStruct((8, width), F32),
        ],
        scratch_shapes=[
            pltpu.VMEM((BLOCK + 8, joint), F32),
            pltpu.VMEM((state_dim, width), F32),
            pltpu.VMEM((LANES, BLOCK), F32),
        ],
        compiler_params=pltpu.CompilerParams(
            dimension_semantics=("arbitrary", "arbitrary"), vmem_limit_bytes=VMEM
        ),
        cost_estimate=FREE,
        name="mixer_backward",
    )(gains, projected, pre, y_all, d_normed, token_rows, states, taps, heads, skip)


def row_sum(value):
    ones = jnp.ones((8, value.shape[1]), BF16)
    high, low = halves(value)
    return mm(ones, high, NT) + mm(ones, low, NT)


def pull_kernel(cot_ref, weight_ref, gate_ref, y_ref, gain_ref, d_normed_ref, dot_ref):
    d_normed = mm(cot_ref[...], weight_ref[...])
    d_normed_ref[...] = d_normed
    gate = gate_ref[...].astype(F32)
    gated = y_ref[...].astype(F32) * (gate * jax.nn.sigmoid(gate))
    dot_ref[0] = row_sum(d_normed * gain_ref[0, 0:1, :] * gated)


def pull_back(cot_all, weight, projected, y_all, gains, gate_place):
    seqs, _, width = gains.shape
    tokens, depth = cot_all.shape
    blocks = tokens // seqs // BLOCK
    row = lambda s, c: (s * blocks + c, 0)
    return pl.pallas_call(
        pull_kernel,
        grid=(seqs, blocks),
        in_specs=[
            pl.BlockSpec((BLOCK, depth), row),
            pl.BlockSpec((depth, width), lambda s, c: (0, 0)),
            pl.BlockSpec((BLOCK, width), lambda s, c: (s * blocks + c, gate_place)),
            pl.BlockSpec((BLOCK, width), row),
            pl.BlockSpec((1, 8, width), lambda s, c: (s, 0, 0)),
        ],
        out_specs=[
            pl.BlockSpec((BLOCK, width), row),
            pl.BlockSpec((1, 8, BLOCK), lambda s, c: (s * blocks + c, 0, 0)),
        ],
        out_shape=[
            jax.ShapeDtypeStruct((tokens, width), F32),
            jax.ShapeDtypeStruct((seqs * blocks, 8, BLOCK), F32),
        ],
        compiler_params=pltpu.CompilerParams(
            dimension_semantics=("arbitrary", "arbitrary"), vmem_limit_bytes=VMEM
        ),
        cost_estimate=FREE,
        name="pull_back",
    )(cot_all, weight, projected, y_all, gains)


def pad_last(array, size):
    extra = size - array.shape[-1]
    if extra == 0:
        return array
    return jnp.pad(array, [(0, 0)] * (array.ndim - 1) + [(0, extra)])


def pad_rows(array, size):
    return jnp.pad(array, [(0, size - array.shape[0]), (0, 0)])


def swap(value, axis, bit):
    size = lax.axis_size(axis)
    return lax.ppermute(value, axis, [(place, place ^ bit) for place in range(size)])


def all_sum(value, axis):
    bit = 1
    while bit < lax.axis_size(axis):
        value = value + swap(value, axis, bit)
        bit *= 2
    return value


NEAR_FAR = ((1, 2), (2, 1))


def reduce_cut(share, block, dtype):
    return [
        jnp.concatenate([block(share, near ^ far, half), block(share, near, half)], axis=0).astype(dtype)
        for half, (near, far) in enumerate(NEAR_FAR)
    ]


def reduce_near(cuts):
    return [swap(cut, "dp", near) for cut, (near, _) in zip(cuts, NEAR_FAR)]


def reduce_far(share, block, got):
    rows = got[0].shape[0] // 2
    kept = [
        (block(share, far, half) + got[half][:rows].astype(F32)).astype(got[half].dtype)
        for half, (_, far) in enumerate(NEAR_FAR)
    ]
    mine = [block(share, 0, half) + got[half][rows:].astype(F32) for half in range(2)]
    kept = lax.optimization_barrier(kept)
    far_got = [swap(piece, "dp", far) for piece, (_, far) in zip(kept, NEAR_FAR)]
    return jnp.concatenate([piece + other.astype(F32) for piece, other in zip(mine, far_got)], axis=0)


def gather_near(own):
    rows = own.shape[0] // 2
    upper, lower = own[:rows], own[rows:]
    upper1, lower2 = swap(upper, "dp", 1), swap(lower, "dp", 2)
    upper2, lower1 = swap(upper, "dp", 2), swap(lower, "dp", 1)
    return [(upper, lower), (upper1, lower1), (upper2, lower2)]


def gather_far(first):
    return first + [(swap(first[1][0], "dp", 2), swap(first[2][1], "dp", 1))]


def line_permute(block, reach):
    chips = lax.axis_size("mp") // 2
    pairs = [(2 * z + c, 2 * ((z + reach) % chips) + c) for z in range(chips) for c in range(2)]
    return lax.ppermute(block, "mp", pairs)


def line_send(shares):
    groups = [list(range(core, lax.axis_size("mp"), 2)) for core in range(2)]
    return lax.all_to_all(shares, "mp", split_axis=0, concat_axis=0, axis_index_groups=groups, tiled=True)


def pair_kernel(place_ref, own_ref, sibling_ref, own_weight_ref, sibling_weight_ref, *out_refs, dims):
    share = mm(own_ref[...], own_weight_ref[...], dims) + mm(sibling_ref[...], sibling_weight_ref[...], dims)
    share = share.astype(BF16)
    if len(out_refs) == 1:
        out_refs[0][0] = share
        return
    for reach, out_ref in enumerate(out_refs):

        @pl.when(pl.program_id(0) == reach)
        def _(out_ref=out_ref):
            out_ref[...] = share


def pair_product(left, theirs, own_weight, sibling_weight, dims, depth, tokens, stacked):
    chips = lax.axis_size("mp") // 2
    inner = left.shape[1]
    whole = lambda i, place: (0, 0)
    place = lax.axis_index("mp").astype(jnp.int32)
    there = lambda i, place: lax.rem(place[0] + i, chips)
    return pl.pallas_call(
        lambda *refs: pair_kernel(*refs, dims=dims),
        grid_spec=pltpu.PrefetchScalarGridSpec(
            num_scalar_prefetch=1,
            grid=(chips,),
            in_specs=[
                pl.BlockSpec((tokens, inner), lambda i, place: (2 * there(i, place) + place[1], 0)),
                pl.BlockSpec((tokens, inner), lambda i, place: (there(i, place), 0)),
                pl.BlockSpec(own_weight.shape, whole),
                pl.BlockSpec(sibling_weight.shape, whole),
            ],
            out_specs=[pl.BlockSpec((1, tokens, depth), lambda i, place: (there(i, place), 0, 0))]
            if stacked
            else [pl.BlockSpec((tokens, depth), whole)] * chips,
        ),
        out_shape=[jax.ShapeDtypeStruct((chips, tokens, depth), BF16)]
        if stacked
        else [jax.ShapeDtypeStruct((tokens, depth), BF16)] * chips,
        compiler_params=pltpu.CompilerParams(dimension_semantics=("arbitrary",), vmem_limit_bytes=VMEM),
        cost_estimate=FREE,
        name="pair_product",
    )(jnp.stack([place // 2, place % 2]), left, theirs, own_weight, sibling_weight)


def for_sibling(left, tokens):
    mp = lax.axis_size("mp")
    by_core = left.reshape(mp // 2, 2, tokens, left.shape[1])
    other = 1 - lax.axis_index("mp") % 2
    return lax.dynamic_index_in_dim(by_core, other, 1, keepdims=False).reshape(-1, left.shape[1])


def in_place_order(pieces):
    place = lax.axis_index("dp")
    pieces = [jnp.concatenate(pair, axis=0) for pair in pieces]
    odd, high = place % 2 == 1, place // 2 == 1
    lows = [jnp.where(odd, pieces[k ^ 1], pieces[k]) for k in range(4)]
    return jnp.concatenate([jnp.where(high, lows[k ^ 2], lows[k]).astype(F32) for k in range(4)], axis=0)


def keep_kernel(in_ref, out_ref):
    out_ref[...] = in_ref[...]


def keep(array):
    rows = 64
    spec = pl.BlockSpec((rows, array.shape[1]), lambda i: (i, 0))
    return pl.pallas_call(
        keep_kernel,
        grid=(array.shape[0] // rows,),
        in_specs=[spec],
        out_specs=spec,
        out_shape=jax.ShapeDtypeStruct(array.shape, array.dtype),
        cost_estimate=FREE,
        name="keep",
    )(array)


def assemble_kernel(place_ref, *refs):
    out_ref = refs[-1]
    for own in range(4):

        @pl.when(place_ref[0] == own)
        def _(own=own):
            order = [refs[2 * (own ^ p) + half][...].astype(F32) for p in range(4) for half in range(2)]
            out_ref[...] = jnp.concatenate(order, axis=0).T


def assemble(gathered):
    pieces = [half for pair in gathered for half in pair]
    half_rows, columns = pieces[0].shape
    chunk = 1280
    return pl.pallas_call(
        assemble_kernel,
        grid=(pl.cdiv(columns, chunk),),
        in_specs=[pl.BlockSpec(memory_space=pltpu.SMEM)]
        + [pl.BlockSpec((half_rows, chunk), lambda i: (0, i)) for _ in pieces],
        out_specs=pl.BlockSpec((chunk, 8 * half_rows), lambda i: (i, 0)),
        out_shape=jax.ShapeDtypeStruct((columns, 8 * half_rows), F32),
        compiler_params=pltpu.CompilerParams(dimension_semantics=("arbitrary",), vmem_limit_bytes=VMEM),
        cost_estimate=pl.CostEstimate(flops=1, bytes_accessed=30 * 2**20, transcendentals=0),
        name="assemble",
    )(lax.axis_index("dp").astype(jnp.int32)[None], *pieces).T


def total(blocks):
    result = blocks[0].astype(F32)
    for index in range(1, len(blocks)):
        result = result + blocks[index].astype(F32)
    return result


def on_device(
    inputs, cotangent, widths, norm_gain, in_weight, conv_weight, conv_bias, step_bias, rate_log,
    skip_gain, out_gain, out_weight,
):
    mp, dp = lax.axis_size("mp"), lax.axis_size("dp")
    mp_place, dp_place = lax.axis_index("mp"), lax.axis_index("dp")
    heads, inner, channels = step_bias.shape[0], out_gain.shape[0], conv_bias.shape[0]
    head_dim, state_dim = inner // heads, (channels - inner) // 2
    own_heads = heads // mp
    own = own_heads * head_dim
    width = -(-own // LANES) * LANES
    joint = 2 * state_dim + width
    columns = joint + width + LANES
    tokens, depth = inputs.shape
    rows = depth // mp
    part = rows // dp
    seqs = widths.shape[0]
    all_tokens = tokens * mp

    slab = lax.dynamic_slice_in_dim(in_weight, dp_place * part, part, 0)
    by_place = lambda piece, size: pad_last(
        piece.reshape(part, mp, piece.shape[1] // mp).transpose(1, 0, 2), size
    )
    send = jnp.concatenate(
        [
            by_place(slab[:, :inner], width),
            jnp.broadcast_to(slab[None, :, 2 * inner : 2 * inner + 2 * state_dim], (mp, part, 2 * state_dim)),
            by_place(slab[:, inner : 2 * inner], width),
            by_place(slab[:, inner + channels :], LANES),
        ],
        axis=2,
    )
    got = lax.all_to_all(send, "mp", split_axis=0, concat_axis=0, tiled=True)

    def reorder(array):
        apart = array.reshape(-1, mp, dp, part)
        return jnp.concatenate(
            [
                lax.dynamic_index_in_dim(apart, dp_place ^ k, 2, keepdims=False).reshape(-1, mp * part)
                for k in range(dp)
            ],
            axis=1,
        )

    def restore(array):
        apart = array.reshape(-1, dp, mp, part)
        return jnp.stack(
            [lax.dynamic_index_in_dim(apart, dp_place ^ k, 1, keepdims=False) for k in range(dp)], axis=2
        ).reshape(-1, depth)

    line = mp <= 16
    inputs_f = inputs.astype(F32)
    rms_scale = lax.rsqrt(jnp.mean(inputs_f * inputs_f, axis=-1, keepdims=True) + EPS)
    gain_in = reorder(norm_gain[None, :])
    normed = reorder(inputs).astype(F32) * rms_scale
    hidden_own = (normed * gain_in).astype(BF16)
    hidden_own, got = lax.optimization_barrier((hidden_own, got))
    weight = jnp.concatenate(sum(gather_far(gather_near(got.reshape(mp * part, columns))), ()), axis=0)
    hidden = lax.all_gather(hidden_own, "mp", axis=0, tiled=True)

    first_chan, first_head = mp_place * own, mp_place * own_heads
    cut = lambda array, first, size: lax.dynamic_slice_in_dim(array, first, size, array.ndim - 1)
    taps_all = jnp.concatenate([conv_weight, conv_bias[None, :]], axis=0)
    taps = pad_rows(
        jnp.concatenate([taps_all[:, inner:], pad_last(cut(taps_all, first_chan, own), width)], axis=1), 8
    )
    head_rows = jnp.stack([step_bias, -jnp.exp(rate_log)])
    head_params = pad_rows(pad_last(cut(head_rows, first_head, own_heads), LANES), 8)
    skip = jnp.repeat(cut(skip_gain, first_head, own_heads), head_dim)[None, :]
    skip = pad_rows(pad_last(skip, width), 8)
    active_heads = heads // 8 * jnp.left_shift(jnp.int32(1), widths)
    head_mask = (first_head + jnp.arange(own_heads, dtype=jnp.int32))[None, :] < active_heads[:, None]
    chan_mask = jnp.repeat(head_mask.astype(F32), head_dim, axis=1)
    mask = pad_last(chan_mask, width)[:, None, :]
    per_token = lambda array: jnp.repeat(array, all_tokens // seqs, axis=0)
    mask_tok = chan_mask if seqs == 1 else per_token(chan_mask)
    active_count = (active_heads * head_dim).astype(F32)[:, None]
    if seqs > 1:
        active_count = per_token(active_count)

    if line:
        sibling_out, sibling_weight = swap(out_weight, "mp", 1), swap(weight, "mp", 1)
        weight, sibling_out, sibling_weight = lax.optimization_barrier((weight, sibling_out, sibling_weight))
    out_turned = pad_rows(out_weight, width).T
    weight, out_turned = lax.optimization_barrier((weight, out_turned))
    projected, y_all, states, squares, pre = mixer_forward(
        mask, hidden, weight, taps, head_params, skip, state_dim, width
    )
    square_rows = all_sum(squares[:, 0, :], "mp")
    total_square = square_rows.reshape(all_tokens)[:, None]
    gate = projected[:, :own].astype(F32)
    y_f = y_all[:, :own].astype(F32)
    gate_sig = jax.nn.sigmoid(gate)
    silu_z = gate * gate_sig
    gated = y_f * silu_z
    gain = cut(out_gain, first_chan, own)[None, :]
    out_root = lax.rsqrt(total_square / active_count + EPS)
    normed_out = (gated * out_root * gain * mask_tok).astype(BF16)
    if line:
        theirs = swap(for_sibling(normed_out, tokens), "mp", 1)
        shares = pair_product(normed_out, theirs, out_weight, sibling_out, NN, depth, tokens, True)[0]
        cot_all = lax.all_gather(cotangent, "mp", axis=0, tiled=True)
        cot_all, shares = lax.optimization_barrier((cot_all, shares))
    else:
        shares = mm(normed_out, out_weight).astype(BF16)
        sent = [lax.psum_scatter(shares, "mp", scatter_dimension=0, tiled=True)]
        late_cot, sent = lax.optimization_barrier((cotangent, sent))
        cot_all = lax.all_gather(late_cot, "mp", axis=0, tiled=True)

    gain_rows = pad_last(cut(out_gain, first_chan, own), width)
    gains = jnp.concatenate(
        [
            gain_rows[None, None, :] * mask,
            mask,
            jnp.broadcast_to((active_heads * head_dim).astype(F32)[:, None, None], mask.shape),
            jnp.zeros((seqs, 5, width), F32),
        ],
        axis=1,
    )
    d_normed, dots = pull_back(cot_all, out_turned, projected, y_all, gains, 0)
    dot_rows = all_sum(dots[:, 0, :], "mp")
    out_part = mm(normed_out, cot_all, TN)
    if line:
        dot_rows, shares = lax.optimization_barrier((dot_rows, shares))
        sent = line_send(shares)
    token_rows = jnp.stack([square_rows, dot_rows] + [jnp.zeros_like(dot_rows)] * 6, axis=1)
    quarter = depth // dp

    def in_block(share, k, half):
        return share[k * quarter + half * (quarter // 2) : k * quarter + (half + 1) * (quarter // 2)]

    def to_rows(mine):
        return lax.all_to_all(mine.astype(BF16).reshape(mp, part, -1), "mp", split_axis=0, concat_axis=0, tiled=True)

    token_rows, out_part = lax.optimization_barrier((token_rows, out_part))
    out_mine = lax.psum_scatter(out_part, "dp", scatter_dimension=0, tiled=True)
    def norm_share(d_hidden):
        share = restore(jnp.sum(d_hidden * normed, axis=0)[None, :])
        return all_sum(share.reshape(-1, LANES), "dp")

    def rows_of(blocks):
        flat = lambda first, size: blocks[:, :, first : first + size].transpose(1, 0, 2).reshape(part, -1)
        shared = jnp.sum(blocks[:, :, width : width + 2 * state_dim].astype(F32), axis=0).astype(BF16)
        return jnp.concatenate(
            [flat(0, own), flat(width + 2 * state_dim, own), shared, flat(width + joint, own_heads)], axis=1
        )

    d_proj, conv_grads, head_grads, gain_grads = mixer_backward(
        gains, projected, pre, y_all, d_normed, token_rows, states, taps, head_params, skip, state_dim
    )
    d_proj, out_mine = lax.optimization_barrier((d_proj, out_mine))
    out_weight_grad = lax.all_gather(out_mine, "dp", axis=0, tiled=True)

    def place_in(array, first, size):
        return lax.dynamic_update_slice_in_dim(
            jnp.zeros(array.shape[:-1] + (size,), F32), array, first, array.ndim - 1
        )

    conv_own = place_in(conv_grads[:5, 2 * state_dim : 2 * state_dim + own], first_chan, inner)
    conv_full = jnp.concatenate([conv_own, conv_grads[:5, : 2 * state_dim]], axis=1)
    head_full = place_in(head_grads[:3, :own_heads], first_head, heads)
    gain_full = place_in(gain_grads[0, :own], first_chan, inner)
    small = [conv_full.reshape(-1), head_full.reshape(-1), gain_full]
    sizes = [piece.shape[0] for piece in small]
    packed = jnp.concatenate(small)
    count = -(-packed.shape[0] // 1024) * 1024
    packed = jnp.pad(packed, (0, count - packed.shape[0])).reshape(-1, LANES)

    if line:
        theirs = swap(for_sibling(d_proj, tokens), "mp", 1)
        d_shares = pair_product(d_proj, theirs, weight, sibling_weight, NT, depth, tokens, False)
        d_shares, d_proj, sent = lax.optimization_barrier((d_shares, d_proj, sent))
        reaches = list(range(1, mp // 2))
        d_blocks = [d_shares[0], line_permute(d_shares[1], 1)]
        share = mm(hidden, d_proj, TN)
        near_cut = reduce_cut(share, in_block, BF16)
        near_cut, d_blocks, out_weight_grad = lax.optimization_barrier((near_cut, d_blocks, out_weight_grad))
        near_got = reduce_near(near_cut)
        d_blocks += [line_permute(d_shares[reach], reach) for reach in reaches[1:2]]
        near_got, d_blocks = lax.optimization_barrier((near_got, d_blocks))
        mine = reduce_far(share, in_block, near_got)
        d_blocks += [line_permute(d_shares[reach], reach) for reach in reaches[2:]]
        mine, packed, d_blocks = lax.optimization_barrier((mine, packed, d_blocks))
        blocks = to_rows(mine)
        d_hidden = total(d_blocks)
        norm_part = norm_share(d_hidden)
        blocks, packed, out_weight_grad, norm_part = lax.optimization_barrier(
            (blocks, all_sum(packed, "dp"), keep(out_weight_grad), norm_part)
        )
        in_weight_grad = assemble(gather_far(gather_near(rows_of(blocks))))
    else:
        packed = all_sum(packed, "dp")
        share = mm(hidden, d_proj, TN)
        d_proj, share = lax.optimization_barrier((d_proj, share))
        blocks = to_rows(reduce_far(share, in_block, reduce_near(reduce_cut(share, in_block, BF16))))
        d_shares = mm(d_proj, weight, NT).astype(BF16)
        d_hidden = lax.psum_scatter(d_shares, "mp", scatter_dimension=0, tiled=True).astype(F32)
        in_weight_grad = in_place_order(gather_far(gather_near(rows_of(blocks))))
    outputs = (inputs_f + total(sent)).astype(BF16)
    if not line:
        norm_part = norm_share(d_hidden)
    everything = all_sum(jnp.concatenate([packed, norm_part], axis=0), "mp")
    norm_total = everything[packed.shape[0] :].reshape(depth)
    packed = everything.reshape(-1)
    conv_total = packed[: sizes[0]].reshape(conv_full.shape)
    head_total = packed[sizes[0] : sizes[0] + sizes[1]].reshape(head_full.shape)
    gain_total = packed[sizes[0] + sizes[1] : sum(sizes)]

    d_normed_in = d_hidden * gain_in
    input_back = rms_scale * (d_normed_in - normed * jnp.mean(d_normed_in * normed, axis=-1, keepdims=True))
    input_grad = restore((reorder(cotangent).astype(F32) + input_back).astype(BF16))

    return (
        outputs,
        input_grad,
        norm_total,
        in_weight_grad,
        conv_total[:4],
        conv_total[4],
        head_total[0],
        head_total[1],
        head_total[2],
        gain_total,
        out_weight_grad,
    )


def solution(mesh):
    rows = P(("dp", "mp"), None)
    return jax.shard_map(
        on_device,
        mesh=mesh,
        in_specs=(rows, rows, P("dp"), P(), P("mp", None), P(), P(), P(), P(), P(), P(), P("mp", None)),
        out_specs=(rows, rows, P(), P("mp", None), P(), P(), P(), P(), P(), P(), P("mp", None)),
        check_vma=False,
    )
```
